768 devices in a mesh: lat: 48 (over y_lo, z, core), lon: 4 (over y_hi), mem: 4 (over x).
Axes of the slice: x: 4, y: 8 (y_hi: 4, y_lo: 2; y = y_hi * 2 + y_lo), z: 12, core: 2. Of those that a mesh axis runs over, the one named last changes fastest.
Arguments:
- column_state: float32 [8, 64, 192, 512], P('mem', None, 'lat', 'lon'), may hold values from -6 to 6
- cotangent: float32 [8, 64, 192, 512], P('mem', None, 'lat', 'lon'), may hold values from -6 to 6
- land_mask: int32 [192, 512], P('lat', 'lon'), may hold values from 0 to 1
- orography: int32 [192, 512], P('lat', 'lon'), may hold values from 0 to 15
- member_seeds: int32 [8], P('mem'), may hold values from 0 to 31
- land_table: float32 [2, 64], replicated, may hold values from -5 to 5
- relief_table: float32 [16, 64], replicated, may hold values from -5 to 5
- seed_table: float32 [32, 64], replicated, may hold values from -5 to 5
- w_hidden: bfloat16 [384, 640], replicated, may hold values from -0.25 to 0.25
- b_hidden: float32 [384], replicated, may hold values from -4 to 4
- w_tendency: bfloat16 [64, 384], replicated, may hold values from -0.3125 to 0.3125
Outputs:
- next_state: float32 [8, 64, 192, 512], P('mem', None, 'lat', 'lon')
- state_grad: float32 [8, 64, 192, 512], P('mem', None, 'lat', 'lon')
- grad_w_hidden: float32 [384, 640], replicated
- grad_b_hidden: float32 [384], replicated
- grad_w_tendency: float32 [64, 384], replicated
The draws below stay inside these ranges and needn't reach their ends.
All inputs are finite; a program needn't handle non-finite values.
Results may differ from the reference program's by a relative error of at most 0.0059.
Values may be sent and summed in bfloat16 or wider, within the bound.
No kernel may reach another device: no remote copies, remote signals or barrier semaphores. Data moves between devices by JAX's collectives and lax.ppermute only.
A program may use at most 64 MiB of HBM per device.

```python
import math
import jax
import jax.numpy as jnp
from jax import lax

S = 64
E = 64
H = 384
LON = 512
MODES = 171
CLASSES = 16
SEEDS = 32
LAT = 192
MEMBERS = 8
IN = 640


def place_ends(values, rng, smallest, top_value):
    longest = values.shape.index(max(values.shape))
    spots = []
    for shift in (0, 1):
        where = [jax.random.randint(jax.random.fold_in(rng, axis), (), 0, length) for axis, length in enumerate(values.shape)]
        where[longest] = (where[longest] + shift) % values.shape[longest]
        spots.append(tuple(where))
    return values.at[spots[0]].set(smallest).at[spots[1]].set(top_value)


def levels(own_key, extent, shards, low, largest):
    factor_of, own = 1.0, jax.random.fold_in(own_key, 6)
    for dim, shards_of in shards:
        steps = jnp.exp(jax.random.uniform(jax.random.fold_in(own, dim), (shards_of,), jnp.float32, low / len(shards), largest / len(shards)))
        factor_of = factor_of * jnp.repeat(steps, extent[dim] // shards_of).reshape([-1 if axis == dim else 1 for axis in range(len(extent))])
    return factor_of


def centred(rng, dims, width, reach, pieces=(), held_as=jnp.bfloat16):
    level = levels(rng, dims, pieces, -0.22, 0.18) if pieces else 1.0
    drawn = jax.random.normal(rng, dims, jnp.float32) * width * level
    return jnp.minimum(jnp.maximum(drawn, -reach), reach).astype(held_as)


def setup_inputs(seed: int = 0) -> dict:
    splits = jax.random.split(jax.random.key(seed), 12)
    return {
        "column_state": centred(splits[0], (MEMBERS, S, LAT, LON), 1.0, 6.0, ((0, 4), (2, 48), (3, 4)), jnp.float32),
        "cotangent": centred(splits[1], (MEMBERS, S, LAT, LON), 1.0, 6.0, ((0, 4), (2, 48), (3, 4)), jnp.float32),
        "land_mask": place_ends(jax.random.randint(splits[2], (LAT, LON), 0, 2), jax.random.fold_in(splits[2], 1), 0, 1).astype(jnp.int32),
        "orography": place_ends(jax.random.randint(splits[3], (LAT, LON), 0, CLASSES), jax.random.fold_in(splits[3], 1), 0, CLASSES - 1).astype(jnp.int32),
        "member_seeds": place_ends(jax.random.randint(splits[4], (MEMBERS,), 0, SEEDS), jax.random.fold_in(splits[4], 1), 0, SEEDS - 1).astype(jnp.int32),
        "land_table": centred(splits[5], (2, E), 1.0, 5.0, (), jnp.float32),
        "relief_table": centred(splits[6], (CLASSES, E), 1.0, 5.0, (), jnp.float32),
        "seed_table": centred(splits[7], (SEEDS, E), 1.0, 5.0, (), jnp.float32),
        "w_hidden": centred(splits[8], (H, IN), IN ** -0.5, 0.25),
        "b_hidden": centred(splits[9], (H,), 0.7, 4.0, (), jnp.float32),
        "w_tendency": centred(splits[10], (S, H), H ** -0.5, 0.3125),
    }


damp_strength = 2.0

def zonal_basis(positions, lon_total):
    wavenumber = jnp.arange(MODES, dtype=jnp.int32)
    phases = wavenumber[:, None] * positions[None, :] % lon_total
    angles = phases.astype(jnp.float32) * (2.0 * math.pi / lon_total)
    analysis = jnp.concatenate([jnp.cos(angles), jnp.sin(angles)], 0)
    weights = jnp.where(wavenumber == 0, 1.0, 2.0).astype(jnp.float32) / lon_total
    weights = jnp.concatenate([weights, weights], 0)
    return (analysis, analysis * weights[:, None])

def removal_table(lat_index, lat_total):
    latitude = math.pi * ((lat_index.astype(jnp.float32) + 0.5) / lat_total - 0.5)
    fraction = jnp.arange(MODES, dtype=jnp.int32).astype(jnp.float32) / MODES
    shrink = 1.0 - jnp.exp(-damp_strength * fraction[None, :] ** 2 / jnp.cos(latitude)[:, None] ** 2)
    return jnp.concatenate([shrink, shrink], 1)

def widen(values):
    looped = jnp.concatenate([values[..., -1:], values, values[..., :1]], -1)
    return jnp.pad(looped, ((0, 0), (1, 1), (0, 0)))

def reference(column_state, cotangent, land_mask, orography, member_seeds, land_table, relief_table, seed_table, w_hidden, b_hidden, w_tendency):
    highest = lax.Precision.HIGHEST
    analysis, synthesis = zonal_basis(jnp.arange(LON, dtype=jnp.int32), LON)
    removal = removal_table(jnp.arange(LAT, dtype=jnp.int32), LAT)
    land_part = jnp.where(land_mask[None] == 1, land_table[1][:, None, None], land_table[0][:, None, None])
    relief = jnp.transpose(relief_table[orography], (2, 0, 1))
    surface = land_part + relief

    def member(inputs):
        current, adjoint, seed_id = inputs
        forcing = surface + seed_table[seed_id][:, None, None]
        padded = widen(current)
        stencil = jnp.concatenate([padded[:, row_off:row_off + LAT, col_off:col_off + LON] for row_off in range(3) for col_off in range(3)], 0)
        features = jnp.concatenate([stencil, forcing], 0).reshape(IN, LAT * LON).astype(jnp.bfloat16)
        preact = jnp.dot(w_hidden, features, preferred_element_type=jnp.float32) + b_hidden[:, None]
        hidden = jax.nn.silu(preact).astype(jnp.bfloat16)
        tendency = jnp.dot(w_tendency, hidden, preferred_element_type=jnp.float32)
        moist = current + tendency.reshape(S, LAT, LON)
        coeffs = jnp.einsum('sji,ki->sjk', moist, analysis, precision=highest)
        next_state = moist - jnp.einsum('sjk,ki->sji', coeffs * removal[None], synthesis, precision=highest)
        replies = jnp.einsum('sji,ki->sjk', adjoint, synthesis, precision=highest)
        moist_grad = adjoint - jnp.einsum('sjk,ki->sji', replies * removal[None], analysis, precision=highest)
        tendency_grad = moist_grad.reshape(S, LAT * LON).astype(jnp.bfloat16)
        grad_out = jnp.dot(tendency_grad, hidden.T, preferred_element_type=jnp.float32)
        hidden_grad = jnp.dot(w_tendency.T, tendency_grad, preferred_element_type=jnp.float32)
        logistic = jax.nn.sigmoid(preact)
        preact_grad = (hidden_grad * logistic * (1.0 + preact * (1.0 - logistic))).astype(jnp.bfloat16)
        grad_in = jnp.dot(preact_grad, features.T, preferred_element_type=jnp.float32)
        grad_bias = lax.optimization_barrier(jnp.sum(preact_grad.astype(jnp.float32), 1))
        stencil_grad = jnp.dot(w_hidden[:, :9 * S].T, preact_grad, preferred_element_type=jnp.float32)
        spread = widen(stencil_grad.reshape(9 * S, LAT, LON))
        state_grad = moist_grad
        for row_off in range(3):
            for col_off in range(3):
                offset = (row_off * 3 + col_off) * S
                state_grad = state_grad + spread[offset:offset + S, 2 - row_off:2 - row_off + LAT, 2 - col_off:2 - col_off + LON]
        return (next_state, state_grad, grad_in, grad_bias, grad_out)
    next_state, state_grad, grad_in, grad_bias, grad_out = lax.map(member, (column_state, cotangent, member_seeds))
    scaling = 1.0 / math.sqrt(MEMBERS * LAT * LON)
    return (next_state, state_grad, lax.optimization_barrier(jnp.sum(grad_in, 0)) * scaling, lax.optimization_barrier(jnp.sum(grad_bias, 0)) * scaling, lax.optimization_barrier(jnp.sum(grad_out, 0)) * scaling)
```

```python
import math

import jax
import jax.numpy as jnp
import numpy as np
from jax import lax
from jax.experimental import pallas as pl
from jax.experimental.pallas import tpu as pltpu
from jax.sharding import Mesh, PartitionSpec as P

MODES = 171
DAMP = 2.0
LANES = 128
BF = jnp.bfloat16
F32 = jnp.float32
VMEM_BYTES = 56 * 1024 * 1024
ROWS_AXES = ("ylo", "z", "core", "lon")
NEAR = ("core", "mem")
FAR = ("ylo", "lon", "z")


def filter_kernels(lat_total, lon_total):
    lat = math.pi * ((np.arange(lat_total) + 0.5) / lat_total - 0.5)
    k = np.arange(MODES)
    removal = 1.0 - np.exp(-DAMP * (k[None] / MODES) ** 2 / np.cos(lat)[:, None] ** 2)
    weights = np.where(k == 0, 1.0, 2.0) / lon_total
    phases = (k[:, None] * np.arange(lon_total)[None]) % lon_total
    return ((removal * weights) @ np.cos(phases * (2.0 * math.pi / lon_total))).astype(np.float32)


def dot(a, b, dims=((1,), (0,))):
    return lax.dot_general(a, b, (dims, ((), ())), preferred_element_type=F32)


def split_dot(x, high, low):
    x_high = x.astype(BF)
    x_low = (x - x_high.astype(F32)).astype(BF)
    return dot(x_high, high) + (dot(x_low, high) + dot(x_high, low))


def joined(ref, start, rows):
    return jnp.concatenate([ref[s, start : start + rows, :] for s in range(ref.shape[0])], axis=1)


def store_split(ref, start, value):
    for s in range(ref.shape[0]):
        ref[s, start : start + value.shape[0], :] = value[:, s * LANES : (s + 1) * LANES].astype(
            ref.dtype
        )


def adjoint_filter_kernel(row_ref, kernel_ref, moist_grad_ref, high_ref, low_ref):
    lon_total = kernel_ref.shape[1]
    rows = moist_grad_ref.shape[0]
    matrix = pltpu.roll(
        jnp.broadcast_to(kernel_ref[...], (lon_total, lon_total)), 0, 1, stride=1, stride_axis=0
    )
    high = matrix.astype(BF)
    low = (matrix - high.astype(F32)).astype(BF)
    high_ref[...] = high
    low_ref[...] = low
    cotangent = joined(row_ref, rows, rows)
    moist_grad_ref[...] = cotangent - split_dot(cotangent, high, low)


def column_kernel(
    seeds_ref,
    row_ref,
    north_ref,
    south_ref,
    moist_grad_ref,
    high_ref,
    low_ref,
    land_ref,
    relief_ref,
    seed_ref,
    w_hidden_ref,
    b_hidden_ref,
    w_tendency_ref,
    next_ref,
    grad_ref,
    to_north_ref,
    to_south_ref,
    weights_ref,
    features_ref,
):
    members = features_ref.shape[0]
    channels = w_tendency_ref.shape[0]
    hidden_units, in_channels = w_hidden_ref.shape
    rows = members * channels
    stencil_rows = 9 * channels
    lon_total = features_ref.shape[2]
    classes = relief_ref.shape[0]

    state = joined(row_ref, 0, rows)
    sources = (
        joined(north_ref, 0, rows).astype(F32),
        state.astype(BF).astype(F32),
        joined(south_ref, 0, rows).astype(F32),
    )
    for a in range(3):
        for b in range(3):
            moved = sources[a]
            if b != 1:
                moved = pltpu.roll(moved, (1 - b) % lon_total, 1)
            moved = moved.astype(BF)
            start = (3 * a + b) * channels
            for m in range(members):
                features_ref[m, start : start + channels, :] = moved[
                    m * channels : (m + 1) * channels
                ]
    code = joined(row_ref, 2 * rows, 8)[0:1]
    class_ids = lax.broadcasted_iota(jnp.int32, (2 * classes, lon_total), 0).astype(F32)
    pick = jnp.where(class_ids == code, 1.0, 0.0).astype(BF)
    surface = jnp.concatenate(
        [land_ref[0:1, :] + relief_ref[...], land_ref[1:2, :] + relief_ref[...]], axis=0
    )
    bias = jnp.transpose(jnp.broadcast_to(b_hidden_ref[...], (8, hidden_units)))[:, 0:1]
    w_hidden = w_hidden_ref[...]
    w_tendency = w_tendency_ref[...]
    high = high_ref[...]
    low = low_ref[...]
    grad_in = jnp.zeros((hidden_units, in_channels), F32)
    grad_out = jnp.zeros((channels, hidden_units), F32)
    grad_bias = jnp.zeros((16, hidden_units), F32)
    ones = jnp.ones((16, lon_total), BF)
    for m in range(members):
        table = (surface + seed_ref[pl.ds(seeds_ref[m], 1), :]).astype(BF)
        forcing = dot(table, pick, ((0,), (0,)))
        features_ref[m, stencil_rows:, :] = forcing.astype(BF)
        features = features_ref[m]
        preact = dot(w_hidden, features) + bias
        logistic = 1.0 / (1.0 + jnp.exp(-preact))
        hidden = (preact * logistic).astype(BF)
        part = slice(m * channels, (m + 1) * channels)
        moist = state[part] + dot(w_tendency, hidden)
        store_split(next_ref, m * channels, moist - split_dot(moist, high, low))
        moist_grad = moist_grad_ref[part, :]
        tendency_grad = moist_grad.astype(BF)
        hidden_grad = dot(w_tendency, tendency_grad, ((0,), (0,)))
        preact_grad = (hidden_grad * logistic * (1.0 + preact * (1.0 - logistic))).astype(BF)
        grad_out += dot(tendency_grad, hidden, ((1,), (1,)))
        grad_in += dot(preact_grad, features, ((1,), (1,)))
        grad_bias += dot(ones, preact_grad, ((1,), (1,)))
        stencil_grad = dot(w_hidden[:, :stencil_rows], preact_grad, ((0,), (0,)))
        sums = []
        for a in range(3):
            total = None
            for b in range(3):
                start = (3 * a + b) * channels
                piece = stencil_grad[start : start + channels]
                if b != 1:
                    piece = pltpu.roll(piece, (b - 1) % lon_total, 1)
                total = piece if total is None else total + piece
            sums.append(total)
        store_split(to_north_ref, m * channels, sums[0])
        store_split(grad_ref, m * channels, moist_grad + sums[1])
        store_split(to_south_ref, m * channels, sums[2])

    shares, share_rows = weights_ref.shape[:2]
    bias_high = grad_bias[0:1].astype(BF).astype(F32)
    bias_low = grad_bias[0:1] - bias_high
    row_ids = lax.broadcasted_iota(jnp.int32, (8, hidden_units), 0)
    bias_rows = jnp.where(row_ids == 0, bias_high, jnp.where(row_ids == 1, bias_low, 0.0))
    for p in range(shares):
        pieces = []
        for value in (grad_in, grad_out, bias_rows):
            count = value.shape[0] // (1 if value is bias_rows else shares)
            first = 0 if value is bias_rows else p * count
            for t in range(value.shape[1] // LANES):
                pieces.append(
                    value[first : first + count, t * LANES : (t + 1) * LANES]
                )
        filled = sum(piece.shape[0] for piece in pieces)
        if filled < share_rows:
            pieces.append(jnp.zeros((share_rows - filled, LANES), F32))
        weights_ref[p] = jnp.concatenate(pieces, axis=0).astype(BF)


def unpack_kernel(scaling, shares_ref, grad_in_ref, grad_bias_ref, grad_out_ref):
    shares = shares_ref.shape[0]
    for p in range(shares):
        share = shares_ref[p].astype(F32) * scaling
        start = 0
        for ref in (grad_in_ref, grad_out_ref):
            count = ref.shape[0] // shares
            for t in range(ref.shape[1] // LANES):
                ref[p * count : (p + 1) * count, t * LANES : (t + 1) * LANES] = share[
                    start : start + count
                ]
                start += count
        if p == 0:
            for t in range(grad_bias_ref.shape[1] // LANES):
                grad_bias_ref[0:1, t * LANES : (t + 1) * LANES] = (
                    share[start : start + 1] + share[start + 1 : start + 2]
                )
                start += 8


def call(kernel, outs, scratch=(), smem_first=False, flops=0, inputs=0):
    vmem = pl.BlockSpec(memory_space=pltpu.VMEM)
    specs = [vmem] * inputs
    if smem_first:
        specs[0] = pl.BlockSpec(memory_space=pltpu.SMEM)
    return pl.pallas_call(
        kernel,
        out_shape=outs,
        in_specs=specs,
        out_specs=jax.tree.map(lambda _: vmem, outs),
        scratch_shapes=list(scratch),
        cost_estimate=pl.CostEstimate(flops=flops, bytes_accessed=4_000_000, transcendentals=0),
        compiler_params=pltpu.CompilerParams(vmem_limit_bytes=VMEM_BYTES),
    )


def exchange(x, axes):
    return lax.all_to_all(x, axes, 0, 0, tiled=True)


def on_device(
    column_state,
    cotangent,
    land_mask,
    orography,
    member_seeds,
    land_table,
    relief_table,
    seed_table,
    w_hidden,
    b_hidden,
    w_tendency,
):
    members, channels, band, lon_cols = column_state.shape
    hidden_units, in_channels = w_hidden.shape
    classes = relief_table.shape[0]
    sectors = lax.axis_size("lon")
    lat_total = band * lax.axis_size(("ylo", "z", "core"))
    lon_total = lon_cols * sectors
    rows = members * channels
    shape = jax.ShapeDtypeStruct

    with jax.named_scope("rows_in"):
        def by_row(values):
            return jnp.transpose(values, (2, 0, 1, 3)).reshape(band, rows, lon_cols)

        code = (jnp.where(land_mask == 1, classes, 0) + orography).astype(F32)
        code = jnp.broadcast_to(code[:, None, :], (band, 8, lon_cols))
        packed = jnp.concatenate([by_row(column_state), by_row(cotangent), code], axis=1)
        row = exchange(packed, "lon")

    with jax.named_scope("row_halo"):
        peers = lax.axis_size(ROWS_AXES)
        south_going = [(i, i + 1) for i in range(peers - 1)]
        north_going = [(j, i) for i, j in south_going]
        edge = row[:, :rows, :].astype(BF)
        north = lax.ppermute(edge, ROWS_AXES, south_going)
        south = lax.ppermute(edge, ROWS_AXES, north_going)

    with jax.named_scope("adjoint_filter"):
        table = jnp.asarray(filter_kernels(lat_total, lon_total))
        kernel_row = lax.dynamic_slice_in_dim(table, lax.axis_index(ROWS_AXES), 1, 0)
        moist_grad, high, low = call(
            adjoint_filter_kernel,
            (
                shape((rows, lon_total), F32),
                shape((lon_total, lon_total), BF),
                shape((lon_total, lon_total), BF),
            ),
            inputs=2,
            flops=6 * rows * lon_total * lon_total,
        )(row, kernel_row)

    near = lax.axis_size(NEAR)
    far = lax.axis_size(FAR)
    share_rows = (
        hidden_units * (in_channels // LANES) // near
        + channels * (hidden_units // LANES) // near
        + 8 * (hidden_units // LANES)
    )
    share_rows = -(-share_rows // far) * far
    share_rows = -(-share_rows // 16) * 16 if share_rows % 16 else share_rows
    with jax.named_scope("columns"):
        block = (sectors, rows, LANES)
        next_rows, grad_rows, to_north, to_south, weights = call(
            column_kernel,
            (
                shape(block, BF),
                shape(block, F32),
                shape(block, BF),
                shape(block, BF),
                shape((near, share_rows, LANES), BF),
            ),
            scratch=[pltpu.VMEM((members, in_channels, lon_total), BF)],
            smem_first=True,
            inputs=13,
            flops=4_000_000_000,
        )(
            member_seeds,
            row,
            north,
            south,
            moist_grad,
            high,
            low,
            land_table,
            relief_table,
            seed_table,
            w_hidden,
            b_hidden.reshape(1, hidden_units),
            w_tendency,
        )

    with jax.named_scope("gradient_halo"):
        from_south = lax.ppermute(to_north, ROWS_AXES, north_going)
        from_north = lax.ppermute(to_south, ROWS_AXES, south_going)

    with jax.named_scope("weights_near"):
        parts = exchange(weights, NEAR)
        share = jnp.sum(parts.astype(F32), 0)

    with jax.named_scope("rows_out"):
        state_grad_rows = grad_rows + from_south.astype(F32) + from_north.astype(F32)
        outgoing = jnp.concatenate([next_rows, state_grad_rows.astype(BF)], axis=1)
        blocks = exchange(outgoing, "lon")

        def by_band(values):
            values = values.reshape(band, members, channels, lon_cols).astype(F32)
            return jnp.transpose(values, (1, 2, 0, 3))

        next_state = by_band(blocks[:, :rows])
        state_grad = by_band(blocks[:, rows:])

    with jax.named_scope("weights_far"):
        parts = exchange(share.reshape(far, share_rows // far, LANES), FAR)
        piece = jnp.sum(parts, 0, keepdims=True)
        gathered = exchange(jnp.broadcast_to(piece, parts.shape), FAR)

    with jax.named_scope("weights_back"):
        share = gathered.reshape(1, share_rows, LANES).astype(BF)
        shares = exchange(jnp.broadcast_to(share, (near, share_rows, LANES)), NEAR)
        columns = members * lax.axis_size("mem") * lat_total * lon_total

        def unpack(*refs):
            unpack_kernel(1.0 / math.sqrt(columns), *refs)

        grad_in, grad_bias, grad_out = call(
            unpack,
            (
                shape((hidden_units, in_channels), F32),
                shape((1, hidden_units), F32),
                shape((channels, hidden_units), F32),
            ),
            inputs=1,
        )(shares)
    return next_state, state_grad, grad_in, grad_bias.reshape(hidden_units), grad_out


def solution(mesh):
    lat, lon, mem = mesh.devices.shape
    devices = mesh.devices.reshape(2, lat // 4, 2, lon, mem)
    split = Mesh(devices, ("ylo", "z", "core", "lon", "mem"))
    lat_axes = ("ylo", "z", "core")
    field = P("mem", None, lat_axes, "lon")
    surface = P(lat_axes, "lon")
    whole = P()
    return jax.shard_map(
        on_device,
        mesh=split,
        in_specs=(field, field, surface, surface, P("mem")) + (whole,) * 6,
        out_specs=(field, field, whole, whole, whole),
        check_vma=False,
    )
```

```python
import math

import jax
import jax.numpy as jnp
import numpy as np
from jax import lax
from jax.experimental import pallas as pl
from jax.experimental.pallas import tpu as pltpu
from jax.sharding import Mesh, PartitionSpec as P

MODES = 171
DAMP = 2.0
LANES = 128
BF = jnp.bfloat16
F32 = jnp.float32
VMEM_BYTES = 56 * 1024 * 1024
ROWS_AXES = ("ylo", "z", "core", "lon")
NEAR = ("core", "mem")
MIDDLE = ("ylo", "lon")


def filter_kernels(lat_total, lon_total):
    lat = math.pi * ((np.arange(lat_total) + 0.5) / lat_total - 0.5)
    k = np.arange(MODES)
    removal = 1.0 - np.exp(-DAMP * (k[None] / MODES) ** 2 / np.cos(lat)[:, None] ** 2)
    weights = np.where(k == 0, 1.0, 2.0) / lon_total
    phases = (k[:, None] * np.arange(lon_total)[None]) % lon_total
    return ((removal * weights) @ np.cos(phases * (2.0 * math.pi / lon_total))).astype(np.float32)


def dot(a, b, dims=((1,), (0,))):
    return lax.dot_general(a, b, (dims, ((), ())), preferred_element_type=F32)


def split_dot(x, high, low):
    x_high = x.astype(BF)
    x_low = (x - x_high.astype(F32)).astype(BF)
    return dot(x_high, high) + (dot(x_low, high) + dot(x_high, low))


def joined(ref, start, rows):
    return jnp.concatenate([ref[s, start : start + rows, :] for s in range(ref.shape[0])], axis=1)


def store_split(ref, start, value):
    for s in range(ref.shape[0]):
        ref[s, start : start + value.shape[0], :] = value[:, s * LANES : (s + 1) * LANES].astype(
            ref.dtype
        )


def by_row_kernel(state_ref, cotangent_ref, land_ref, orography_ref, classes, out_ref, adjoint_ref):
    band, rows = out_ref.shape[:2]
    members = state_ref.shape[0]
    channels = rows // members
    code = jnp.where(land_ref[...] == 1, classes, 0) + orography_ref[...]
    code = code.astype(F32)
    for q in range(band):
        for m in range(members):
            picked = pl.ds(q, channels, stride=band)
            out_ref[q, m * channels : (m + 1) * channels, :] = state_ref[m, picked, :]
            adjoint_ref[q, m * channels : (m + 1) * channels, :] = cotangent_ref[m, picked, :]
        adjoint_ref[q, rows:, :] = jnp.broadcast_to(code[q : q + 1], (8, LANES))


def adjoint_filter_kernel(place_ref, row_ref, table_ref, moist_grad_ref, high_ref, low_ref):
    lon_total = table_ref.shape[1]
    rows = moist_grad_ref.shape[0]
    kernel = table_ref[pl.ds(place_ref[0], 1), :]
    matrix = pltpu.roll(
        jnp.broadcast_to(kernel, (lon_total, lon_total)), 0, 1, stride=1, stride_axis=0
    )
    high = matrix.astype(BF)
    low = (matrix - high.astype(F32)).astype(BF)
    high_ref[...] = high
    low_ref[...] = low
    cotangent = joined(row_ref, 0, rows)
    moist_grad_ref[...] = cotangent - split_dot(cotangent, high, low)


def column_kernel(
    seeds_ref,
    row_ref,
    adjoint_ref,
    north_ref,
    south_ref,
    moist_grad_ref,
    high_ref,
    low_ref,
    land_ref,
    relief_ref,
    seed_ref,
    w_hidden_ref,
    b_hidden_ref,
    w_tendency_ref,
    next_ref,
    grad_ref,
    to_north_ref,
    to_south_ref,
    weights_ref,
    features_ref,
):
    members = features_ref.shape[0]
    channels = w_tendency_ref.shape[0]
    hidden_units, in_channels = w_hidden_ref.shape
    rows = members * channels
    stencil_rows = 9 * channels
    lon_total = features_ref.shape[2]
    classes = relief_ref.shape[0]

    state = joined(row_ref, 0, rows)
    sources = (
        joined(north_ref, 0, rows).astype(F32),
        state.astype(BF).astype(F32),
        joined(south_ref, 0, rows).astype(F32),
    )
    for a in range(3):
        for b in range(3):
            moved = sources[a]
            if b != 1:
                moved = pltpu.roll(moved, (1 - b) % lon_total, 1)
            moved = moved.astype(BF)
            start = (3 * a + b) * channels
            for m in range(members):
                features_ref[m, start : start + channels, :] = moved[
                    m * channels : (m + 1) * channels
                ]
    code = joined(adjoint_ref, rows, 8)[0:1]
    class_ids = lax.broadcasted_iota(jnp.int32, (2 * classes, lon_total), 0).astype(F32)
    pick = jnp.where(class_ids == code, 1.0, 0.0).astype(BF)
    surface = jnp.concatenate(
        [land_ref[0:1, :] + relief_ref[...], land_ref[1:2, :] + relief_ref[...]], axis=0
    )
    bias = jnp.transpose(jnp.broadcast_to(b_hidden_ref[...], (8, hidden_units)))[:, 0:1]
    w_hidden = w_hidden_ref[...]
    w_tendency = w_tendency_ref[...]
    high = high_ref[...]
    low = low_ref[...]
    grad_in = jnp.zeros((hidden_units, in_channels), F32)
    grad_out = jnp.zeros((channels, hidden_units), F32)
    grad_bias = jnp.zeros((16, hidden_units), F32)
    ones = jnp.ones((16, lon_total), BF)
    for m in range(members):
        table = (surface + seed_ref[pl.ds(seeds_ref[m], 1), :]).astype(BF)
        forcing = dot(table, pick, ((0,), (0,)))
        features_ref[m, stencil_rows:, :] = forcing.astype(BF)
        features = features_ref[m]
        preact = dot(w_hidden, features) + bias
        logistic = 1.0 / (1.0 + jnp.exp(-preact))
        hidden = (preact * logistic).astype(BF)
        part = slice(m * channels, (m + 1) * channels)
        moist = state[part] + dot(w_tendency, hidden)
        store_split(next_ref, m * channels, moist - split_dot(moist, high, low))
        moist_grad = moist_grad_ref[part, :]
        tendency_grad = moist_grad.astype(BF)
        hidden_grad = dot(w_tendency, tendency_grad, ((0,), (0,)))
        preact_grad = (hidden_grad * logistic * (1.0 + preact * (1.0 - logistic))).astype(BF)
        grad_out += dot(tendency_grad, hidden, ((1,), (1,)))
        grad_in += dot(preact_grad, features, ((1,), (1,)))
        grad_bias += dot(ones, preact_grad, ((1,), (1,)))
        stencil_grad = dot(w_hidden[:, :stencil_rows], preact_grad, ((0,), (0,)))
        sums = []
        for a in range(3):
            total = None
            for b in range(3):
                start = (3 * a + b) * channels
                piece = stencil_grad[start : start + channels]
                if b != 1:
                    piece = pltpu.roll(piece, (b - 1) % lon_total, 1)
                total = piece if total is None else total + piece
            sums.append(total)
        store_split(to_north_ref, m * channels, sums[0])
        store_split(grad_ref, m * channels, moist_grad + sums[1])
        store_split(to_south_ref, m * channels, sums[2])

    shares, share_rows = weights_ref.shape[:2]
    bias_high = grad_bias[0:1].astype(BF).astype(F32)
    bias_low = grad_bias[0:1] - bias_high
    tiles = hidden_units // LANES
    bias_rows = [half[:, t * LANES : (t + 1) * LANES] for half in (bias_high, bias_low) for t in range(tiles)]
    bias_rows = jnp.concatenate(bias_rows + [jnp.zeros((8 - 2 * tiles, LANES), F32)], axis=0)
    for p in range(shares):
        pieces = []
        for value in (grad_in, grad_out):
            count = value.shape[0] // shares
            for t in range(value.shape[1] // LANES):
                pieces.append(value[p * count : (p + 1) * count, t * LANES : (t + 1) * LANES])
        weights_ref[p] = jnp.concatenate(pieces + [bias_rows], axis=0).astype(BF)


def near_sum_kernel(parts_ref, next_ref, grad_ref, south_ref, north_ref, share_ref, out_ref, sum_ref):
    sectors, rows = next_ref.shape[:2]
    for s in range(sectors):
        out_ref[s, :rows, :] = next_ref[s]
        total = grad_ref[s] + south_ref[s].astype(F32) + north_ref[s].astype(F32)
        out_ref[s, rows:, :] = total.astype(BF)
    total = parts_ref[0].astype(F32)
    for p in range(1, parts_ref.shape[0]):
        total = total + parts_ref[p].astype(F32)
    sum_ref[...] = total
    pieces, piece_rows = share_ref.shape[:2]
    for p in range(pieces):
        share_ref[p] = sum_ref[p * piece_rows : (p + 1) * piece_rows, :]


def spread_kernel(pieces_ref, shares_ref, sum_ref):
    pieces, piece_rows = pieces_ref.shape[:2]
    for p in range(pieces):
        sum_ref[p * piece_rows : (p + 1) * piece_rows, :] = pieces_ref[p].astype(F32)
    share = sum_ref[...].astype(BF)
    for p in range(shares_ref.shape[0]):
        shares_ref[p] = share


def unpack_kernel(scaling, shares_ref, grad_in_ref, grad_bias_ref, grad_out_ref):
    shares = shares_ref.shape[0]
    for p in range(shares):
        share = shares_ref[p].astype(F32) * scaling
        start = 0
        for ref in (grad_in_ref, grad_out_ref):
            count = ref.shape[0] // shares
            for t in range(ref.shape[1] // LANES):
                ref[p * count : (p + 1) * count, t * LANES : (t + 1) * LANES] = share[
                    start : start + count
                ]
                start += count
        if p == 0:
            tiles = grad_bias_ref.shape[0] // LANES
            for t in range(tiles):
                both = share[start + t : start + t + 1] + share[start + tiles + t : start + tiles + t + 1]
                grad_bias_ref[t * LANES : (t + 1) * LANES] = both[0]


def call(kernel, outs, scratch=(), smem_first=False, flops=0, inputs=0):
    vmem = pl.BlockSpec(memory_space=pltpu.VMEM)
    specs = [vmem] * inputs
    if smem_first:
        specs[0] = pl.BlockSpec(memory_space=pltpu.SMEM)
    return pl.pallas_call(
        kernel,
        out_shape=outs,
        in_specs=specs,
        out_specs=jax.tree.map(lambda _: vmem, outs),
        scratch_shapes=list(scratch),
        cost_estimate=pl.CostEstimate(flops=flops, bytes_accessed=4_000_000, transcendentals=0),
        compiler_params=pltpu.CompilerParams(vmem_limit_bytes=VMEM_BYTES),
    )


def exchange(x, axes):
    return lax.all_to_all(x, axes, 0, 0, tiled=True)


def on_device(
    column_state,
    cotangent,
    land_mask,
    orography,
    member_seeds,
    land_table,
    relief_table,
    seed_table,
    w_hidden,
    b_hidden,
    w_tendency,
):
    members, channels, band, lon_cols = column_state.shape
    hidden_units, in_channels = w_hidden.shape
    classes = relief_table.shape[0]
    sectors = lax.axis_size("lon")
    lat_total = band * lax.axis_size(("ylo", "z", "core"))
    lon_total = lon_cols * sectors
    rows = members * channels
    shape = jax.ShapeDtypeStruct

    with jax.named_scope("rows_in"):
        def by_row(*refs):
            by_row_kernel(*refs[:4], classes, *refs[4:])

        flat = (members, channels * band, lon_cols)
        state_rows, adjoint_rows = call(
            by_row,
            (shape((band, rows, lon_cols), F32), shape((band, rows + 8, lon_cols), F32)),
            inputs=4,
        )(column_state.reshape(flat), cotangent.reshape(flat), land_mask, orography)
        row = exchange(state_rows, "lon")
        adjoint_row = exchange(adjoint_rows, "lon")

    with jax.named_scope("row_halo"):
        peers = lax.axis_size(ROWS_AXES)
        south_going = [(i, i + 1) for i in range(peers - 1)]
        north_going = [(j, i) for i, j in south_going]
        edge = row.astype(BF)
        north = lax.ppermute(edge, ROWS_AXES, south_going)
        south = lax.ppermute(edge, ROWS_AXES, north_going)

    with jax.named_scope("adjoint_filter"):
        moist_grad, high, low = call(
            adjoint_filter_kernel,
            (
                shape((rows, lon_total), F32),
                shape((lon_total, lon_total), BF),
                shape((lon_total, lon_total), BF),
            ),
            smem_first=True,
            inputs=3,
            flops=6 * rows * lon_total * lon_total,
        )(
            lax.axis_index(ROWS_AXES).reshape(1),
            adjoint_row,
            jnp.asarray(filter_kernels(lat_total, lon_total)),
        )

    near = lax.axis_size(NEAR)
    middle = lax.axis_size(MIDDLE)
    length = lax.axis_size("z")
    share_rows = (hidden_units * in_channels + channels * hidden_units) // (LANES * near) + 8
    piece_rows = share_rows // middle
    with jax.named_scope("columns"):
        block = (sectors, rows, LANES)
        next_rows, grad_rows, to_north, to_south, weights = call(
            column_kernel,
            (
                shape(block, BF),
                shape(block, F32),
                shape(block, BF),
                shape(block, BF),
                shape((near, share_rows, LANES), BF),
            ),
            scratch=[pltpu.VMEM((members, in_channels, lon_total), BF)],
            smem_first=True,
            inputs=14,
            flops=4_000_000_000,
        )(
            member_seeds,
            row,
            adjoint_row,
            north,
            south,
            moist_grad,
            high,
            low,
            land_table,
            relief_table,
            seed_table,
            w_hidden,
            b_hidden.reshape(1, hidden_units),
            w_tendency,
        )

    with jax.named_scope("gradient_halo"):
        from_south = lax.ppermute(to_north, ROWS_AXES, north_going)
        from_north = lax.ppermute(to_south, ROWS_AXES, south_going)

    with jax.named_scope("weights_near"):
        parts = exchange(weights, NEAR)
        share, outgoing = call(
            near_sum_kernel,
            (shape((middle, piece_rows, LANES), F32), shape((sectors, 2 * rows, LANES), BF)),
            scratch=[pltpu.VMEM((share_rows, LANES), F32)],
            inputs=5,
        )(parts, next_rows, grad_rows, from_south, from_north)

    with jax.named_scope("weights_middle"):
        parts = exchange(share, MIDDLE)
        piece = jnp.sum(parts, 0, keepdims=True).astype(BF)

    with jax.named_scope("rows_out"):
        blocks = exchange(outgoing, "lon")

        def by_band(values):
            values = values.reshape(band, members, channels, lon_cols).astype(F32)
            return jnp.transpose(values, (1, 2, 0, 3))

        next_state = by_band(blocks[:, :rows])
        state_grad = by_band(blocks[:, rows:])

    with jax.named_scope("weights_length"):
        parts = exchange(jnp.broadcast_to(piece, (length, piece_rows, LANES)), "z")
        piece = jnp.sum(parts.astype(F32), 0, keepdims=True).astype(BF)

    with jax.named_scope("weights_back"):
        pieces = exchange(jnp.broadcast_to(piece, (middle, piece_rows, LANES)), MIDDLE)
        spread = call(
            spread_kernel,
            shape((near, share_rows, LANES), BF),
            scratch=[pltpu.VMEM((share_rows, LANES), F32)],
            inputs=1,
        )(pieces)
        shares = exchange(spread, NEAR)
        columns = members * lax.axis_size("mem") * lat_total * lon_total

        def unpack(*refs):
            unpack_kernel(1.0 / math.sqrt(columns), *refs)

        grad_in, grad_bias, grad_out = call(
            unpack,
            (
                shape((hidden_units, in_channels), F32),
                shape((hidden_units,), F32),
                shape((channels, hidden_units), F32),
            ),
            inputs=1,
        )(shares)
    return next_state, state_grad, grad_in, grad_bias, grad_out


def solution(mesh):
    lat, lon, mem = mesh.devices.shape
    devices = mesh.devices.reshape(2, lat // 4, 2, lon, mem)
    split = Mesh(devices, ("ylo", "z", "core", "lon", "mem"))
    lat_axes = ("ylo", "z", "core")
    field = P("mem", None, lat_axes, "lon")
    surface = P(lat_axes, "lon")
    whole = P()
    return jax.shard_map(
        on_device,
        mesh=split,
        in_specs=(field, field, surface, surface, P("mem")) + (whole,) * 6,
        out_specs=(field, field, whole, whole, whole),
        check_vma=False,
    )
```

```python
import math

import jax
import jax.numpy as jnp
import numpy as np
from jax import lax
from jax.experimental import pallas as pl
from jax.experimental.pallas import tpu as pltpu
from jax.sharding import Mesh, PartitionSpec as P

MODES = 171
DAMP = 2.0
LANES = 128
BF = jnp.bfloat16
F32 = jnp.float32
MIB = 1024 * 1024
PLACE = ("ylo", "z", "core", "lon")
NEAR = ("core", "mem", "ylo")
BIAS_ROWS = 8


def whole_multiple(value, unit):
    return -(-value // unit) * unit


def filter_tables(lat_total, lon_total):
    padded = whole_multiple(2 * MODES, LANES)
    k = np.arange(MODES)
    angles = (k[:, None] * np.arange(lon_total)[None]) % lon_total * (2.0 * math.pi / lon_total)
    analysis = np.zeros((padded, lon_total))
    analysis[: 2 * MODES] = np.concatenate([np.cos(angles), np.sin(angles)], 0)
    lat = math.pi * ((np.arange(lat_total) + 0.5) / lat_total - 0.5)
    removal = 1.0 - np.exp(-DAMP * (k[None] / MODES) ** 2 / np.cos(lat)[:, None] ** 2)
    removal = removal * np.where(k == 0, 1.0, 2.0) / lon_total
    scale = np.zeros((lat_total, padded), np.float32)
    scale[:, : 2 * MODES] = np.concatenate([removal, removal], 1)
    high = analysis.astype(np.float32).astype(BF)
    low = (analysis - high.astype(np.float64)).astype(np.float32).astype(BF)
    return high, low, scale


def dot(a, b, dims=((1,), (0,))):
    return lax.dot_general(a, b, (dims, ((), ())), preferred_element_type=F32)


def split_dot(x, high, low, dims=((1,), (0,))):
    x_high = x.astype(BF)
    x_low = (x - x_high.astype(F32)).astype(BF)
    return dot(x_high, high, dims) + (dot(x_low, high, dims) + dot(x_high, low, dims))


def filtered(x, scale, high, low):
    coeffs = split_dot(x, high, low, ((1,), (1,))) * scale
    return x - split_dot(coeffs, high, low)


def joined(ref, start, rows):
    return jnp.concatenate([ref[s, start : start + rows, :] for s in range(ref.shape[0])], axis=1)


def store_split(ref, start, value):
    for s in range(ref.shape[0]):
        ref[s, start : start + value.shape[0], :] = value[:, s * LANES : (s + 1) * LANES].astype(
            ref.dtype
        )


def by_row_kernel(state_ref, cotangent_ref, land_ref, orography_ref, out_ref, adjoint_ref, *, classes):
    sectors, rows = out_ref.shape[:2]
    members = state_ref.shape[0]
    band = land_ref.shape[0]
    taken = band * members // sectors
    channels = rows // taken
    code = (jnp.where(land_ref[...] == 1, classes, 0) + orography_ref[...]).astype(F32)
    for q in range(sectors):
        m, first = q * taken // band, q * taken % band
        for k in range(taken):
            picked = pl.ds(first + k, channels, stride=band)
            out_ref[q, k * channels : (k + 1) * channels, :] = state_ref[m, picked, :]
            adjoint_ref[q, k * channels : (k + 1) * channels, :] = cotangent_ref[m, picked, :]
        spare = jnp.zeros((8 - taken, LANES), F32)
        adjoint_ref[q, rows:, :] = jnp.concatenate([code[first : first + taken], spare], axis=0)


def own_scale(place, scale_ref, taken, sectors, band, rows):
    first = place // sectors * band + place % (band // taken) * taken
    channels = rows // taken
    wide = (channels, scale_ref.shape[1])
    return jnp.concatenate(
        [jnp.broadcast_to(scale_ref[pl.ds(first + k, 1), :], wide) for k in range(taken)], axis=0
    )


def adjoint_filter_kernel(
    place_ref, row_ref, scale_ref, high_ref, low_ref, moist_grad_ref, *, taken, band
):
    rows = moist_grad_ref.shape[0]
    scale = own_scale(place_ref[0], scale_ref, taken, row_ref.shape[0], band, rows)
    cotangent = joined(row_ref, 0, rows)
    moist_grad_ref[...] = filtered(cotangent, scale, high_ref[...], low_ref[...])


def column_kernel(
    place_ref,
    seeds_ref,
    row_ref,
    adjoint_ref,
    north_ref,
    south_ref,
    moist_grad_ref,
    scale_ref,
    high_ref,
    low_ref,
    land_ref,
    relief_ref,
    seed_ref,
    w_hidden_ref,
    b_hidden_ref,
    w_tendency_ref,
    next_ref,
    grad_ref,
    to_north_ref,
    to_south_ref,
    weights_ref,
    features_ref,
    stage_ref,
    *,
    band,
):
    taken = features_ref.shape[0]
    sectors = row_ref.shape[0]
    channels = w_tendency_ref.shape[0]
    hidden_units, in_channels = w_hidden_ref.shape
    rows = taken * channels
    stencil_rows = 9 * channels
    lon_total = features_ref.shape[2]
    classes = relief_ref.shape[0]
    place = place_ref[0]

    state = joined(row_ref, 0, rows)
    rounded = state.astype(BF).astype(F32)
    sources = [joined(north_ref, 0, channels).astype(F32)]
    sources += [rounded[k * channels : (k + 1) * channels] for k in range(taken)]
    sources += [joined(south_ref, 0, channels).astype(F32)]
    for j, source in enumerate(sources):
        for b in range(3):
            moved = source if b == 1 else pltpu.roll(source, (1 - b) % lon_total, 1)
            moved = moved.astype(BF)
            for a in range(3):
                if 0 <= j - a < taken:
                    start = (3 * a + b) * channels
                    features_ref[j - a, start : start + channels, :] = moved
    class_ids = lax.broadcasted_iota(jnp.int32, (2 * classes, lon_total), 0).astype(F32)
    codes = joined(adjoint_ref, rows, 8)
    surface = jnp.concatenate(
        [land_ref[0:1, :] + relief_ref[...], land_ref[1:2, :] + relief_ref[...]], axis=0
    )
    seed = seeds_ref[place % sectors * taken // band]
    table = (surface + seed_ref[pl.ds(seed, 1), :]).astype(BF)
    bias = jnp.transpose(jnp.broadcast_to(b_hidden_ref[...], (8, hidden_units)))[:, 0:1]
    w_hidden = w_hidden_ref[...]
    w_tendency = w_tendency_ref[...]
    grad_in = jnp.zeros((hidden_units, in_channels), F32)
    grad_out = jnp.zeros((channels, hidden_units), F32)
    grad_bias = jnp.zeros((16, hidden_units), F32)
    ones = jnp.ones((16, lon_total), BF)
    moist = []
    sums = []
    for k in range(taken):
        pick = jnp.where(class_ids == codes[k : k + 1], 1.0, 0.0).astype(BF)
        features_ref[k, stencil_rows:, :] = dot(table, pick, ((0,), (0,))).astype(BF)
        features = features_ref[k]
        preact = dot(w_hidden, features) + bias
        logistic = 1.0 / (1.0 + jnp.exp(-preact))
        hidden = (preact * logistic).astype(BF)
        part = slice(k * channels, (k + 1) * channels)
        moist.append(state[part] + dot(w_tendency, hidden))
        tendency_grad = moist_grad_ref[part, :].astype(BF)
        hidden_grad = dot(w_tendency, tendency_grad, ((0,), (0,)))
        preact_grad = (hidden_grad * logistic * (1.0 + preact * (1.0 - logistic))).astype(BF)
        grad_out += dot(tendency_grad, hidden, ((1,), (1,)))
        grad_in += dot(preact_grad, features, ((1,), (1,)))
        grad_bias += dot(ones, preact_grad, ((1,), (1,)))
        stencil_grad = dot(w_hidden[:, :stencil_rows], preact_grad, ((0,), (0,)))
        sums.append([])
        for a in range(3):
            total = None
            for b in range(3):
                start = (3 * a + b) * channels
                piece = stencil_grad[start : start + channels]
                if b != 1:
                    piece = pltpu.roll(piece, (b - 1) % lon_total, 1)
                total = piece if total is None else total + piece
            sums[k].append(total)
    store_split(to_north_ref, 0, sums[0][0])
    store_split(to_south_ref, 0, sums[-1][2])
    for k in range(taken):
        total = moist_grad_ref[k * channels : (k + 1) * channels, :] + sums[k][1]
        if k > 0:
            total = total + sums[k - 1][2]
        if k + 1 < taken:
            total = total + sums[k + 1][0]
        store_split(grad_ref, k * channels, total)
    scale = own_scale(place, scale_ref, taken, sectors, band, rows)
    moist = jnp.concatenate(moist, axis=0)
    store_split(next_ref, 0, filtered(moist, scale, high_ref[...], low_ref[...]))

    bias_high = grad_bias[0:1].astype(BF).astype(F32)
    bias_low = grad_bias[0:1] - bias_high
    tiles = hidden_units // LANES
    shares, share_rows = weights_ref.shape[:2]
    stage_ref[...] = jnp.zeros(stage_ref.shape, F32)
    for p in range(shares):
        start = 0
        for value in (grad_in, grad_out):
            count = value.shape[0] // shares
            for t in range(value.shape[1] // LANES):
                stage_ref[p, start : start + count, :] = value[
                    p * count : (p + 1) * count, t * LANES : (t + 1) * LANES
                ]
                start += count
        if p == 0:
            for half in (bias_high, bias_low):
                for t in range(tiles):
                    stage_ref[p, start : start + 1, :] = half[:, t * LANES : (t + 1) * LANES]
                    start += 1
        weights_ref[p] = stage_ref[p].astype(BF)


def near_sum_kernel(
    parts_ref, next_ref, grad_ref, south_ref, north_ref, out_ref, sum_ref, stage_ref
):
    sectors, rows = next_ref.shape[:2]
    channels = south_ref.shape[1]
    total = parts_ref[0].astype(F32)
    for p in range(1, parts_ref.shape[0]):
        total = total + parts_ref[p].astype(F32)
    sum_ref[...] = total
    piece_rows = sum_ref.shape[0] // sectors
    half_rows = stage_ref.shape[0] // 2
    stage_ref[...] = jnp.zeros(stage_ref.shape, F32)
    for s in range(sectors):
        out_ref[s, :rows, :] = next_ref[s]
        part = grad_ref[s]
        first = part[:channels] + north_ref[s].astype(F32)
        last = part[rows - channels :] + south_ref[s].astype(F32)
        inner = [part[channels : rows - channels]] if rows > 2 * channels else []
        part = jnp.concatenate([first] + inner + [last], axis=0)
        out_ref[s, rows : 2 * rows, :] = part.astype(BF)
        piece = sum_ref[s * piece_rows : (s + 1) * piece_rows, :]
        high = piece.astype(BF).astype(F32)
        stage_ref[:piece_rows, :] = high
        stage_ref[half_rows : half_rows + piece_rows, :] = piece - high
        out_ref[s, 2 * rows :, :] = stage_ref[...].astype(BF)


def spread_kernel(pieces_ref, shares_ref, sum_ref):
    pieces, piece_rows = pieces_ref.shape[:2]
    for p in range(pieces):
        sum_ref[p * piece_rows : (p + 1) * piece_rows, :] = pieces_ref[p].astype(F32)
    share = sum_ref[...].astype(BF)
    for p in range(shares_ref.shape[0]):
        shares_ref[p] = share


def unpack_kernel(shares_ref, grad_in_ref, grad_bias_ref, grad_out_ref, stage_ref, *, scaling):
    shares = shares_ref.shape[0]
    for p in range(shares):
        stage_ref[p] = shares_ref[p].astype(F32) * scaling
        start = 0
        for ref in (grad_in_ref, grad_out_ref):
            count = ref.shape[0] // shares
            for t in range(ref.shape[1] // LANES):
                ref[p * count : (p + 1) * count, t * LANES : (t + 1) * LANES] = stage_ref[
                    p, start : start + count, :
                ]
                start += count
        if p == 0:
            tiles = grad_bias_ref.shape[0] // LANES
            for t in range(tiles):
                both = stage_ref[p, start + t, :] + stage_ref[p, start + tiles + t, :]
                grad_bias_ref[t * LANES : (t + 1) * LANES] = both


def call(kernel, outs, inputs, smem=0, scratch=(), flops=0, vmem=8, **static):
    on_vmem = pl.BlockSpec(memory_space=pltpu.VMEM)
    on_smem = pl.BlockSpec(memory_space=pltpu.SMEM)

    def body(*refs):
        kernel(*refs, **static)

    return pl.pallas_call(
        body,
        out_shape=outs,
        in_specs=[on_smem] * smem + [on_vmem] * (inputs - smem),
        out_specs=jax.tree.map(lambda _: on_vmem, outs),
        scratch_shapes=list(scratch),
        cost_estimate=pl.CostEstimate(flops=flops, bytes_accessed=1_000_000, transcendentals=0),
        compiler_params=pltpu.CompilerParams(vmem_limit_bytes=vmem * MIB),
    )


def exchange(x, axes):
    return lax.all_to_all(x, axes, 0, 0, tiled=True)


def on_device(
    column_state,
    cotangent,
    land_mask,
    orography,
    member_seeds,
    land_table,
    relief_table,
    seed_table,
    w_hidden,
    b_hidden,
    w_tendency,
):
    members, channels, band, lon_cols = column_state.shape
    hidden_units, in_channels = w_hidden.shape
    classes = relief_table.shape[0]
    sectors = lax.axis_size("lon")
    peers = lax.axis_size(PLACE)
    lat_total = band * (peers // sectors)
    lon_total = lon_cols * sectors
    taken = band * members // sectors
    groups = band // taken
    rows = taken * channels
    shape = jax.ShapeDtypeStruct

    with jax.named_scope("rows_in"):
        flat = (members, channels * band, lon_cols)
        state_rows, adjoint_rows = call(
            by_row_kernel,
            (shape((sectors, rows, lon_cols), F32), shape((sectors, rows + 8, lon_cols), F32)),
            4,
            classes=classes,
        )(column_state.reshape(flat), cotangent.reshape(flat), land_mask, orography)
        row = exchange(state_rows, "lon")
        adjoint_row = exchange(adjoint_rows, "lon")

    with jax.named_scope("row_halo"):
        south_going = []
        for i in range(peers):
            j = i + 1 if i % groups < groups - 1 else i + sectors - (groups - 1)
            if j < peers:
                south_going.append((i, j))
        north_going = [(j, i) for i, j in south_going]
        north = lax.ppermute(row[:, rows - channels :].astype(BF), PLACE, south_going)
        south = lax.ppermute(row[:, :channels].astype(BF), PLACE, north_going)

    place = lax.axis_index(PLACE).reshape(1)
    high, low, scale = [jnp.asarray(t) for t in filter_tables(lat_total, lon_total)]
    with jax.named_scope("adjoint_filter"):
        moist_grad = call(
            adjoint_filter_kernel,
            shape((rows, lon_total), F32),
            5,
            smem=1,
            flops=12 * rows * lon_total * high.shape[0],
            vmem=12,
            taken=taken,
            band=band,
        )(place, adjoint_row, scale, high, low)

    near = lax.axis_size(NEAR)
    length = lax.axis_size("z")
    filled = (hidden_units * in_channels + channels * hidden_units) // (LANES * near)
    share_rows = whole_multiple(filled + BIAS_ROWS, 16)
    piece_rows = share_rows // sectors
    half_rows = whole_multiple(piece_rows, 16)
    with jax.named_scope("columns"):
        block = (sectors, rows, LANES)
        edge = (sectors, channels, LANES)
        next_rows, grad_rows, to_north, to_south, weights = call(
            column_kernel,
            (
                shape(block, BF),
                shape(block, F32),
                shape(edge, BF),
                shape(edge, BF),
                shape((near, share_rows, LANES), BF),
            ),
            16,
            smem=2,
            scratch=[
                pltpu.VMEM((taken, in_channels, lon_total), BF),
                pltpu.VMEM((near, share_rows, LANES), F32),
            ],
            flops=4_000_000_000,
            vmem=32,
            band=band,
        )(
            place,
            member_seeds,
            row,
            adjoint_row,
            north,
            south,
            moist_grad,
            scale,
            high,
            low,
            land_table,
            relief_table,
            seed_table,
            w_hidden,
            b_hidden.reshape(1, hidden_units),
            w_tendency,
        )

    with jax.named_scope("gradient_halo"):
        from_south = lax.ppermute(to_north, PLACE, north_going)
        from_north = lax.ppermute(to_south, PLACE, south_going)

    with jax.named_scope("weights_near"):
        parts = exchange(weights, NEAR)
        outgoing = call(
            near_sum_kernel,
            shape((sectors, 2 * rows + 2 * half_rows, LANES), BF),
            5,
            scratch=[pltpu.VMEM((share_rows, LANES), F32), pltpu.VMEM((2 * half_rows, LANES), F32)],
        )(parts, next_rows, grad_rows, from_south, from_north)

    with jax.named_scope("rows_out"):
        blocks = exchange(outgoing, "lon")

        def by_band(values):
            values = values.reshape(members, groups, taken, channels, lon_cols).astype(F32)
            values = jnp.transpose(values, (0, 3, 1, 2, 4))
            return values.reshape(members, channels, band, lon_cols)

        next_state = by_band(blocks[:, :rows])
        state_grad = by_band(blocks[:, rows : 2 * rows])

    with jax.named_scope("weights_length"):
        start = 2 * rows
        highs = blocks[:, start : start + piece_rows].astype(F32)
        start += half_rows
        lows = blocks[:, start : start + piece_rows].astype(F32)
        piece = jnp.sum(highs + lows, 0, keepdims=True).astype(BF)
        parts = exchange(jnp.broadcast_to(piece, (length, piece_rows, LANES)), "z")
        piece = jnp.sum(parts.astype(F32), 0, keepdims=True).astype(BF)

    with jax.named_scope("weights_back"):
        pieces = exchange(jnp.broadcast_to(piece, (sectors, piece_rows, LANES)), "lon")
        spread = call(
            spread_kernel,
            shape((near, share_rows, LANES), BF),
            1,
            scratch=[pltpu.VMEM((share_rows, LANES), F32)],
        )(pieces)
        shares = exchange(spread, NEAR)
        columns = members * lax.axis_size("mem") * lat_total * lon_total
        grad_in, grad_bias, grad_out = call(
            unpack_kernel,
            (
                shape((hidden_units, in_channels), F32),
                shape((hidden_units,), F32),
                shape((channels, hidden_units), F32),
            ),
            1,
            scratch=[pltpu.VMEM((near, share_rows, LANES), F32)],
            scaling=1.0 / math.sqrt(columns),
        )(shares)
    return next_state, state_grad, grad_in, grad_bias, grad_out


def solution(mesh):
    lat, lon, mem = mesh.devices.shape
    devices = mesh.devices.reshape(2, lat // 4, 2, lon, mem)
    split = Mesh(devices, ("ylo", "z", "core", "lon", "mem"))
    lat_axes = ("ylo", "z", "core")
    field = P("mem", None, lat_axes, "lon")
    surface = P(lat_axes, "lon")
    whole = P()
    return jax.shard_map(
        on_device,
        mesh=split,
        in_specs=(field, field, surface, surface, P("mem")) + (whole,) * 6,
        out_specs=(field, field, whole, whole, whole),
        check_vma=False,
    )
```

```python
import math

import jax
import jax.numpy as jnp
import numpy as np
from jax import lax
from jax.experimental import pallas as pl
from jax.experimental.pallas import tpu as pltpu
from jax.sharding import Mesh, PartitionSpec as P

MODES = 171
DAMP = 2.0
LANES = 128
BF = jnp.bfloat16
F32 = jnp.float32
MIB = 1024 * 1024
PLACE = ("ylo", "z", "core", "lon")
NEAR = ("core", "mem", "ylo")
BIAS_ROWS = 8


def whole_multiple(value, unit):
    return -(-value // unit) * unit


def filter_tables(lat_total, lon_total):
    padded = whole_multiple(2 * MODES, LANES)
    k = np.arange(MODES)
    angles = (k[:, None] * np.arange(lon_total)[None]) % lon_total * (2.0 * math.pi / lon_total)
    analysis = np.zeros((padded, lon_total))
    analysis[: 2 * MODES] = np.concatenate([np.cos(angles), np.sin(angles)], 0)
    lat = math.pi * ((np.arange(lat_total) + 0.5) / lat_total - 0.5)
    removal = 1.0 - np.exp(-DAMP * (k[None] / MODES) ** 2 / np.cos(lat)[:, None] ** 2)
    removal = removal * np.where(k == 0, 1.0, 2.0) / lon_total
    scale = np.zeros((lat_total, padded), np.float32)
    scale[:, : 2 * MODES] = np.concatenate([removal, removal], 1)
    high = analysis.astype(np.float32).astype(BF)
    low = (analysis - high.astype(np.float64)).astype(np.float32).astype(BF)
    return high, low, scale


def dot(a, b, dims=((1,), (0,))):
    return lax.dot_general(a, b, (dims, ((), ())), preferred_element_type=F32)


def split_dot(x, high, low, dims=((1,), (0,))):
    x_high = x.astype(BF)
    x_low = (x - x_high.astype(F32)).astype(BF)
    return dot(x_high, high, dims) + (dot(x_low, high, dims) + dot(x_high, low, dims))


def filtered(x, scale, high, low):
    coeffs = split_dot(x, high, low, ((1,), (1,))) * scale
    return x - split_dot(coeffs, high, low)


def joined(ref, start, rows):
    return jnp.concatenate([ref[s, start : start + rows, :] for s in range(ref.shape[0])], axis=1)


def store_split(ref, start, value):
    for s in range(ref.shape[0]):
        ref[s, start : start + value.shape[0], :] = value[:, s * LANES : (s + 1) * LANES].astype(
            ref.dtype
        )


def by_row_kernel(
    state_hbm, cotangent_hbm, land_hbm, orography_hbm, out_ref, adjoint_ref,
    state_ref, cotangent_ref, land_ref, orography_ref, sems, *, classes
):
    moves = [
        pltpu.make_async_copy(source, target, sems.at[i])
        for i, (source, target) in enumerate(
            (
                (state_hbm, state_ref),
                (cotangent_hbm, cotangent_ref),
                (land_hbm, land_ref),
                (orography_hbm, orography_ref),
            )
        )
    ]
    for move in moves:
        move.start()
    sectors, rows = out_ref.shape[:2]
    members = state_ref.shape[0]
    band = land_ref.shape[0]
    taken = band * members // sectors
    channels = rows // taken
    for source, target, move in ((state_ref, out_ref, 0), (cotangent_ref, adjoint_ref, 1)):
        moves[move].wait()
        for q in range(sectors):
            m, first = q * taken // band, q * taken % band
            for k in range(taken):
                target[q, k * channels : (k + 1) * channels, :] = source[
                    m, pl.ds(first + k, channels, stride=band), :
                ]
    moves[2].wait()
    moves[3].wait()
    code = (jnp.where(land_ref[...] == 1, classes, 0) + orography_ref[...]).astype(F32)
    for q in range(sectors):
        first = q * taken % band
        spare = jnp.zeros((8 - taken, LANES), F32)
        adjoint_ref[q, rows:, :] = jnp.concatenate([code[first : first + taken], spare], axis=0)


def own_scale(place, scale_ref, taken, sectors, band, rows):
    first = place // sectors * band + place % (band // taken) * taken
    channels = rows // taken
    wide = (channels, scale_ref.shape[1])
    return jnp.concatenate(
        [jnp.broadcast_to(scale_ref[pl.ds(first + k, 1), :], wide) for k in range(taken)], axis=0
    )


def rolled(value, shift):
    return pltpu.roll(value, shift % value.shape[1], 1) if shift else value


def early_kernel(
    place_ref,
    seeds_ref,
    row_ref,
    adjoint_ref,
    scale_ref,
    high_ref,
    low_ref,
    land_ref,
    relief_ref,
    seed_ref,
    w_hidden_ref,
    b_hidden_ref,
    w_tendency_ref,
    moist_grad_ref,
    features_ref,
    preact_ref,
    hidden_grad_ref,
    *,
    band,
):
    taken = features_ref.shape[0]
    sectors = row_ref.shape[0]
    channels, hidden_units = w_tendency_ref.shape
    rows = taken * channels
    lon_total = features_ref.shape[2]
    classes = relief_ref.shape[0]
    place = place_ref[0]
    scale = own_scale(place, scale_ref, taken, sectors, band, rows)
    moist_grad = filtered(joined(adjoint_ref, 0, rows), scale, high_ref[...], low_ref[...])
    moist_grad_ref[...] = moist_grad
    rounded = joined(row_ref, 0, rows).astype(BF).astype(F32)
    for j in range(-1, taken + 1):
        for b in range(3):
            if 0 <= j < taken:
                moved = rolled(rounded[j * channels : (j + 1) * channels], 1 - b).astype(BF)
            else:
                moved = jnp.zeros((channels, lon_total), BF)
            for a in range(3):
                if 0 <= j + 1 - a < taken:
                    start = (3 * a + b) * channels
                    features_ref[j + 1 - a, start : start + channels, :] = moved
    class_ids = lax.broadcasted_iota(jnp.int32, (2 * classes, lon_total), 0).astype(F32)
    codes = joined(adjoint_ref, rows, 8)
    surface = jnp.concatenate(
        [land_ref[0:1, :] + relief_ref[...], land_ref[1:2, :] + relief_ref[...]], axis=0
    )
    seed = seeds_ref[place % sectors * taken // band]
    table = (surface + seed_ref[pl.ds(seed, 1), :]).astype(BF)
    bias = jnp.transpose(jnp.broadcast_to(b_hidden_ref[...], (8, hidden_units)))[:, 0:1]
    for k in range(taken):
        pick = jnp.where(class_ids == codes[k : k + 1], 1.0, 0.0).astype(BF)
        features_ref[k, 9 * channels :, :] = dot(table, pick, ((0,), (0,))).astype(BF)
        preact_ref[k] = dot(w_hidden_ref[...], features_ref[k]) + bias
        tendency_grad = moist_grad[k * channels : (k + 1) * channels].astype(BF)
        hidden_grad_ref[k] = dot(w_tendency_ref[...], tendency_grad, ((0,), (0,)))


def weights_kernel(
    north_ref,
    south_ref,
    moist_grad_ref,
    early_ref,
    preact_ref,
    hidden_grad_ref,
    w_hidden_ref,
    hidden_ref,
    preact_grad_ref,
    weights_ref,
    features_ref,
    stage_ref,
):
    taken, in_channels, lon_total = features_ref.shape
    channels = north_ref.shape[1]
    hidden_units = w_hidden_ref.shape[0]
    group = 3 * channels
    grad_in = jnp.zeros((hidden_units, in_channels), F32)
    grad_out = jnp.zeros((channels, hidden_units), F32)
    grad_bias = jnp.zeros((16, hidden_units), F32)
    ones = jnp.ones((16, lon_total), BF)
    for k in range(taken):
        features_ref[k] = early_ref[k]
        preact = preact_ref[k]
        for ref, a, row in ((north_ref, 0, 0), (south_ref, 2, taken - 1)):
            if row == k:
                edge = joined(ref, 0, channels).astype(F32)
                halo = jnp.concatenate([rolled(edge, 1 - b).astype(BF) for b in range(3)], axis=0)
                features_ref[k, a * group : (a + 1) * group, :] = halo
                preact = preact + dot(w_hidden_ref[:, a * group : (a + 1) * group], halo)
        logistic = 1.0 / (1.0 + jnp.exp(-preact))
        hidden = (preact * logistic).astype(BF)
        slope = logistic * (1.0 + preact * (1.0 - logistic))
        preact_grad = (hidden_grad_ref[k] * slope).astype(BF)
        hidden_ref[k] = hidden
        preact_grad_ref[k] = preact_grad
        tendency_grad = moist_grad_ref[k * channels : (k + 1) * channels, :].astype(BF)
        grad_out += dot(tendency_grad, hidden, ((1,), (1,)))
        grad_in += dot(preact_grad, features_ref[k], ((1,), (1,)))
        grad_bias += dot(ones, preact_grad, ((1,), (1,)))

    bias_high = grad_bias[0:1].astype(BF).astype(F32)
    bias_low = grad_bias[0:1] - bias_high
    tiles = hidden_units // LANES
    shares, share_rows = weights_ref.shape[:2]
    filled = (grad_in.size + grad_out.size) // (LANES * shares)
    for p in range(shares):
        stage_ref[p, filled // 8 * 8 :, :] = jnp.zeros((share_rows - filled // 8 * 8, LANES), F32)
        start = 0
        for value in (grad_in, grad_out):
            count = value.shape[0] // shares
            for t in range(value.shape[1] // LANES):
                stage_ref[p, start : start + count, :] = value[
                    p * count : (p + 1) * count, t * LANES : (t + 1) * LANES
                ]
                start += count
        if p == 0:
            for half in (bias_high, bias_low):
                for t in range(tiles):
                    stage_ref[p, start : start + 1, :] = half[:, t * LANES : (t + 1) * LANES]
                    start += 1
        weights_ref[p] = stage_ref[p].astype(BF)


def fields_kernel(
    place_ref,
    row_ref,
    moist_grad_ref,
    scale_ref,
    high_ref,
    low_ref,
    hidden_ref,
    preact_grad_ref,
    w_hidden_ref,
    w_tendency_ref,
    to_north_ref,
    to_south_ref,
    next_ref,
    grad_ref,
    *,
    band,
):
    taken = hidden_ref.shape[0]
    sectors, rows = row_ref.shape[:2]
    channels = rows // taken
    w_stencil = w_hidden_ref[:, : 9 * channels]
    sums = []
    for k in range(taken):
        stencil_grad = dot(w_stencil, preact_grad_ref[k], ((0,), (0,)))
        sums.append([])
        for a in range(3):
            total = None
            for b in range(3):
                start = (3 * a + b) * channels
                piece = rolled(stencil_grad[start : start + channels], b - 1)
                total = piece if total is None else total + piece
            sums[k].append(total)
    store_split(to_north_ref, 0, sums[0][0])
    store_split(to_south_ref, 0, sums[-1][2])
    for k in range(taken):
        total = moist_grad_ref[k * channels : (k + 1) * channels, :] + sums[k][1]
        if k > 0:
            total = total + sums[k - 1][2]
        if k + 1 < taken:
            total = total + sums[k + 1][0]
        store_split(grad_ref, k * channels, total)
    tendency = [dot(w_tendency_ref[...], hidden_ref[k]) for k in range(taken)]
    moist = joined(row_ref, 0, rows) + jnp.concatenate(tendency, axis=0)
    scale = own_scale(place_ref[0], scale_ref, taken, sectors, band, rows)
    store_split(next_ref, 0, filtered(moist, scale, high_ref[...], low_ref[...]))


def outgoing_kernel(place_ref, next_ref, grad_ref, south_ref, north_ref, *refs):
    sends, blocks_ref = refs[:-1], refs[-1]
    sectors, rows = next_ref.shape[:2]
    channels = south_ref.shape[1]
    for s in range(sectors):
        blocks_ref[s, :rows, :] = next_ref[s]
        part = grad_ref[s]
        first = part[:channels] + north_ref[s].astype(F32)
        last = part[rows - channels :] + south_ref[s].astype(F32)
        inner = [part[channels : rows - channels]] if rows > 2 * channels else []
        blocks_ref[s, rows:, :] = jnp.concatenate([first] + inner + [last], axis=0).astype(BF)
    for t in range(sectors):
        sends[t][...] = blocks_ref[(place_ref[0] + t) % sectors]


def by_band_kernel(place_ref, *refs, band):
    blocks_ref = refs[-1]
    outs = refs[-3:-1]
    sectors, rows = blocks_ref.shape[0], blocks_ref.shape[1] // 2
    members = outs[0].shape[0]
    taken = band * members // sectors
    channels = rows // taken
    for t in range(sectors):
        blocks_ref[t] = refs[t][...].astype(F32)
    for q in range(sectors):
        t = (place_ref[0] + sectors - q) % sectors
        m, first = q * taken // band, q * taken % band
        for i in range(2):
            for k in range(taken):
                start = i * rows + k * channels
                outs[i][m, pl.ds(first + k, channels, stride=band), :] = blocks_ref[
                    t, start : start + channels, :
                ]


def summed(ref):
    total = ref[0].astype(F32)
    for p in range(1, ref.shape[0]):
        total = total + ref[p].astype(F32)
    return total


def near_sum_kernel(parts_ref, *refs):
    pieces_ref, sum_ref = refs[-2:]
    sum_ref[...] = summed(parts_ref)
    pieces, piece_rows = pieces_ref.shape[:2]
    for p in range(pieces):
        pieces_ref[p] = sum_ref[p * piece_rows : (p + 1) * piece_rows, :]


def sum_and_copy_kernel(parts_ref, *refs):
    copies_ref = refs[-1]
    total = summed(parts_ref).astype(BF)
    for p in range(copies_ref.shape[0]):
        copies_ref[p] = total


def spread_kernel(pieces_ref, shares_ref, sum_ref):
    pieces, piece_rows = pieces_ref.shape[:2]
    for p in range(pieces):
        sum_ref[p * piece_rows : (p + 1) * piece_rows, :] = pieces_ref[p].astype(F32)
    share = sum_ref[...].astype(BF)
    for p in range(shares_ref.shape[0]):
        shares_ref[p] = share


def unpack_kernel(shares_ref, grad_in_ref, grad_bias_ref, grad_out_ref, stage_ref, *, scaling):
    shares = shares_ref.shape[0]
    for p in range(shares):
        stage_ref[p] = shares_ref[p].astype(F32) * scaling
        start = 0
        for ref in (grad_in_ref, grad_out_ref):
            count = ref.shape[0] // shares
            for t in range(ref.shape[1] // LANES):
                ref[p * count : (p + 1) * count, t * LANES : (t + 1) * LANES] = stage_ref[
                    p, start : start + count, :
                ]
                start += count
        if p == 0:
            tiles = grad_bias_ref.shape[0] // LANES
            for t in range(tiles):
                both = stage_ref[p, start + t, :] + stage_ref[p, start + tiles + t, :]
                grad_bias_ref[t * LANES : (t + 1) * LANES] = both


def call(kernel, outs, inputs, smem=0, scratch=(), flops=0, vmem=8, inputs_in=pltpu.VMEM, **static):
    on_vmem = pl.BlockSpec(memory_space=pltpu.VMEM)
    on_input = pl.BlockSpec(memory_space=inputs_in)
    on_smem = pl.BlockSpec(memory_space=pltpu.SMEM)

    def body(*refs):
        kernel(*refs, **static)

    return pl.pallas_call(
        body,
        out_shape=outs,
        in_specs=[on_smem] * smem + [on_input] * (inputs - smem),
        out_specs=jax.tree.map(lambda _: on_vmem, outs),
        scratch_shapes=list(scratch),
        cost_estimate=pl.CostEstimate(flops=flops, bytes_accessed=1_000_000, transcendentals=0),
        compiler_params=pltpu.CompilerParams(vmem_limit_bytes=vmem * MIB),
    )


def exchange(x, axes):
    return lax.all_to_all(x, axes, 0, 0, tiled=True)


def on_device(
    column_state,
    cotangent,
    land_mask,
    orography,
    member_seeds,
    land_table,
    relief_table,
    seed_table,
    w_hidden,
    b_hidden,
    w_tendency,
):
    members, channels, band, lon_cols = column_state.shape
    hidden_units, in_channels = w_hidden.shape
    classes = relief_table.shape[0]
    sectors = lax.axis_size("lon")
    peers = lax.axis_size(PLACE)
    lat_total = band * (peers // sectors)
    lon_total = lon_cols * sectors
    taken = band * members // sectors
    groups = band // taken
    rows = taken * channels
    shape = jax.ShapeDtypeStruct

    with jax.named_scope("rows_in"):
        flat = (members, channels * band, lon_cols)
        state_rows, adjoint_rows = call(
            by_row_kernel,
            (shape((sectors, rows, lon_cols), F32), shape((sectors, rows + 8, lon_cols), F32)),
            4,
            scratch=[
                pltpu.VMEM(flat, F32),
                pltpu.VMEM(flat, F32),
                pltpu.VMEM(land_mask.shape, land_mask.dtype),
                pltpu.VMEM(orography.shape, orography.dtype),
                pltpu.SemaphoreType.DMA((4,)),
            ],
            inputs_in=pltpu.HBM,
            classes=classes,
        )(column_state.reshape(flat), cotangent.reshape(flat), land_mask, orography)
        row = exchange(state_rows, "lon")
        adjoint_row = exchange(adjoint_rows, "lon")

    with jax.named_scope("row_halo"):
        south_going = []
        for i in range(peers):
            j = i + 1 if i % groups < groups - 1 else i + sectors - (groups - 1)
            if j < peers:
                south_going.append((i, j))
        north_going = [(j, i) for i, j in south_going]
        north = lax.ppermute(row[:, rows - channels :].astype(BF), PLACE, south_going)
        south = lax.ppermute(row[:, :channels].astype(BF), PLACE, north_going)

    place = lax.axis_index(PLACE).reshape(1)
    high, low, scale = [jnp.asarray(t) for t in filter_tables(lat_total, lon_total)]
    per_hidden = shape((taken, hidden_units, lon_total), F32)
    per_hidden_bf = shape((taken, hidden_units, lon_total), BF)
    features_shape = (taken, in_channels, lon_total)
    with jax.named_scope("early"):
        moist_grad, features, preact, hidden_grad = call(
            early_kernel,
            (shape((rows, lon_total), F32), shape(features_shape, BF), per_hidden, per_hidden),
            13,
            smem=2,
            flops=3_000_000_000,
            vmem=24,
            band=band,
        )(
            place,
            member_seeds,
            row,
            adjoint_row,
            scale,
            high,
            low,
            land_table,
            relief_table,
            seed_table,
            w_hidden,
            b_hidden.reshape(1, hidden_units),
            w_tendency,
        )

    near = lax.axis_size(NEAR)
    length = lax.axis_size("z")
    filled = (hidden_units * in_channels + channels * hidden_units) // (LANES * near)
    share_rows = whole_multiple(filled + BIAS_ROWS, 16)
    piece_rows = share_rows // sectors
    with jax.named_scope("weights"):
        hidden, preact_grad, weights = call(
            weights_kernel,
            (per_hidden_bf, per_hidden_bf, shape((near, share_rows, LANES), BF)),
            7,
            scratch=[
                pltpu.VMEM(features_shape, BF),
                pltpu.VMEM((near, share_rows, LANES), F32),
            ],
            flops=3_000_000_000,
            vmem=28,
        )(north, south, moist_grad, features, preact, hidden_grad, w_hidden)

    with jax.named_scope("fields"):
        block = (sectors, rows, LANES)
        edge = (sectors, channels, LANES)
        to_north, to_south, next_rows, grad_rows = call(
            fields_kernel,
            (shape(edge, BF), shape(edge, BF), shape(block, BF), shape(block, F32)),
            10,
            smem=1,
            flops=3_000_000_000,
            vmem=20,
            band=band,
        )(
            place,
            row,
            moist_grad,
            scale,
            high,
            low,
            hidden,
            preact_grad,
            w_hidden,
            w_tendency,
        )
        from_south = lax.ppermute(to_north, PLACE, north_going)
        from_north = lax.ppermute(to_south, PLACE, south_going)

    with jax.named_scope("weights_near"):
        parts = exchange(weights, NEAR)
        share = call(
            near_sum_kernel,
            shape((sectors, piece_rows, LANES), F32),
            3,
            scratch=[pltpu.VMEM((share_rows, LANES), F32)],
        )(parts, from_south, from_north)

    with jax.named_scope("rows_out"):
        sends = call(
            outgoing_kernel,
            (shape((2 * rows, LANES), BF),) * sectors,
            5,
            smem=1,
            scratch=[pltpu.VMEM((sectors, 2 * rows, LANES), BF)],
        )(place, next_rows, grad_rows, from_south, from_north)
        received = [sends[0]]
        for t in range(1, sectors):
            turn = [(i, (i + t) % sectors) for i in range(sectors)]
            received.append(lax.ppermute(sends[t], "lon", turn))
    with jax.named_scope("weights_middle"):
        copies = call(sum_and_copy_kernel, shape((length, piece_rows, LANES), BF), 2)(
            exchange(share, "lon"), received[1]
        )

    with jax.named_scope("weights_length"):
        copies = call(sum_and_copy_kernel, shape((sectors, piece_rows, LANES), BF), sectors - 1)(
            exchange(copies, "z"), *received[2:]
        )

    with jax.named_scope("bands_out"):
        next_state, state_grad = call(
            by_band_kernel,
            (shape(flat, F32), shape(flat, F32)),
            1 + sectors,
            smem=1,
            scratch=[pltpu.VMEM((sectors, 2 * rows, LANES), F32)],
            band=band,
        )(place, *received)
        next_state = next_state.reshape(column_state.shape)
        state_grad = state_grad.reshape(column_state.shape)

    with jax.named_scope("weights_back"):
        pieces = exchange(copies, "lon")
        spread = call(
            spread_kernel,
            shape((near, share_rows, LANES), BF),
            1,
            scratch=[pltpu.VMEM((share_rows, LANES), F32)],
        )(pieces)
        shares = exchange(spread, NEAR)
        columns = members * lax.axis_size("mem") * lat_total * lon_total
        grad_in, grad_bias, grad_out = call(
            unpack_kernel,
            (
                shape((hidden_units, in_channels), F32),
                shape((hidden_units,), F32),
                shape((channels, hidden_units), F32),
            ),
            1,
            scratch=[pltpu.VMEM((near, share_rows, LANES), F32)],
            scaling=1.0 / math.sqrt(columns),
        )(shares)
    return next_state, state_grad, grad_in, grad_bias, grad_out


def solution(mesh):
    lat, lon, mem = mesh.devices.shape
    devices = mesh.devices.reshape(2, lat // 4, 2, lon, mem)
    split = Mesh(devices, ("ylo", "z", "core", "lon", "mem"))
    lat_axes = ("ylo", "z", "core")
    field = P("mem", None, lat_axes, "lon")
    surface = P(lat_axes, "lon")
    whole = P()
    return jax.shard_map(
        on_device,
        mesh=split,
        in_specs=(field, field, surface, surface, P("mem")) + (whole,) * 6,
        out_specs=(field, field, whole, whole, whole),
        check_vma=False,
    )
```

```python
import math

import jax
import jax.numpy as jnp
import numpy as np
from jax import lax
from jax.experimental import pallas as pl
from jax.experimental.pallas import tpu as pltpu
from jax.sharding import Mesh, PartitionSpec as P

MODES = 171
DAMP = 2.0
LANES = 128
BF = jnp.bfloat16
F32 = jnp.float32
MIB = 1024 * 1024
PLACE = ("ylo", "z", "core", "lon")
NEAR = ("core", "mem", "ylo")
BIAS_ROWS = 8


def whole_multiple(value, unit):
    return -(-value // unit) * unit


def filter_tables(lat_total, lon_total):
    padded = whole_multiple(2 * MODES, LANES)
    k = np.arange(MODES)
    angles = (k[:, None] * np.arange(lon_total)[None]) % lon_total * (2.0 * math.pi / lon_total)
    analysis = np.zeros((padded, lon_total))
    analysis[: 2 * MODES] = np.concatenate([np.cos(angles), np.sin(angles)], 0)
    lat = math.pi * ((np.arange(lat_total) + 0.5) / lat_total - 0.5)
    removal = 1.0 - np.exp(-DAMP * (k[None] / MODES) ** 2 / np.cos(lat)[:, None] ** 2)
    removal = removal * np.where(k == 0, 1.0, 2.0) / lon_total
    scale = np.zeros((lat_total, padded), np.float32)
    scale[:, : 2 * MODES] = np.concatenate([removal, removal], 1)
    high = analysis.astype(np.float32).astype(BF)
    low = (analysis - high.astype(np.float64)).astype(np.float32).astype(BF)
    return high, low, scale


def dot(a, b, dims=((1,), (0,))):
    return lax.dot_general(a, b, (dims, ((), ())), preferred_element_type=F32)


def split_dot(x, high, low, dims=((1,), (0,))):
    x_high = x.astype(BF)
    x_low = (x - x_high.astype(F32)).astype(BF)
    return dot(x_high, high, dims) + (dot(x_low, high, dims) + dot(x_high, low, dims))


def filtered(x, scale, high, low):
    coeffs = split_dot(x, high, low, ((1,), (1,))) * scale
    return x - split_dot(coeffs, high, low)


def joined(ref, start, rows):
    return jnp.concatenate([ref[s, start : start + rows, :] for s in range(ref.shape[0])], axis=1)


def store_split(ref, start, value):
    for s in range(ref.shape[0]):
        ref[s, start : start + value.shape[0], :] = value[:, s * LANES : (s + 1) * LANES].astype(
            ref.dtype
        )


def by_row_kernel(
    state_hbm, cotangent_hbm, land_hbm, orography_hbm, out_ref,
    state_ref, cotangent_ref, land_ref, orography_ref, sems, *, classes
):
    sources = (state_hbm, cotangent_hbm, land_hbm, orography_hbm)
    targets = (state_ref, cotangent_ref, land_ref, orography_ref)
    moves = [
        pltpu.make_async_copy(source, target, sems.at[i])
        for i, (source, target) in enumerate(zip(sources, targets))
    ]
    for move in moves:
        move.start()
    sectors, rows = out_ref.shape[0], (out_ref.shape[1] - 8) // 2
    members = state_ref.shape[0]
    band = land_ref.shape[0]
    taken = band * members // sectors
    channels = rows // taken
    for i in range(2):
        moves[i].wait()
        for q in range(sectors):
            m, first = q * taken // band, q * taken % band
            for k in range(taken):
                start = i * rows + k * channels
                out_ref[q, start : start + channels, :] = targets[i][
                    m, pl.ds(first + k, channels, stride=band), :
                ]
    moves[2].wait()
    moves[3].wait()
    code = (jnp.where(land_ref[...] == 1, classes, 0) + orography_ref[...]).astype(F32)
    for q in range(sectors):
        first = q * taken % band
        spare = jnp.zeros((8 - taken, LANES), F32)
        out_ref[q, 2 * rows :, :] = jnp.concatenate([code[first : first + taken], spare], axis=0)


def own_scale(place, scale_ref, taken, sectors, band, rows):
    first = place // sectors * band + place % (band // taken) * taken
    channels = rows // taken
    wide = (channels, scale_ref.shape[1])
    return jnp.concatenate(
        [jnp.broadcast_to(scale_ref[pl.ds(first + k, 1), :], wide) for k in range(taken)], axis=0
    )


def rolled(value, shift):
    return pltpu.roll(value, shift % value.shape[1], 1) if shift else value


def early_kernel(
    place_ref,
    seeds_ref,
    row_ref,
    scale_ref,
    high_ref,
    low_ref,
    land_ref,
    relief_ref,
    seed_ref,
    w_hidden_ref,
    b_hidden_ref,
    w_tendency_ref,
    moist_grad_ref,
    features_ref,
    preact_ref,
    hidden_grad_ref,
    *,
    band,
):
    taken = features_ref.shape[0]
    sectors = row_ref.shape[0]
    channels, hidden_units = w_tendency_ref.shape
    rows = taken * channels
    lon_total = features_ref.shape[2]
    classes = relief_ref.shape[0]
    place = place_ref[0]
    scale = own_scale(place, scale_ref, taken, sectors, band, rows)
    moist_grad = filtered(joined(row_ref, rows, rows), scale, high_ref[...], low_ref[...])
    moist_grad_ref[...] = moist_grad
    rounded = joined(row_ref, 0, rows).astype(BF).astype(F32)
    for j in range(-1, taken + 1):
        for b in range(3):
            if 0 <= j < taken:
                moved = rolled(rounded[j * channels : (j + 1) * channels], 1 - b).astype(BF)
            else:
                moved = jnp.zeros((channels, lon_total), BF)
            for a in range(3):
                if 0 <= j + 1 - a < taken:
                    start = (3 * a + b) * channels
                    features_ref[j + 1 - a, start : start + channels, :] = moved
    class_ids = lax.broadcasted_iota(jnp.int32, (2 * classes, lon_total), 0).astype(F32)
    codes = joined(row_ref, 2 * rows, 8)
    surface = jnp.concatenate(
        [land_ref[0:1, :] + relief_ref[...], land_ref[1:2, :] + relief_ref[...]], axis=0
    )
    seed = seeds_ref[place % sectors * taken // band]
    table = (surface + seed_ref[pl.ds(seed, 1), :]).astype(BF)
    bias = jnp.transpose(jnp.broadcast_to(b_hidden_ref[...], (8, hidden_units)))[:, 0:1]
    for k in range(taken):
        pick = jnp.where(class_ids == codes[k : k + 1], 1.0, 0.0).astype(BF)
        features_ref[k, 9 * channels :, :] = dot(table, pick, ((0,), (0,))).astype(BF)
        preact_ref[k] = dot(w_hidden_ref[...], features_ref[k]) + bias
        tendency_grad = moist_grad[k * channels : (k + 1) * channels].astype(BF)
        hidden_grad_ref[k] = dot(w_tendency_ref[...], tendency_grad, ((0,), (0,)))


def weights_kernel(
    north_ref,
    south_ref,
    row_ref,
    moist_grad_ref,
    early_ref,
    preact_ref,
    hidden_grad_ref,
    w_hidden_ref,
    w_tendency_ref,
    to_north_ref,
    to_south_ref,
    moist_ref,
    grad_ref,
    weights_ref,
    features_ref,
    stage_ref,
):
    taken, in_channels, lon_total = features_ref.shape
    channels, hidden_units = w_tendency_ref.shape
    group = 3 * channels
    w_stencil = w_hidden_ref[:, : 3 * group]
    state = joined(row_ref, 0, taken * channels)
    grad_in = jnp.zeros((hidden_units, in_channels), F32)
    grad_out = jnp.zeros((channels, hidden_units), F32)
    grad_bias = jnp.zeros((16, hidden_units), F32)
    ones = jnp.ones((16, lon_total), BF)
    sums = []
    for k in range(taken):
        part = slice(k * channels, (k + 1) * channels)
        features_ref[k] = early_ref[k]
        preact = preact_ref[k]
        for ref, a, row in ((north_ref, 0, 0), (south_ref, 2, taken - 1)):
            if row == k:
                edge = joined(ref, 0, channels).astype(F32)
                halo = jnp.concatenate([rolled(edge, 1 - b).astype(BF) for b in range(3)], axis=0)
                features_ref[k, a * group : (a + 1) * group, :] = halo
                preact = preact + dot(w_hidden_ref[:, a * group : (a + 1) * group], halo)
        logistic = 0.5 + 0.5 * jnp.tanh(0.5 * preact)
        hidden = (preact * logistic).astype(BF)
        slope = logistic * (1.0 + preact * (1.0 - logistic))
        preact_grad = (hidden_grad_ref[k] * slope).astype(BF)
        tendency_grad = moist_grad_ref[part, :].astype(BF)
        grad_out += dot(tendency_grad, hidden, ((1,), (1,)))
        grad_in += dot(preact_grad, features_ref[k], ((1,), (1,)))
        grad_bias += dot(ones, preact_grad, ((1,), (1,)))
        moist_ref[part, :] = state[part] + dot(w_tendency_ref[...], hidden)
        stencil_grad = dot(w_stencil, preact_grad, ((0,), (0,)))
        sums.append([])
        for a in range(3):
            total = None
            for b in range(3):
                start = (3 * a + b) * channels
                piece = rolled(stencil_grad[start : start + channels], b - 1)
                total = piece if total is None else total + piece
            sums[k].append(total)
    store_split(to_north_ref, 0, sums[0][0])
    store_split(to_south_ref, 0, sums[-1][2])
    for k in range(taken):
        total = moist_grad_ref[k * channels : (k + 1) * channels, :] + sums[k][1]
        if k > 0:
            total = total + sums[k - 1][2]
        if k + 1 < taken:
            total = total + sums[k + 1][0]
        store_split(grad_ref, k * channels, total)

    bias_high = grad_bias[0:1].astype(BF).astype(F32)
    bias_low = grad_bias[0:1] - bias_high
    tiles = hidden_units // LANES
    shares, share_rows = weights_ref.shape[:2]
    filled = (grad_in.size + grad_out.size) // (LANES * shares)
    for p in range(shares):
        stage_ref[p, filled // 8 * 8 :, :] = jnp.zeros((share_rows - filled // 8 * 8, LANES), F32)
        start = 0
        for value in (grad_in, grad_out):
            count = value.shape[0] // shares
            for t in range(value.shape[1] // LANES):
                stage_ref[p, start : start + count, :] = value[
                    p * count : (p + 1) * count, t * LANES : (t + 1) * LANES
                ]
                start += count
        if p == 0:
            for half in (bias_high, bias_low):
                for t in range(tiles):
                    stage_ref[p, start : start + 1, :] = half[:, t * LANES : (t + 1) * LANES]
                    start += 1
        weights_ref[p] = stage_ref[p].astype(BF)


def fields_kernel(
    place_ref, moist_ref, scale_ref, high_ref, low_ref, grad_ref, south_ref, north_ref, out_ref,
    *, band
):
    sectors, rows = grad_ref.shape[:2]
    channels = south_ref.shape[1]
    scale = own_scale(place_ref[0], scale_ref, rows // channels, sectors, band, rows)
    store_split(out_ref, 0, filtered(moist_ref[...], scale, high_ref[...], low_ref[...]))
    for s in range(sectors):
        part = grad_ref[s]
        first = part[:channels] + north_ref[s].astype(F32)
        last = part[rows - channels :] + south_ref[s].astype(F32)
        inner = [part[channels : rows - channels]] if rows > 2 * channels else []
        out_ref[s, rows:, :] = jnp.concatenate([first] + inner + [last], axis=0).astype(BF)


def summed(ref):
    total = ref[0].astype(F32)
    for p in range(1, ref.shape[0]):
        total = total + ref[p].astype(F32)
    return total


def near_sum_kernel(parts_ref, *refs):
    pieces_ref, sum_ref = refs[-2:]
    sum_ref[...] = summed(parts_ref)
    pieces, piece_rows = pieces_ref.shape[:2]
    for p in range(pieces):
        pieces_ref[p] = sum_ref[p * piece_rows : (p + 1) * piece_rows, :]


def sum_and_copy_kernel(parts_ref, *refs):
    copies_ref = refs[-1]
    total = summed(parts_ref).astype(BF)
    for p in range(copies_ref.shape[0]):
        copies_ref[p] = total


def join_kernel(parts_ref, fields_ref, out_ref, stage_ref):
    rows, piece_rows = fields_ref.shape[1], parts_ref.shape[1]
    stage_ref[...] = jnp.zeros(stage_ref.shape, F32)
    stage_ref[:piece_rows, :] = summed(parts_ref)
    for s in range(out_ref.shape[0]):
        out_ref[s, :rows, :] = fields_ref[s]
        out_ref[s, rows:, :] = stage_ref[...].astype(BF)


def spread_kernel(blocks_ref, shares_ref, sum_ref, *, start):
    pieces = blocks_ref.shape[0]
    piece_rows = shares_ref.shape[1] // pieces
    for p in range(pieces):
        piece = blocks_ref[p, start:, :].astype(F32)
        sum_ref[p * piece_rows : (p + 1) * piece_rows, :] = piece[:piece_rows]
    share = sum_ref[...].astype(BF)
    for p in range(shares_ref.shape[0]):
        shares_ref[p] = share


def unpack_kernel(shares_ref, grad_in_ref, grad_bias_ref, grad_out_ref, stage_ref, *, scaling):
    shares = shares_ref.shape[0]
    for p in range(shares):
        stage_ref[p] = shares_ref[p].astype(F32) * scaling
        start = 0
        for ref in (grad_in_ref, grad_out_ref):
            count = ref.shape[0] // shares
            for t in range(ref.shape[1] // LANES):
                ref[p * count : (p + 1) * count, t * LANES : (t + 1) * LANES] = stage_ref[
                    p, start : start + count, :
                ]
                start += count
        if p == 0:
            tiles = grad_bias_ref.shape[0] // LANES
            for t in range(tiles):
                both = stage_ref[p, start + t, :] + stage_ref[p, start + tiles + t, :]
                grad_bias_ref[t * LANES : (t + 1) * LANES] = both


def call(kernel, outs, inputs, smem=0, scratch=(), flops=0, vmem=8, inputs_in=pltpu.VMEM, **static):
    on_vmem = pl.BlockSpec(memory_space=pltpu.VMEM)
    on_input = pl.BlockSpec(memory_space=inputs_in)
    on_smem = pl.BlockSpec(memory_space=pltpu.SMEM)

    def body(*refs):
        kernel(*refs, **static)

    return pl.pallas_call(
        body,
        out_shape=outs,
        in_specs=[on_smem] * smem + [on_input] * (inputs - smem),
        out_specs=jax.tree.map(lambda _: on_vmem, outs),
        scratch_shapes=list(scratch),
        cost_estimate=pl.CostEstimate(flops=flops, bytes_accessed=1_000_000, transcendentals=0),
        compiler_params=pltpu.CompilerParams(vmem_limit_bytes=vmem * MIB),
    )


def exchange(x, axes):
    return lax.all_to_all(x, axes, 0, 0, tiled=True)


def on_device(
    column_state,
    cotangent,
    land_mask,
    orography,
    member_seeds,
    land_table,
    relief_table,
    seed_table,
    w_hidden,
    b_hidden,
    w_tendency,
):
    members, channels, band, lon_cols = column_state.shape
    hidden_units, in_channels = w_hidden.shape
    classes = relief_table.shape[0]
    sectors = lax.axis_size("lon")
    peers = lax.axis_size(PLACE)
    lat_total = band * (peers // sectors)
    lon_total = lon_cols * sectors
    taken = band * members // sectors
    groups = band // taken
    rows = taken * channels
    shape = jax.ShapeDtypeStruct

    with jax.named_scope("rows_in"):
        flat = (members, channels * band, lon_cols)
        packed = call(
            by_row_kernel,
            shape((sectors, 2 * rows + 8, lon_cols), F32),
            4,
            scratch=[
                pltpu.VMEM(flat, F32),
                pltpu.VMEM(flat, F32),
                pltpu.VMEM(land_mask.shape, land_mask.dtype),
                pltpu.VMEM(orography.shape, orography.dtype),
                pltpu.SemaphoreType.DMA((4,)),
            ],
            vmem=56,
            inputs_in=pltpu.HBM,
            classes=classes,
        )(column_state.reshape(flat), cotangent.reshape(flat), land_mask, orography)
        row = exchange(packed, "lon")

    with jax.named_scope("row_halo"):
        south_going = []
        for i in range(peers):
            j = i + 1 if i % groups < groups - 1 else i + sectors - (groups - 1)
            if j < peers:
                south_going.append((i, j))
        north_going = [(j, i) for i, j in south_going]
        north = lax.ppermute(row[:, rows - channels : rows].astype(BF), PLACE, south_going)
        south = lax.ppermute(row[:, :channels].astype(BF), PLACE, north_going)

    place = lax.axis_index(PLACE).reshape(1)
    high, low, scale = [jnp.asarray(t) for t in filter_tables(lat_total, lon_total)]
    per_hidden = shape((taken, hidden_units, lon_total), F32)
    features_shape = (taken, in_channels, lon_total)
    with jax.named_scope("early"):
        moist_grad, features, preact, hidden_grad = call(
            early_kernel,
            (shape((rows, lon_total), F32), shape(features_shape, BF), per_hidden, per_hidden),
            12,
            smem=2,
            flops=3_000_000_000,
            vmem=24,
            band=band,
        )(
            place,
            member_seeds,
            row,
            scale,
            high,
            low,
            land_table,
            relief_table,
            seed_table,
            w_hidden,
            b_hidden.reshape(1, hidden_units),
            w_tendency,
        )

    near = lax.axis_size(NEAR)
    length = lax.axis_size("z")
    filled = (hidden_units * in_channels + channels * hidden_units) // (LANES * near)
    share_rows = whole_multiple(filled + BIAS_ROWS, 16)
    piece_rows = share_rows // sectors
    with jax.named_scope("weights"):
        block = (sectors, rows, LANES)
        edge = (sectors, channels, LANES)
        to_north, to_south, moist, grad_rows, weights = call(
            weights_kernel,
            (
                shape(edge, BF),
                shape(edge, BF),
                shape((rows, lon_total), F32),
                shape(block, F32),
                shape((near, share_rows, LANES), BF),
            ),
            9,
            scratch=[
                pltpu.VMEM(features_shape, BF),
                pltpu.VMEM((near, share_rows, LANES), F32),
            ],
            flops=3_000_000_000,
            vmem=28,
        )(north, south, row, moist_grad, features, preact, hidden_grad, w_hidden, w_tendency)
        from_south = lax.ppermute(to_north, PLACE, north_going)
        from_north = lax.ppermute(to_south, PLACE, south_going)

    with jax.named_scope("weights_near"):
        parts = exchange(weights, NEAR)
        share = call(
            near_sum_kernel,
            shape((sectors, piece_rows, LANES), F32),
            2,
            scratch=[pltpu.VMEM((share_rows, LANES), F32)],
        )(parts, from_south)

    with jax.named_scope("weights_middle"):
        copies = call(sum_and_copy_kernel, shape((length, piece_rows, LANES), BF), 2)(
            exchange(share, "lon"), from_north
        )

    with jax.named_scope("fields"):
        fields = call(
            fields_kernel,
            shape((sectors, 2 * rows, LANES), BF),
            8,
            smem=1,
            flops=1_000_000_000,
            band=band,
        )(place, moist, scale, high, low, grad_rows, from_south, from_north)

    with jax.named_scope("weights_length"):
        half_rows = whole_multiple(piece_rows, 16)
        outgoing = call(
            join_kernel,
            shape((sectors, 2 * rows + half_rows, LANES), BF),
            2,
            scratch=[pltpu.VMEM((half_rows, LANES), F32)],
        )(exchange(copies, "z"), fields)

    with jax.named_scope("rows_out"):
        blocks = exchange(outgoing, "lon")

        def by_band(values):
            values = values.reshape(members, groups, taken, channels, lon_cols).astype(F32)
            values = jnp.transpose(values, (0, 3, 1, 2, 4))
            return values.reshape(members, channels, band, lon_cols)

        next_state = by_band(blocks[:, :rows])
        state_grad = by_band(blocks[:, rows : 2 * rows])

    with jax.named_scope("weights_back"):
        spread = call(
            spread_kernel,
            shape((near, share_rows, LANES), BF),
            1,
            scratch=[pltpu.VMEM((share_rows, LANES), F32)],
            start=2 * rows,
        )(blocks)
        shares = exchange(spread, NEAR)
        columns = members * lax.axis_size("mem") * lat_total * lon_total
        grad_in, grad_bias, grad_out = call(
            unpack_kernel,
            (
                shape((hidden_units, in_channels), F32),
                shape((hidden_units,), F32),
                shape((channels, hidden_units), F32),
            ),
            1,
            scratch=[pltpu.VMEM((near, share_rows, LANES), F32)],
            scaling=1.0 / math.sqrt(columns),
        )(shares)
    return next_state, state_grad, grad_in, grad_bias, grad_out


def solution(mesh):
    lat, lon, mem = mesh.devices.shape
    devices = mesh.devices.reshape(2, lat // 4, 2, lon, mem)
    split = Mesh(devices, ("ylo", "z", "core", "lon", "mem"))
    lat_axes = ("ylo", "z", "core")
    field = P("mem", None, lat_axes, "lon")
    surface = P(lat_axes, "lon")
    whole = P()
    return jax.shard_map(
        on_device,
        mesh=split,
        in_specs=(field, field, surface, surface, P("mem")) + (whole,) * 6,
        out_specs=(field, field, whole, whole, whole),
        check_vma=False,
    )
```

```python
import math

import jax
import jax.numpy as jnp
import numpy as np
from jax import lax
from jax.experimental import pallas as pl
from jax.experimental.pallas import tpu as pltpu
from jax.sharding import Mesh, PartitionSpec as P

MODES = 171
DAMP = 2.0
LANES = 128
BF = jnp.bfloat16
F32 = jnp.float32
MIB = 1024 * 1024
PLACE = ("ylo", "z", "core", "lon")
NEAR = ("core", "mem", "ylo")
BIAS_ROWS = 8


def whole_multiple(value, unit):
    return -(-value // unit) * unit


def filter_tables(lat_total, lon_total):
    padded = whole_multiple(2 * MODES, LANES)
    k = np.arange(MODES)
    angles = (k[:, None] * np.arange(lon_total)[None]) % lon_total * (2.0 * math.pi / lon_total)
    analysis = np.zeros((padded, lon_total))
    analysis[: 2 * MODES] = np.concatenate([np.cos(angles), np.sin(angles)], 0)
    lat = math.pi * ((np.arange(lat_total) + 0.5) / lat_total - 0.5)
    removal = 1.0 - np.exp(-DAMP * (k[None] / MODES) ** 2 / np.cos(lat)[:, None] ** 2)
    removal = removal * np.where(k == 0, 1.0, 2.0) / lon_total
    scale = np.zeros((lat_total, padded), np.float32)
    scale[:, : 2 * MODES] = np.concatenate([removal, removal], 1)
    high = analysis.astype(np.float32).astype(BF)
    low = (analysis - high.astype(np.float64)).astype(np.float32).astype(BF)
    return high, low, scale


def dot(a, b, dims=((1,), (0,))):
    return lax.dot_general(a, b, (dims, ((), ())), preferred_element_type=F32)


def split_dot(x, high, low, dims=((1,), (0,))):
    x_high = x.astype(BF)
    x_low = (x - x_high.astype(F32)).astype(BF)
    return dot(x_high, high, dims) + (dot(x_low, high, dims) + dot(x_high, low, dims))


def filtered(x, scale, high, low):
    coeffs = split_dot(x, high, low, ((1,), (1,))) * scale
    return x - split_dot(coeffs, high, low)


def joined(ref, start, rows):
    return jnp.concatenate([ref[s, start : start + rows, :] for s in range(ref.shape[0])], axis=1)


def store_split(ref, start, value):
    for s in range(ref.shape[0]):
        ref[s, start : start + value.shape[0], :] = value[:, s * LANES : (s + 1) * LANES].astype(
            ref.dtype
        )


def position(place, sectors):
    band, q = place // sectors, place % sectors
    return band, q, (q + band) % 2


def by_row_kernel(
    place_ref, state_hbm, cotangent_hbm, land_hbm, orography_hbm, out_hbm,
    state_ref, cotangent_ref, land_ref, orography_ref, out_ref, sems, *, classes
):
    sources = (state_hbm, cotangent_hbm, land_hbm, orography_hbm)
    targets = (state_ref, cotangent_ref, land_ref, orography_ref)
    moves = [
        pltpu.make_async_copy(source, target, sems.at[i])
        for i, (source, target) in enumerate(zip(sources, targets))
    ]
    for move in moves:
        move.start()
    sectors, packed_rows = out_ref.shape[:2]
    rows = (packed_rows - 8) // 2
    members = state_ref.shape[0]
    band = land_ref.shape[0]
    taken = band * members // sectors
    channels = rows // taken
    odd = place_ref[0] // sectors % 2
    leaving = []
    for i in range(2):
        moves[i].wait()
        if i == 1:
            moves[2].wait()
            moves[3].wait()
            code = (jnp.where(land_ref[...] == 1, classes, 0) + orography_ref[...]).astype(F32)
        for m in range(members):
            for pair in range(2):
                q = 2 * m + (pair + odd) % 2
                first = pair * taken
                for k in range(taken):
                    start = i * rows + k * channels
                    out_ref[q, start : start + channels, :] = targets[i][
                        m, pl.ds(first + k, channels, stride=band), :
                    ]
                if i == 1:
                    spare = jnp.zeros((8 - taken, LANES), F32)
                    out_ref[q, 2 * rows :, :] = jnp.concatenate(
                        [code[first : first + taken], spare], axis=0
                    )
        part = pl.ds(i * rows, rows if i == 0 else rows + 8)
        leaving.append(
            pltpu.make_async_copy(out_ref.at[:, part], out_hbm.at[:, part], sems.at[4 + i])
        )
        leaving[i].start()
    for move in leaving:
        move.wait()


def own_scale(place, scale_ref, taken, sectors, rows):
    band, _, pair = position(place, sectors)
    first = (2 * band + pair) * taken
    channels = rows // taken
    wide = (channels, scale_ref.shape[1])
    return jnp.concatenate(
        [jnp.broadcast_to(scale_ref[pl.ds(first + k, 1), :], wide) for k in range(taken)], axis=0
    )


def rolled(value, shift):
    return pltpu.roll(value, shift % value.shape[1], 1) if shift else value


def early_kernel(
    place_ref,
    seeds_ref,
    row_ref,
    scale_ref,
    high_ref,
    low_ref,
    land_ref,
    relief_ref,
    seed_ref,
    w_hidden_ref,
    b_hidden_ref,
    w_tendency_ref,
    moist_grad_ref,
    features_ref,
    preact_ref,
    hidden_grad_ref,
):
    taken = features_ref.shape[0]
    sectors = row_ref.shape[0]
    channels, hidden_units = w_tendency_ref.shape
    rows = taken * channels
    lon_total = features_ref.shape[2]
    classes = relief_ref.shape[0]
    place = place_ref[0]
    scale = own_scale(place, scale_ref, taken, sectors, rows)
    moist_grad = filtered(joined(row_ref, rows, rows), scale, high_ref[...], low_ref[...])
    moist_grad_ref[...] = moist_grad
    rounded = joined(row_ref, 0, rows).astype(BF).astype(F32)
    for j in range(-1, taken + 1):
        for b in range(3):
            if 0 <= j < taken:
                moved = rolled(rounded[j * channels : (j + 1) * channels], 1 - b).astype(BF)
            else:
                moved = jnp.zeros((channels, lon_total), BF)
            for a in range(3):
                if 0 <= j + 1 - a < taken:
                    start = (3 * a + b) * channels
                    features_ref[j + 1 - a, start : start + channels, :] = moved
    class_ids = lax.broadcasted_iota(jnp.int32, (2 * classes, lon_total), 0).astype(F32)
    codes = joined(row_ref, 2 * rows, 8)
    surface = jnp.concatenate(
        [land_ref[0:1, :] + relief_ref[...], land_ref[1:2, :] + relief_ref[...]], axis=0
    )
    seed = seeds_ref[place % sectors // 2]
    table = (surface + seed_ref[pl.ds(seed, 1), :]).astype(BF)
    bias = jnp.transpose(jnp.broadcast_to(b_hidden_ref[...], (8, hidden_units)))[:, 0:1]
    for k in range(taken):
        pick = jnp.where(class_ids == codes[k : k + 1], 1.0, 0.0).astype(BF)
        features_ref[k, 9 * channels :, :] = dot(table, pick, ((0,), (0,))).astype(BF)
        preact_ref[k] = dot(w_hidden_ref[...], features_ref[k]) + bias
        tendency_grad = moist_grad[k * channels : (k + 1) * channels].astype(BF)
        hidden_grad_ref[k] = dot(w_tendency_ref[...], tendency_grad, ((0,), (0,)))


def weights_kernel(
    place_ref,
    across_ref,
    inside_ref,
    row_ref,
    moist_grad_ref,
    early_ref,
    preact_ref,
    hidden_grad_ref,
    w_hidden_ref,
    w_tendency_ref,
    to_across_ref,
    to_inside_ref,
    moist_ref,
    grad_ref,
    weights_ref,
    features_ref,
    stage_ref,
):
    taken, in_channels, lon_total = features_ref.shape
    channels, hidden_units = w_tendency_ref.shape
    group = 3 * channels
    w_stencil = w_hidden_ref[:, : 3 * group]
    state = joined(row_ref, 0, taken * channels)
    grad_in = jnp.zeros((hidden_units, in_channels), F32)
    grad_out = jnp.zeros((channels, hidden_units), F32)
    grad_bias = jnp.zeros((16, hidden_units), F32)
    ones = jnp.ones((16, lon_total), BF)
    northern = position(place_ref[0], row_ref.shape[0])[2] == 0
    across = joined(across_ref, 0, channels).astype(F32)
    inside = joined(inside_ref, 0, channels).astype(F32)
    edges = (
        (jnp.where(northern, across, inside), 0, 0),
        (jnp.where(northern, inside, across), 2, taken - 1),
    )
    sums = []
    for k in range(taken):
        part = slice(k * channels, (k + 1) * channels)
        features_ref[k] = early_ref[k]
        preact = preact_ref[k]
        for edge, a, row in edges:
            if row == k:
                halo = jnp.concatenate([rolled(edge, 1 - b).astype(BF) for b in range(3)], axis=0)
                features_ref[k, a * group : (a + 1) * group, :] = halo
                preact = preact + dot(w_hidden_ref[:, a * group : (a + 1) * group], halo)
        logistic = 0.5 + 0.5 * jnp.tanh(0.5 * preact)
        hidden = (preact * logistic).astype(BF)
        slope = logistic * (1.0 + preact * (1.0 - logistic))
        preact_grad = (hidden_grad_ref[k] * slope).astype(BF)
        tendency_grad = moist_grad_ref[part, :].astype(BF)
        grad_out += dot(tendency_grad, hidden, ((1,), (1,)))
        grad_in += dot(preact_grad, features_ref[k], ((1,), (1,)))
        grad_bias += dot(ones, preact_grad, ((1,), (1,)))
        moist_ref[part, :] = state[part] + dot(w_tendency_ref[...], hidden)
        stencil_grad = dot(w_stencil, preact_grad, ((0,), (0,)))
        sums.append([])
        for a in range(3):
            total = None
            for b in range(3):
                start = (3 * a + b) * channels
                piece = rolled(stencil_grad[start : start + channels], b - 1)
                total = piece if total is None else total + piece
            sums[k].append(total)
    to_north, to_south = sums[0][0], sums[-1][2]
    store_split(to_across_ref, 0, jnp.where(northern, to_north, to_south))
    store_split(to_inside_ref, 0, jnp.where(northern, to_south, to_north))
    for k in range(taken):
        total = moist_grad_ref[k * channels : (k + 1) * channels, :] + sums[k][1]
        if k > 0:
            total = total + sums[k - 1][2]
        if k + 1 < taken:
            total = total + sums[k + 1][0]
        store_split(grad_ref, k * channels, total)

    bias_high = grad_bias[0:1].astype(BF).astype(F32)
    bias_low = grad_bias[0:1] - bias_high
    tiles = hidden_units // LANES
    shares, share_rows = weights_ref.shape[:2]
    filled = (grad_in.size + grad_out.size) // (LANES * shares)
    for p in range(shares):
        stage_ref[p, filled // 8 * 8 :, :] = jnp.zeros((share_rows - filled // 8 * 8, LANES), F32)
        start = 0
        for value in (grad_in, grad_out):
            count = value.shape[0] // shares
            for t in range(value.shape[1] // LANES):
                stage_ref[p, start : start + count, :] = value[
                    p * count : (p + 1) * count, t * LANES : (t + 1) * LANES
                ]
                start += count
        if p == 0:
            for half in (bias_high, bias_low):
                for t in range(tiles):
                    stage_ref[p, start : start + 1, :] = half[:, t * LANES : (t + 1) * LANES]
                    start += 1
        weights_ref[p] = stage_ref[p].astype(BF)


def fields_kernel(
    place_ref, moist_ref, scale_ref, high_ref, low_ref, grad_ref, across_ref, inside_ref, out_ref
):
    sectors, rows = grad_ref.shape[:2]
    channels = across_ref.shape[1]
    place = place_ref[0]
    northern = position(place, sectors)[2] == 0
    scale = own_scale(place, scale_ref, rows // channels, sectors, rows)
    store_split(out_ref, 0, filtered(moist_ref[...], scale, high_ref[...], low_ref[...]))
    for s in range(sectors):
        part = grad_ref[s]
        across, inside = across_ref[s].astype(F32), inside_ref[s].astype(F32)
        first = part[:channels] + jnp.where(northern, across, inside)
        last = part[rows - channels :] + jnp.where(northern, inside, across)
        inner = [part[channels : rows - channels]] if rows > 2 * channels else []
        out_ref[s, rows:, :] = jnp.concatenate([first] + inner + [last], axis=0).astype(BF)


def summed(ref):
    total = ref[0].astype(F32)
    for p in range(1, ref.shape[0]):
        total = total + ref[p].astype(F32)
    return total


def near_sum_kernel(parts_ref, *refs):
    pieces_ref, sum_ref = refs[-2:]
    sum_ref[...] = summed(parts_ref)
    pieces, piece_rows = pieces_ref.shape[:2]
    for p in range(pieces):
        pieces_ref[p] = sum_ref[p * piece_rows : (p + 1) * piece_rows, :]


def join_kernel(parts_ref, fields_ref, out_ref, stage_ref):
    rows, piece_rows = fields_ref.shape[1], parts_ref.shape[1]
    stage_ref[...] = jnp.zeros(stage_ref.shape, F32)
    stage_ref[:piece_rows, :] = summed(parts_ref)
    for s in range(out_ref.shape[0]):
        out_ref[s, :rows, :] = fields_ref[s]
        out_ref[s, rows:, :] = stage_ref[...].astype(BF)


def spread_kernel(blocks_ref, shares_ref, sum_ref, *, start):
    pieces = blocks_ref.shape[0]
    piece_rows = shares_ref.shape[1] // pieces
    for p in range(pieces):
        piece = blocks_ref[p, start:, :].astype(F32)
        sum_ref[p * piece_rows : (p + 1) * piece_rows, :] = piece[:piece_rows]
    share = sum_ref[...].astype(BF)
    for p in range(shares_ref.shape[0]):
        shares_ref[p] = share


def unpack_kernel(shares_ref, grad_in_ref, grad_bias_ref, grad_out_ref, stage_ref, *, scaling):
    shares = shares_ref.shape[0]
    for p in range(shares):
        stage_ref[p] = shares_ref[p].astype(F32) * scaling
        start = 0
        for ref in (grad_in_ref, grad_out_ref):
            count = ref.shape[0] // shares
            for t in range(ref.shape[1] // LANES):
                ref[p * count : (p + 1) * count, t * LANES : (t + 1) * LANES] = stage_ref[
                    p, start : start + count, :
                ]
                start += count
        if p == 0:
            tiles = grad_bias_ref.shape[0] // LANES
            for t in range(tiles):
                both = stage_ref[p, start + t, :] + stage_ref[p, start + tiles + t, :]
                grad_bias_ref[t * LANES : (t + 1) * LANES] = both


def call(kernel, outs, inputs, smem=0, scratch=(), flops=0, vmem=8, inputs_in=pltpu.VMEM, outs_in=pltpu.VMEM, **static):
    on_output = pl.BlockSpec(memory_space=outs_in)
    on_input = pl.BlockSpec(memory_space=inputs_in)
    on_smem = pl.BlockSpec(memory_space=pltpu.SMEM)

    def body(*refs):
        kernel(*refs, **static)

    return pl.pallas_call(
        body,
        out_shape=outs,
        in_specs=[on_smem] * smem + [on_input] * (inputs - smem),
        out_specs=jax.tree.map(lambda _: on_output, outs),
        scratch_shapes=list(scratch),
        cost_estimate=pl.CostEstimate(flops=flops, bytes_accessed=1_000_000, transcendentals=0),
        compiler_params=pltpu.CompilerParams(vmem_limit_bytes=vmem * MIB),
    )


def exchange(x, axes):
    return lax.all_to_all(x, axes, 0, 0, tiled=True)


def on_device(
    column_state,
    cotangent,
    land_mask,
    orography,
    member_seeds,
    land_table,
    relief_table,
    seed_table,
    w_hidden,
    b_hidden,
    w_tendency,
):
    members, channels, band, lon_cols = column_state.shape
    hidden_units, in_channels = w_hidden.shape
    classes = relief_table.shape[0]
    sectors = lax.axis_size("lon")
    peers = lax.axis_size(PLACE)
    lat_total = band * (peers // sectors)
    lon_total = lon_cols * sectors
    taken = band * members // sectors
    rows = taken * channels
    assert 2 * taken == band and 2 * members == sectors
    shape = jax.ShapeDtypeStruct
    place = lax.axis_index(PLACE)
    band_index, _, pair = position(place, sectors)
    place = place.reshape(1)

    with jax.named_scope("rows_in"):
        flat = (members, channels * band, lon_cols)
        packed_shape = (sectors, 2 * rows + 8, lon_cols)
        packed = call(
            by_row_kernel,
            shape(packed_shape, F32),
            5,
            smem=1,
            scratch=[
                pltpu.VMEM(flat, F32),
                pltpu.VMEM(flat, F32),
                pltpu.VMEM(land_mask.shape, land_mask.dtype),
                pltpu.VMEM(orography.shape, orography.dtype),
                pltpu.VMEM(packed_shape, F32),
                pltpu.SemaphoreType.DMA((6,)),
            ],
            vmem=56,
            inputs_in=pltpu.HBM,
            outs_in=pltpu.HBM,
            classes=classes,
        )(place, column_state.reshape(flat), cotangent.reshape(flat), land_mask, orography)
        row = exchange(packed, "lon")

    with jax.named_scope("row_halo"):
        inside_swaps, across_swaps = [], []
        for i in range(peers):
            _, q, southern = position(i, sectors)
            inside_swaps.append((i, i - q + (q ^ 1)))
            j = i + sectors if southern else i - sectors
            if 0 <= j < peers:
                across_swaps.append((i, j))

        def edge_row(southern):
            start = southern * (rows - channels)
            return lax.dynamic_slice_in_dim(row, start, channels, 1).astype(BF)

        inside = lax.ppermute(edge_row(1 - pair), PLACE, inside_swaps)
        across = lax.ppermute(edge_row(pair), PLACE, across_swaps)

    high, low, scale = [jnp.asarray(t) for t in filter_tables(lat_total, lon_total)]
    per_hidden = shape((taken, hidden_units, lon_total), F32)
    features_shape = (taken, in_channels, lon_total)
    with jax.named_scope("early"):
        moist_grad, features, preact, hidden_grad = call(
            early_kernel,
            (shape((rows, lon_total), F32), shape(features_shape, BF), per_hidden, per_hidden),
            12,
            smem=2,
            flops=3_000_000_000,
            vmem=24,
        )(
            place,
            member_seeds,
            row,
            scale,
            high,
            low,
            land_table,
            relief_table,
            seed_table,
            w_hidden,
            b_hidden.reshape(1, hidden_units),
            w_tendency,
        )

    near = lax.axis_size(NEAR)
    length = lax.axis_size("z")
    filled = (hidden_units * in_channels + channels * hidden_units) // (LANES * near)
    share_rows = whole_multiple(filled + BIAS_ROWS, 16)
    piece_rows = share_rows // sectors
    with jax.named_scope("weights"):
        block = (sectors, rows, LANES)
        edge = (sectors, channels, LANES)
        to_across, to_inside, moist, grad_rows, weights = call(
            weights_kernel,
            (
                shape(edge, BF),
                shape(edge, BF),
                shape((rows, lon_total), F32),
                shape(block, F32),
                shape((near, share_rows, LANES), BF),
            ),
            10,
            smem=1,
            scratch=[
                pltpu.VMEM(features_shape, BF),
                pltpu.VMEM((near, share_rows, LANES), F32),
            ],
            flops=3_000_000_000,
            vmem=28,
        )(
            place,
            across,
            inside,
            row,
            moist_grad,
            features,
            preact,
            hidden_grad,
            w_hidden,
            w_tendency,
        )

    with jax.named_scope("fields"):
        from_across = lax.ppermute(to_across, PLACE, across_swaps)
        from_inside = lax.ppermute(to_inside, PLACE, inside_swaps)
        fields = call(
            fields_kernel,
            shape((sectors, 2 * rows, LANES), BF),
            8,
            smem=1,
            flops=1_000_000_000,
        )(place, moist, scale, high, low, grad_rows, from_across, from_inside)

    with jax.named_scope("weights_near"):
        parts = exchange(weights, NEAR)
        share = call(
            near_sum_kernel,
            shape((sectors, piece_rows, LANES), F32),
            2,
            scratch=[pltpu.VMEM((share_rows, LANES), F32)],
        )(parts, fields)

    with jax.named_scope("weights_middle"):
        piece = jnp.sum(exchange(share, "lon"), 0, keepdims=True).astype(BF)
        copies = jnp.broadcast_to(piece, (length, piece_rows, LANES))

    with jax.named_scope("weights_length"):
        half_rows = whole_multiple(piece_rows, 16)
        outgoing = call(
            join_kernel,
            shape((sectors, 2 * rows + half_rows, LANES), BF),
            2,
            scratch=[pltpu.VMEM((half_rows, LANES), F32)],
        )(exchange(copies, "z"), fields)

    with jax.named_scope("rows_out"):
        blocks = exchange(outgoing, "lon")

        def by_band(values):
            values = values.reshape(members, 2, taken, channels, lon_cols).astype(F32)
            values = jnp.where(band_index % 2 == 1, values[:, ::-1], values)
            values = jnp.transpose(values, (0, 3, 1, 2, 4))
            return values.reshape(members, channels, band, lon_cols)

        next_state = by_band(blocks[:, :rows])
        state_grad = by_band(blocks[:, rows : 2 * rows])

    with jax.named_scope("weights_back"):
        spread = call(
            spread_kernel,
            shape((near, share_rows, LANES), BF),
            1,
            scratch=[pltpu.VMEM((share_rows, LANES), F32)],
            start=2 * rows,
        )(blocks)
        shares = exchange(spread, NEAR)
        columns = members * lax.axis_size("mem") * lat_total * lon_total
        grad_in, grad_bias, grad_out = call(
            unpack_kernel,
            (
                shape((hidden_units, in_channels), F32),
                shape((hidden_units,), F32),
                shape((channels, hidden_units), F32),
            ),
            1,
            scratch=[pltpu.VMEM((near, share_rows, LANES), F32)],
            scaling=1.0 / math.sqrt(columns),
        )(shares)
    return next_state, state_grad, grad_in, grad_bias, grad_out


def solution(mesh):
    lat, lon, mem = mesh.devices.shape
    devices = mesh.devices.reshape(2, lat // 4, 2, lon, mem)
    split = Mesh(devices, ("ylo", "z", "core", "lon", "mem"))
    lat_axes = ("ylo", "z", "core")
    field = P("mem", None, lat_axes, "lon")
    surface = P(lat_axes, "lon")
    whole = P()
    return jax.shard_map(
        on_device,
        mesh=split,
        in_specs=(field, field, surface, surface, P("mem")) + (whole,) * 6,
        out_specs=(field, field, whole, whole, whole),
        check_vma=False,
    )
```

```python
import math

import jax
import jax.numpy as jnp
import numpy as np
from jax import lax
from jax.experimental import pallas as pl
from jax.experimental.pallas import tpu as pltpu
from jax.sharding import Mesh, PartitionSpec as P

MODES = 171
DAMP = 2.0
LANES = 128
BF = jnp.bfloat16
F32 = jnp.float32
MIB = 1024 * 1024
PLACE = ("ylo", "z", "core", "lon")
PLANE = ("mem", "ylo", "lon")


def whole_multiple(value, unit):
    return -(-value // unit) * unit


def filter_tables(lat_total, lon_total):
    padded = whole_multiple(2 * MODES, LANES)
    k = np.arange(MODES)
    angles = (k[:, None] * np.arange(lon_total)[None]) % lon_total * (2.0 * math.pi / lon_total)
    analysis = np.zeros((padded, lon_total))
    analysis[: 2 * MODES] = np.concatenate([np.cos(angles), np.sin(angles)], 0)
    lat = math.pi * ((np.arange(lat_total) + 0.5) / lat_total - 0.5)
    removal = 1.0 - np.exp(-DAMP * (k[None] / MODES) ** 2 / np.cos(lat)[:, None] ** 2)
    removal = removal * np.where(k == 0, 1.0, 2.0) / lon_total
    scale = np.zeros((lat_total, padded), np.float32)
    scale[:, : 2 * MODES] = np.concatenate([removal, removal], 1)
    high = analysis.astype(np.float32).astype(BF)
    low = (analysis - high.astype(np.float64)).astype(np.float32).astype(BF)
    return high, low, scale


def split_rows(total, pieces):
    each = total // pieces
    return each // 8 * 8, each % 8


def dot(a, b, dims=((1,), (0,))):
    return lax.dot_general(a, b, (dims, ((), ())), preferred_element_type=F32)


def split_dot(x, high, low, dims=((1,), (0,))):
    x_high = x.astype(BF)
    x_low = (x - x_high.astype(F32)).astype(BF)
    return dot(x_high, high, dims) + (dot(x_low, high, dims) + dot(x_high, low, dims))


def filtered(x, scale, high, low):
    coeffs = split_dot(x, high, low, ((1,), (1,))) * scale
    return x - split_dot(coeffs, high, low)


def joined(ref, start, rows):
    return jnp.concatenate([ref[s, start : start + rows, :] for s in range(ref.shape[0])], axis=1)


def store_split(ref, start, value):
    for s in range(ref.shape[0]):
        ref[s, start : start + value.shape[0], :] = value[:, s * LANES : (s + 1) * LANES].astype(
            ref.dtype
        )


def position(place, sectors):
    band, q = place // sectors, place % sectors
    return band, q, (q + band) % 2


def by_row_kernel(
    place_ref, state_hbm, cotangent_hbm, land_hbm, orography_hbm, out_hbm,
    state_ref, cotangent_ref, land_ref, orography_ref, out_ref, sems, *, classes
):
    sources = (state_hbm, cotangent_hbm, land_hbm, orography_hbm)
    targets = (state_ref, cotangent_ref, land_ref, orography_ref)
    moves = [
        pltpu.make_async_copy(source, target, sems.at[i])
        for i, (source, target) in enumerate(zip(sources, targets))
    ]
    for move in moves:
        move.start()
    sectors, packed_rows = out_ref.shape[:2]
    rows = (packed_rows - 8) // 2
    members = state_ref.shape[0]
    band = land_ref.shape[0]
    taken = band * members // sectors
    channels = rows // taken
    odd = place_ref[0] // sectors % 2
    leaving = []
    for i in range(2):
        moves[i].wait()
        if i == 1:
            moves[2].wait()
            moves[3].wait()
            code = (jnp.where(land_ref[...] == 1, classes, 0) + orography_ref[...]).astype(F32)
        for m in range(members):
            for pair in range(2):
                q = 2 * m + (pair + odd) % 2
                first = pair * taken
                for k in range(taken):
                    start = i * rows + k * channels
                    out_ref[q, start : start + channels, :] = targets[i][
                        m, pl.ds(first + k, channels, stride=band), :
                    ]
                if i == 1:
                    spare = jnp.zeros((8 - taken, LANES), F32)
                    out_ref[q, 2 * rows :, :] = jnp.concatenate(
                        [code[first : first + taken], spare], axis=0
                    )
        part = pl.ds(i * rows, rows if i == 0 else rows + 8)
        leaving.append(
            pltpu.make_async_copy(out_ref.at[:, part], out_hbm.at[:, part], sems.at[4 + i])
        )
        leaving[i].start()
    for move in leaving:
        move.wait()


def own_scale(place, scale_ref, taken, sectors, rows):
    band, _, pair = position(place, sectors)
    first = (2 * band + pair) * taken
    channels = rows // taken
    wide = (channels, scale_ref.shape[1])
    return jnp.concatenate(
        [jnp.broadcast_to(scale_ref[pl.ds(first + k, 1), :], wide) for k in range(taken)], axis=0
    )


def rolled(value, shift):
    return pltpu.roll(value, shift % value.shape[1], 1) if shift else value


def early_kernel(
    place_ref,
    seeds_ref,
    row_ref,
    scale_ref,
    high_ref,
    low_ref,
    land_ref,
    relief_ref,
    seed_ref,
    w_hidden_ref,
    b_hidden_ref,
    w_tendency_ref,
    moist_grad_ref,
    features_ref,
    preact_ref,
    hidden_grad_ref,
):
    taken = features_ref.shape[0]
    sectors = row_ref.shape[0]
    channels, hidden_units = w_tendency_ref.shape
    rows = taken * channels
    lon_total = features_ref.shape[2]
    classes = relief_ref.shape[0]
    place = place_ref[0]
    scale = own_scale(place, scale_ref, taken, sectors, rows)
    moist_grad = filtered(joined(row_ref, rows, rows), scale, high_ref[...], low_ref[...])
    moist_grad_ref[...] = moist_grad
    rounded = joined(row_ref, 0, rows).astype(BF).astype(F32)
    for j in range(-1, taken + 1):
        for b in range(3):
            if 0 <= j < taken:
                moved = rolled(rounded[j * channels : (j + 1) * channels], 1 - b).astype(BF)
            else:
                moved = jnp.zeros((channels, lon_total), BF)
            for a in range(3):
                if 0 <= j + 1 - a < taken:
                    start = (3 * a + b) * channels
                    features_ref[j + 1 - a, start : start + channels, :] = moved
    class_ids = lax.broadcasted_iota(jnp.int32, (2 * classes, lon_total), 0).astype(F32)
    codes = joined(row_ref, 2 * rows, 8)
    surface = jnp.concatenate(
        [land_ref[0:1, :] + relief_ref[...], land_ref[1:2, :] + relief_ref[...]], axis=0
    )
    seed = seeds_ref[place % sectors // 2]
    table = (surface + seed_ref[pl.ds(seed, 1), :]).astype(BF)
    bias = jnp.transpose(jnp.broadcast_to(b_hidden_ref[...], (8, hidden_units)))[:, 0:1]
    for k in range(taken):
        pick = jnp.where(class_ids == codes[k : k + 1], 1.0, 0.0).astype(BF)
        features_ref[k, 9 * channels :, :] = dot(table, pick, ((0,), (0,))).astype(BF)
        preact_ref[k] = dot(w_hidden_ref[...], features_ref[k]) + bias
        tendency_grad = moist_grad[k * channels : (k + 1) * channels].astype(BF)
        hidden_grad_ref[k] = dot(w_tendency_ref[...], tendency_grad, ((0,), (0,)))


def weights_kernel(
    place_ref,
    across_ref,
    inside_ref,
    row_ref,
    moist_grad_ref,
    early_ref,
    preact_ref,
    hidden_grad_ref,
    w_hidden_ref,
    w_tendency_ref,
    to_across_ref,
    to_inside_ref,
    moist_ref,
    grad_ref,
    own_ref,
    other_ref,
    features_ref,
    flat_ref,
    stage_ref,
):
    taken, in_channels, lon_total = features_ref.shape
    channels, hidden_units = w_tendency_ref.shape
    group = 3 * channels
    w_stencil = w_hidden_ref[:, : 3 * group]
    state = joined(row_ref, 0, taken * channels)
    grad_in = jnp.zeros((hidden_units, in_channels), F32)
    grad_out = jnp.zeros((channels, hidden_units), F32)
    grad_bias = jnp.zeros((16, hidden_units), F32)
    ones = jnp.ones((16, lon_total), BF)
    northern = position(place_ref[0], row_ref.shape[0])[2] == 0
    across = joined(across_ref, 0, channels).astype(F32)
    inside = joined(inside_ref, 0, channels).astype(F32)
    edges = (
        (jnp.where(northern, across, inside), 0, 0),
        (jnp.where(northern, inside, across), 2, taken - 1),
    )
    sums = []
    for k in range(taken):
        part = slice(k * channels, (k + 1) * channels)
        features_ref[k] = early_ref[k]
        preact = preact_ref[k]
        for edge, a, row in edges:
            if row == k:
                halo = jnp.concatenate([rolled(edge, 1 - b).astype(BF) for b in range(3)], axis=0)
                features_ref[k, a * group : (a + 1) * group, :] = halo
                preact = preact + dot(w_hidden_ref[:, a * group : (a + 1) * group], halo)
        logistic = 0.5 + 0.5 * jnp.tanh(0.5 * preact)
        hidden = (preact * logistic).astype(BF)
        slope = logistic * (1.0 + preact * (1.0 - logistic))
        preact_grad = (hidden_grad_ref[k] * slope).astype(BF)
        tendency_grad = moist_grad_ref[part, :].astype(BF)
        grad_out += dot(tendency_grad, hidden, ((1,), (1,)))
        grad_in += dot(preact_grad, features_ref[k], ((1,), (1,)))
        grad_bias += dot(ones, preact_grad, ((1,), (1,)))
        moist_ref[part, :] = state[part] + dot(w_tendency_ref[...], hidden)
        stencil_grad = dot(w_stencil, preact_grad, ((0,), (0,)))
        sums.append([])
        for a in range(3):
            total = None
            for b in range(3):
                start = (3 * a + b) * channels
                piece = rolled(stencil_grad[start : start + channels], b - 1)
                total = piece if total is None else total + piece
            sums[k].append(total)
    to_north, to_south = sums[0][0], sums[-1][2]
    store_split(to_across_ref, 0, jnp.where(northern, to_north, to_south))
    store_split(to_inside_ref, 0, jnp.where(northern, to_south, to_north))
    for k in range(taken):
        total = moist_grad_ref[k * channels : (k + 1) * channels, :] + sums[k][1]
        if k > 0:
            total = total + sums[k - 1][2]
        if k + 1 < taken:
            total = total + sums[k + 1][0]
        store_split(grad_ref, k * channels, total)

    bias_high = grad_bias[0:1].astype(BF).astype(F32)
    bias_low = grad_bias[0:1] - bias_high
    tiles = hidden_units // LANES
    pieces = own_ref.shape[0]
    base, rest = split_rows(flat_ref.shape[1], pieces)
    stage_ref[:, :, base + rest :, :] = jnp.zeros((2, pieces, tiles, LANES), F32)
    for h in range(2):
        start = 0
        for value in (grad_in, grad_out):
            count = value.shape[0] // 2
            for t in range(value.shape[1] // LANES):
                flat_ref[h, start : start + count, :] = value[
                    h * count : (h + 1) * count, t * LANES : (t + 1) * LANES
                ]
                start += count
        for p in range(pieces):
            stage_ref[h, p, :base, :] = flat_ref[h, p * base : (p + 1) * base, :]
            start = pieces * base + p * rest
            stage_ref[h, p, base : base + rest, :] = flat_ref[h, start : start + rest, :]
        for p, half in enumerate((bias_high, bias_low)):
            for t in range(tiles):
                row = base + rest + t
                stage_ref[h, p, row : row + 1, :] = half[:, t * LANES : (t + 1) * LANES]
    core = position(place_ref[0], row_ref.shape[0])[0] % 2
    own_ref[...] = stage_ref[core]
    other_ref[...] = stage_ref[1 - core].astype(BF)


def fields_kernel(
    place_ref, moist_ref, scale_ref, high_ref, low_ref, grad_ref, across_ref, inside_ref, *refs
):
    sends, blocks_ref = refs[:-1], refs[-1]
    sectors, rows = grad_ref.shape[:2]
    channels = across_ref.shape[1]
    place = place_ref[0]
    _, q, pair = position(place, sectors)
    scale = own_scale(place, scale_ref, rows // channels, sectors, rows)
    store_split(blocks_ref, 0, filtered(moist_ref[...], scale, high_ref[...], low_ref[...]))
    for s in range(sectors):
        part = grad_ref[s]
        across, inside = across_ref[s].astype(F32), inside_ref[s].astype(F32)
        first = part[:channels] + jnp.where(pair == 0, across, inside)
        last = part[rows - channels :] + jnp.where(pair == 0, inside, across)
        inner = [part[channels : rows - channels]] if rows > 2 * channels else []
        blocks_ref[s, rows:, :] = jnp.concatenate([first] + inner + [last], axis=0).astype(BF)
    for t in range(sectors):
        sends[t][...] = blocks_ref[q ^ t]


def by_band_kernel(place_ref, *refs, band):
    blocks_ref = refs[-1]
    outs = refs[-3:-1]
    sectors, rows = blocks_ref.shape[0], blocks_ref.shape[1] // 2
    members = outs[0].shape[0]
    taken = band * members // sectors
    channels = rows // taken
    band_index, q, _ = position(place_ref[0], sectors)
    for t in range(sectors):
        blocks_ref[t] = refs[t][...].astype(F32)
    for m in range(members):
        for pair in range(2):
            t = q ^ (2 * m + (pair + band_index) % 2)
            for i in range(2):
                for k in range(taken):
                    start = i * rows + k * channels
                    outs[i][m, pl.ds(pair * taken + k, channels, stride=band), :] = blocks_ref[
                        t, start : start + channels, :
                    ]


def sum_and_copy_kernel(parts_ref, *refs):
    copies_ref = refs[-1]
    total = parts_ref[0].astype(F32)
    for p in range(1, parts_ref.shape[0]):
        total = total + parts_ref[p].astype(F32)
    total = total.astype(BF)
    for p in range(copies_ref.shape[0]):
        copies_ref[p] = total


def unpack_kernel(
    place_ref, own_ref, other_ref, grad_in_ref, grad_bias_ref, grad_out_ref, flat_ref,
    *, scaling, sectors
):
    pieces = own_ref.shape[0]
    base, rest = split_rows(flat_ref.shape[1], pieces)
    core = position(place_ref[0], sectors)[0] % 2
    bias = None
    for ref, h in ((own_ref, core), (other_ref, 1 - core)):
        for p in range(pieces):
            piece = ref[p].astype(F32) * scaling
            flat_ref[h, p * base : (p + 1) * base, :] = piece[:base]
            start = pieces * base + p * rest
            flat_ref[h, start : start + rest, :] = piece[base : base + rest]
            if ref is own_ref and p < 2:
                half = piece[base + rest :]
                bias = half if bias is None else bias + half
    for t in range(grad_bias_ref.shape[0] // LANES):
        grad_bias_ref[t * LANES : (t + 1) * LANES] = bias[t]
    for h in range(2):
        start = 0
        for ref in (grad_in_ref, grad_out_ref):
            count = ref.shape[0] // 2
            for t in range(ref.shape[1] // LANES):
                ref[h * count : (h + 1) * count, t * LANES : (t + 1) * LANES] = flat_ref[
                    h, start : start + count, :
                ]
                start += count


def call(kernel, outs, inputs, smem=0, scratch=(), flops=0, vmem=8, inputs_in=pltpu.VMEM, outs_in=pltpu.VMEM, **static):
    on_output = pl.BlockSpec(memory_space=outs_in)
    on_input = pl.BlockSpec(memory_space=inputs_in)
    on_smem = pl.BlockSpec(memory_space=pltpu.SMEM)

    def body(*refs):
        kernel(*refs, **static)

    return pl.pallas_call(
        body,
        out_shape=outs,
        in_specs=[on_smem] * smem + [on_input] * (inputs - smem),
        out_specs=jax.tree.map(lambda _: on_output, outs),
        scratch_shapes=list(scratch),
        cost_estimate=pl.CostEstimate(flops=flops, bytes_accessed=1_000_000, transcendentals=0),
        compiler_params=pltpu.CompilerParams(vmem_limit_bytes=vmem * MIB),
    )


def exchange(x, axes):
    return lax.all_to_all(x, axes, 0, 0, tiled=True)


def on_device(
    column_state,
    cotangent,
    land_mask,
    orography,
    member_seeds,
    land_table,
    relief_table,
    seed_table,
    w_hidden,
    b_hidden,
    w_tendency,
):
    members, channels, band, lon_cols = column_state.shape
    hidden_units, in_channels = w_hidden.shape
    classes = relief_table.shape[0]
    sectors = lax.axis_size("lon")
    peers = lax.axis_size(PLACE)
    lat_total = band * (peers // sectors)
    lon_total = lon_cols * sectors
    taken = band * members // sectors
    rows = taken * channels
    assert 2 * taken == band and 2 * members == sectors
    shape = jax.ShapeDtypeStruct
    place = lax.axis_index(PLACE)
    band_index, _, pair = position(place, sectors)
    place = place.reshape(1)

    with jax.named_scope("rows_in"):
        flat = (members, channels * band, lon_cols)
        packed_shape = (sectors, 2 * rows + 8, lon_cols)
        packed = call(
            by_row_kernel,
            shape(packed_shape, F32),
            5,
            smem=1,
            scratch=[
                pltpu.VMEM(flat, F32),
                pltpu.VMEM(flat, F32),
                pltpu.VMEM(land_mask.shape, land_mask.dtype),
                pltpu.VMEM(orography.shape, orography.dtype),
                pltpu.VMEM(packed_shape, F32),
                pltpu.SemaphoreType.DMA((6,)),
            ],
            vmem=56,
            inputs_in=pltpu.HBM,
            outs_in=pltpu.HBM,
            classes=classes,
        )(place, column_state.reshape(flat), cotangent.reshape(flat), land_mask, orography)
        row = exchange(packed, "lon")

    with jax.named_scope("row_halo"):
        inside_swaps, across_swaps = [], []
        for i in range(peers):
            _, q, southern = position(i, sectors)
            inside_swaps.append((i, i - q + (q ^ 1)))
            j = i + sectors if southern else i - sectors
            if 0 <= j < peers:
                across_swaps.append((i, j))

        def edge_row(southern):
            start = southern * (rows - channels)
            return lax.dynamic_slice_in_dim(row, start, channels, 1).astype(BF)

        inside = lax.ppermute(edge_row(1 - pair), PLACE, inside_swaps)
        across = lax.ppermute(edge_row(pair), PLACE, across_swaps)

    high, low, scale = [jnp.asarray(t) for t in filter_tables(lat_total, lon_total)]
    per_hidden = shape((taken, hidden_units, lon_total), F32)
    features_shape = (taken, in_channels, lon_total)
    with jax.named_scope("early"):
        moist_grad, features, preact, hidden_grad = call(
            early_kernel,
            (shape((rows, lon_total), F32), shape(features_shape, BF), per_hidden, per_hidden),
            12,
            smem=2,
            flops=3_000_000_000,
            vmem=24,
        )(
            place,
            member_seeds,
            row,
            scale,
            high,
            low,
            land_table,
            relief_table,
            seed_table,
            w_hidden,
            b_hidden.reshape(1, hidden_units),
            w_tendency,
        )

    pieces = lax.axis_size(PLANE)
    length = lax.axis_size("z")
    half_rows = (hidden_units * in_channels + channels * hidden_units) // (2 * LANES)
    piece_rows = half_rows // pieces + hidden_units // LANES
    share = (pieces, piece_rows, LANES)
    flat_rows = pltpu.VMEM((2, half_rows, LANES), F32)
    with jax.named_scope("weights"):
        block = (sectors, rows, LANES)
        edge = (sectors, channels, LANES)
        to_across, to_inside, moist, grad_rows, own, other = call(
            weights_kernel,
            (
                shape(edge, BF),
                shape(edge, BF),
                shape((rows, lon_total), F32),
                shape(block, F32),
                shape(share, F32),
                shape(share, BF),
            ),
            10,
            smem=1,
            scratch=[
                pltpu.VMEM(features_shape, BF),
                flat_rows,
                pltpu.VMEM((2,) + share, F32),
            ],
            flops=3_000_000_000,
            vmem=28,
        )(
            place,
            across,
            inside,
            row,
            moist_grad,
            features,
            preact,
            hidden_grad,
            w_hidden,
            w_tendency,
        )

    with jax.named_scope("weights_core"):
        swap = [(0, 1), (1, 0)]
        halves = (own + lax.ppermute(other, "core", swap).astype(F32)).astype(BF)

    with jax.named_scope("fields"):
        from_across = lax.ppermute(to_across, PLACE, across_swaps)
        from_inside = lax.ppermute(to_inside, PLACE, inside_swaps)
        fields = call(
            fields_kernel,
            (shape((2 * rows, LANES), BF),) * sectors,
            8,
            smem=1,
            scratch=[pltpu.VMEM((sectors, 2 * rows, LANES), BF)],
            flops=1_000_000_000,
        )(place, moist, scale, high, low, grad_rows, from_across, from_inside)

    with jax.named_scope("weights_plane"):
        copies = call(sum_and_copy_kernel, shape((length, piece_rows, LANES), BF), 2)(
            exchange(halves, PLANE), fields[0]
        )

    with jax.named_scope("rows_out"):
        received = [fields[0]]
        for t in range(1, sectors):
            received.append(lax.ppermute(fields[t], "lon", [(i, i ^ t) for i in range(sectors)]))

    with jax.named_scope("weights_length"):
        copies = call(sum_and_copy_kernel, shape(share, BF), sectors)(
            exchange(copies, "z"), *received[1:]
        )

    with jax.named_scope("bands_out"):
        next_state, state_grad = call(
            by_band_kernel,
            (shape(flat, F32), shape(flat, F32)),
            1 + sectors,
            smem=1,
            scratch=[pltpu.VMEM((sectors, 2 * rows, LANES), F32)],
            band=band,
        )(place, *received)
        next_state = next_state.reshape(column_state.shape)
        state_grad = state_grad.reshape(column_state.shape)

    with jax.named_scope("weights_back"):
        own = exchange(copies, PLANE)
        other = lax.ppermute(own, "core", swap)
        columns = members * lax.axis_size("mem") * lat_total * lon_total
        grad_in, grad_bias, grad_out = call(
            unpack_kernel,
            (
                shape((hidden_units, in_channels), F32),
                shape((hidden_units,), F32),
                shape((channels, hidden_units), F32),
            ),
            3,
            smem=1,
            scratch=[flat_rows],
            scaling=1.0 / math.sqrt(columns),
            sectors=sectors,
        )(place, own, other)
    return next_state, state_grad, grad_in, grad_bias, grad_out


def solution(mesh):
    lat, lon, mem = mesh.devices.shape
    devices = mesh.devices.reshape(2, lat // 4, 2, lon, mem)
    split = Mesh(devices, ("ylo", "z", "core", "lon", "mem"))
    lat_axes = ("ylo", "z", "core")
    field = P("mem", None, lat_axes, "lon")
    surface = P(lat_axes, "lon")
    whole = P()
    return jax.shard_map(
        on_device,
        mesh=split,
        in_specs=(field, field, surface, surface, P("mem")) + (whole,) * 6,
        out_specs=(field, field, whole, whole, whole),
        check_vma=False,
    )
```

```python
import math

import jax
import jax.numpy as jnp
import numpy as np
from jax import lax
from jax.experimental import pallas as pl
from jax.experimental.pallas import tpu as pltpu
from jax.sharding import Mesh, PartitionSpec as P

MODES = 171
DAMP = 2.0
LANES = 128
BF = jnp.bfloat16
F32 = jnp.float32
MIB = 1024 * 1024
PLACE = ("ylo", "z", "core", "lon")
PLANE = ("mem", "ylo", "lon")


def whole_multiple(value, unit):
    return -(-value // unit) * unit


def filter_tables(lat_total, lon_total):
    padded = whole_multiple(2 * MODES, LANES)
    k = np.arange(MODES)
    angles = (k[:, None] * np.arange(lon_total)[None]) % lon_total * (2.0 * math.pi / lon_total)
    analysis = np.zeros((padded, lon_total))
    analysis[: 2 * MODES] = np.concatenate([np.cos(angles), np.sin(angles)], 0)
    lat = math.pi * ((np.arange(lat_total) + 0.5) / lat_total - 0.5)
    removal = 1.0 - np.exp(-DAMP * (k[None] / MODES) ** 2 / np.cos(lat)[:, None] ** 2)
    removal = removal * np.where(k == 0, 1.0, 2.0) / lon_total
    scale = np.zeros((lat_total, padded), np.float32)
    scale[:, : 2 * MODES] = np.concatenate([removal, removal], 1)
    high = analysis.astype(np.float32).astype(BF)
    low = (analysis - high.astype(np.float64)).astype(np.float32).astype(BF)
    return high, low, scale


def split_rows(total, pieces):
    each = total // pieces
    return each // 8 * 8, each % 8


def dot(a, b, dims=((1,), (0,))):
    return lax.dot_general(a, b, (dims, ((), ())), preferred_element_type=F32)


def split_dot(x, high, low, dims=((1,), (0,))):
    x_high = x.astype(BF)
    x_low = (x - x_high.astype(F32)).astype(BF)
    return dot(x_high, high, dims) + (dot(x_low, high, dims) + dot(x_high, low, dims))


def filtered(x, scale, high, low):
    coeffs = split_dot(x, high, low, ((1,), (1,))) * scale
    return x - split_dot(coeffs, high, low)


def joined(ref, start, rows):
    return jnp.concatenate([ref[s, start : start + rows, :] for s in range(ref.shape[0])], axis=1)


def store_split(ref, start, value):
    for s in range(ref.shape[0]):
        ref[s, start : start + value.shape[0], :] = value[:, s * LANES : (s + 1) * LANES].astype(
            ref.dtype
        )


def position(place, sectors):
    band, q = place // sectors, place % sectors
    return band, q, (q + band) % 2


def by_row_kernel(
    place_ref, state_hbm, cotangent_hbm, land_hbm, orography_hbm, out_hbm,
    state_ref, cotangent_ref, land_ref, orography_ref, out_ref, sems, *, classes
):
    sources = (state_hbm, cotangent_hbm, land_hbm, orography_hbm)
    targets = (state_ref, cotangent_ref, land_ref, orography_ref)
    moves = [
        pltpu.make_async_copy(source, target, sems.at[i])
        for i, (source, target) in enumerate(zip(sources, targets))
    ]
    for move in moves:
        move.start()
    sectors, packed_rows = out_ref.shape[:2]
    rows = (packed_rows - 8) // 2
    members = state_ref.shape[0]
    band = land_ref.shape[0]
    taken = band * members // sectors
    channels = rows // taken
    odd = place_ref[0] // sectors % 2
    leaving = []
    for i in range(2):
        moves[i].wait()
        if i == 1:
            moves[2].wait()
            moves[3].wait()
            code = (jnp.where(land_ref[...] == 1, classes, 0) + orography_ref[...]).astype(F32)
        for m in range(members):
            for pair in range(2):
                q = 2 * m + (pair + odd) % 2
                first = pair * taken
                for k in range(taken):
                    start = i * rows + k * channels
                    out_ref[q, start : start + channels, :] = targets[i][
                        m, pl.ds(first + k, channels, stride=band), :
                    ]
                if i == 1:
                    spare = jnp.zeros((8 - taken, LANES), F32)
                    out_ref[q, 2 * rows :, :] = jnp.concatenate(
                        [code[first : first + taken], spare], axis=0
                    )
        part = pl.ds(i * rows, rows if i == 0 else rows + 8)
        leaving.append(
            pltpu.make_async_copy(out_ref.at[:, part], out_hbm.at[:, part], sems.at[4 + i])
        )
        leaving[i].start()
    for move in leaving:
        move.wait()


def own_scale(place, scale_ref, taken, sectors, rows):
    band, _, pair = position(place, sectors)
    first = (2 * band + pair) * taken
    channels = rows // taken
    wide = (channels, scale_ref.shape[1])
    return jnp.concatenate(
        [jnp.broadcast_to(scale_ref[pl.ds(first + k, 1), :], wide) for k in range(taken)], axis=0
    )


def rolled(value, shift):
    return pltpu.roll(value, shift % value.shape[1], 1) if shift else value


def early_kernel(
    place_ref,
    seeds_ref,
    row_ref,
    scale_ref,
    high_ref,
    low_ref,
    land_ref,
    relief_ref,
    seed_ref,
    w_hidden_ref,
    b_hidden_ref,
    w_tendency_ref,
    moist_grad_ref,
    features_ref,
    preact_ref,
    hidden_grad_ref,
):
    taken = features_ref.shape[0]
    sectors = row_ref.shape[0]
    channels, hidden_units = w_tendency_ref.shape
    rows = taken * channels
    lon_total = features_ref.shape[2]
    classes = relief_ref.shape[0]
    place = place_ref[0]
    scale = own_scale(place, scale_ref, taken, sectors, rows)
    moist_grad = filtered(joined(row_ref, rows, rows), scale, high_ref[...], low_ref[...])
    moist_grad_ref[...] = moist_grad
    rounded = joined(row_ref, 0, rows).astype(BF).astype(F32)
    for j in range(-1, taken + 1):
        for b in range(3):
            if 0 <= j < taken:
                moved = rolled(rounded[j * channels : (j + 1) * channels], 1 - b).astype(BF)
            else:
                moved = jnp.zeros((channels, lon_total), BF)
            for a in range(3):
                if 0 <= j + 1 - a < taken:
                    start = (3 * a + b) * channels
                    features_ref[j + 1 - a, start : start + channels, :] = moved
    class_ids = lax.broadcasted_iota(jnp.int32, (2 * classes, lon_total), 0).astype(F32)
    codes = joined(row_ref, 2 * rows, 8)
    surface = jnp.concatenate(
        [land_ref[0:1, :] + relief_ref[...], land_ref[1:2, :] + relief_ref[...]], axis=0
    )
    seed = seeds_ref[place % sectors // 2]
    table = (surface + seed_ref[pl.ds(seed, 1), :]).astype(BF)
    bias = jnp.transpose(jnp.broadcast_to(b_hidden_ref[...], (8, hidden_units)))[:, 0:1]
    for k in range(taken):
        pick = jnp.where(class_ids == codes[k : k + 1], 1.0, 0.0).astype(BF)
        features_ref[k, 9 * channels :, :] = dot(table, pick, ((0,), (0,))).astype(BF)
        preact_ref[k] = dot(w_hidden_ref[...], features_ref[k]) + bias
        tendency_grad = moist_grad[k * channels : (k + 1) * channels].astype(BF)
        hidden_grad_ref[k] = dot(w_tendency_ref[...], tendency_grad, ((0,), (0,)))


def weights_kernel(
    place_ref,
    across_ref,
    inside_ref,
    row_ref,
    moist_grad_ref,
    early_ref,
    preact_ref,
    hidden_grad_ref,
    w_hidden_ref,
    w_tendency_ref,
    to_across_ref,
    to_inside_ref,
    moist_ref,
    grad_ref,
    own_ref,
    other_ref,
    features_ref,
    flat_ref,
    stage_ref,
):
    taken, in_channels, lon_total = features_ref.shape
    channels, hidden_units = w_tendency_ref.shape
    group = 3 * channels
    w_stencil = w_hidden_ref[:, : 3 * group]
    state = joined(row_ref, 0, taken * channels)
    grad_in = jnp.zeros((hidden_units, in_channels), F32)
    grad_out = jnp.zeros((channels, hidden_units), F32)
    grad_bias = jnp.zeros((16, hidden_units), F32)
    ones = jnp.ones((16, lon_total), BF)
    northern = position(place_ref[0], row_ref.shape[0])[2] == 0
    across = joined(across_ref, 0, channels).astype(F32)
    inside = joined(inside_ref, 0, channels).astype(F32)
    edges = (
        (jnp.where(northern, across, inside), 0, 0),
        (jnp.where(northern, inside, across), 2, taken - 1),
    )
    sums = []
    for k in range(taken):
        part = slice(k * channels, (k + 1) * channels)
        features_ref[k] = early_ref[k]
        preact = preact_ref[k]
        for edge, a, row in edges:
            if row == k:
                halo = jnp.concatenate([rolled(edge, 1 - b).astype(BF) for b in range(3)], axis=0)
                features_ref[k, a * group : (a + 1) * group, :] = halo
                preact = preact + dot(w_hidden_ref[:, a * group : (a + 1) * group], halo)
        logistic = 0.5 + 0.5 * jnp.tanh(0.5 * preact)
        hidden = (preact * logistic).astype(BF)
        slope = logistic * (1.0 + preact * (1.0 - logistic))
        preact_grad = (hidden_grad_ref[k] * slope).astype(BF)
        tendency_grad = moist_grad_ref[part, :].astype(BF)
        grad_out += dot(tendency_grad, hidden, ((1,), (1,)))
        grad_in += dot(preact_grad, features_ref[k], ((1,), (1,)))
        grad_bias += dot(ones, preact_grad, ((1,), (1,)))
        moist_ref[part, :] = state[part] + dot(w_tendency_ref[...], hidden)
        stencil_grad = dot(w_stencil, preact_grad, ((0,), (0,)))
        sums.append([])
        for a in range(3):
            total = None
            for b in range(3):
                start = (3 * a + b) * channels
                piece = rolled(stencil_grad[start : start + channels], b - 1)
                total = piece if total is None else total + piece
            sums[k].append(total)
    to_north, to_south = sums[0][0], sums[-1][2]
    store_split(to_across_ref, 0, jnp.where(northern, to_north, to_south))
    store_split(to_inside_ref, 0, jnp.where(northern, to_south, to_north))
    for k in range(taken):
        total = moist_grad_ref[k * channels : (k + 1) * channels, :] + sums[k][1]
        if k > 0:
            total = total + sums[k - 1][2]
        if k + 1 < taken:
            total = total + sums[k + 1][0]
        store_split(grad_ref, k * channels, total)

    bias_high = grad_bias[0:1].astype(BF).astype(F32)
    bias_low = grad_bias[0:1] - bias_high
    tiles = hidden_units // LANES
    pieces = own_ref.shape[0]
    base, rest = split_rows(flat_ref.shape[1], pieces)
    stage_ref[:, :, base + rest :, :] = jnp.zeros((2, pieces, tiles, LANES), F32)
    for h in range(2):
        start = 0
        for value in (grad_in, grad_out):
            count = value.shape[0] // 2
            for t in range(value.shape[1] // LANES):
                flat_ref[h, start : start + count, :] = value[
                    h * count : (h + 1) * count, t * LANES : (t + 1) * LANES
                ]
                start += count
        for p in range(pieces):
            stage_ref[h, p, :base, :] = flat_ref[h, p * base : (p + 1) * base, :]
            start = pieces * base + p * rest
            stage_ref[h, p, base : base + rest, :] = flat_ref[h, start : start + rest, :]
        for p, half in enumerate((bias_high, bias_low)):
            for t in range(tiles):
                row = base + rest + t
                stage_ref[h, p, row : row + 1, :] = half[:, t * LANES : (t + 1) * LANES]
    core = position(place_ref[0], row_ref.shape[0])[0] % 2
    own_ref[...] = stage_ref[core]
    other_ref[...] = stage_ref[1 - core].astype(BF)


def fields_kernel(
    place_ref, moist_ref, scale_ref, high_ref, low_ref, grad_ref, across_ref, inside_ref, *refs
):
    sends, blocks_ref = refs[:-1], refs[-1]
    sectors, rows = grad_ref.shape[:2]
    channels = across_ref.shape[1]
    place = place_ref[0]
    _, q, pair = position(place, sectors)
    scale = own_scale(place, scale_ref, rows // channels, sectors, rows)
    store_split(blocks_ref, 0, filtered(moist_ref[...], scale, high_ref[...], low_ref[...]))
    for s in range(sectors):
        part = grad_ref[s]
        across, inside = across_ref[s].astype(F32), inside_ref[s].astype(F32)
        first = part[:channels] + jnp.where(pair == 0, across, inside)
        last = part[rows - channels :] + jnp.where(pair == 0, inside, across)
        inner = [part[channels : rows - channels]] if rows > 2 * channels else []
        blocks_ref[s, rows:, :] = jnp.concatenate([first] + inner + [last], axis=0).astype(BF)
    for t in range(sectors):
        sends[t][...] = blocks_ref[q ^ t]


def by_band_kernel(place_ref, *refs, band):
    blocks_ref = refs[-1]
    outs = refs[-3:-1]
    sectors, rows = blocks_ref.shape[0], blocks_ref.shape[1] // 2
    members = outs[0].shape[0]
    taken = band * members // sectors
    channels = rows // taken
    band_index, q, _ = position(place_ref[0], sectors)
    for t in range(sectors):
        blocks_ref[t] = refs[t][...].astype(F32)
    for m in range(members):
        for pair in range(2):
            t = q ^ (2 * m + (pair + band_index) % 2)
            for i in range(2):
                for k in range(taken):
                    start = i * rows + k * channels
                    outs[i][m, pl.ds(pair * taken + k, channels, stride=band), :] = blocks_ref[
                        t, start : start + channels, :
                    ]


def sum_and_copy_kernel(parts_ref, *refs):
    copies_ref = refs[-1]
    total = parts_ref[0].astype(F32)
    for p in range(1, parts_ref.shape[0]):
        total = total + parts_ref[p].astype(F32)
    total = total.astype(BF)
    for p in range(copies_ref.shape[0]):
        copies_ref[p] = total


def unpack_kernel(
    place_ref, own_ref, other_ref, grad_in_ref, grad_bias_ref, grad_out_ref, flat_ref,
    *, scaling, sectors
):
    pieces = own_ref.shape[0]
    base, rest = split_rows(flat_ref.shape[1], pieces)
    core = position(place_ref[0], sectors)[0] % 2
    bias = None
    for ref, h in ((own_ref, core), (other_ref, 1 - core)):
        for p in range(pieces):
            piece = ref[p].astype(F32) * scaling
            flat_ref[h, p * base : (p + 1) * base, :] = piece[:base]
            start = pieces * base + p * rest
            flat_ref[h, start : start + rest, :] = piece[base : base + rest]
            if ref is own_ref and p < 2:
                half = piece[base + rest :]
                bias = half if bias is None else bias + half
    for t in range(grad_bias_ref.shape[0] // LANES):
        grad_bias_ref[t * LANES : (t + 1) * LANES] = bias[t]
    for h in range(2):
        start = 0
        for ref in (grad_in_ref, grad_out_ref):
            count = ref.shape[0] // 2
            for t in range(ref.shape[1] // LANES):
                ref[h * count : (h + 1) * count, t * LANES : (t + 1) * LANES] = flat_ref[
                    h, start : start + count, :
                ]
                start += count


def call(kernel, outs, inputs, smem=0, scratch=(), flops=0, vmem=8, inputs_in=pltpu.VMEM, outs_in=pltpu.VMEM, **static):
    on_output = pl.BlockSpec(memory_space=outs_in)
    on_input = pl.BlockSpec(memory_space=inputs_in)
    on_smem = pl.BlockSpec(memory_space=pltpu.SMEM)

    def body(*refs):
        kernel(*refs, **static)

    return pl.pallas_call(
        body,
        out_shape=outs,
        in_specs=[on_smem] * smem + [on_input] * (inputs - smem),
        out_specs=jax.tree.map(lambda _: on_output, outs),
        scratch_shapes=list(scratch),
        cost_estimate=pl.CostEstimate(flops=flops, bytes_accessed=1_000_000, transcendentals=0),
        compiler_params=pltpu.CompilerParams(vmem_limit_bytes=vmem * MIB),
    )


def copy_kernel(x_ref, *refs):
    refs[-1][...] = x_ref[...]


def exchange(x, axes):
    return lax.all_to_all(x, axes, 0, 0, tiled=True)


def on_device(
    column_state,
    cotangent,
    land_mask,
    orography,
    member_seeds,
    land_table,
    relief_table,
    seed_table,
    w_hidden,
    b_hidden,
    w_tendency,
):
    members, channels, band, lon_cols = column_state.shape
    hidden_units, in_channels = w_hidden.shape
    classes = relief_table.shape[0]
    sectors = lax.axis_size("lon")
    peers = lax.axis_size(PLACE)
    lat_total = band * (peers // sectors)
    lon_total = lon_cols * sectors
    taken = band * members // sectors
    rows = taken * channels
    assert 2 * taken == band and 2 * members == sectors
    shape = jax.ShapeDtypeStruct
    place = lax.axis_index(PLACE)
    band_index, _, pair = position(place, sectors)
    place = place.reshape(1)

    with jax.named_scope("rows_in"):
        flat = (members, channels * band, lon_cols)
        packed_shape = (sectors, 2 * rows + 8, lon_cols)
        packed = call(
            by_row_kernel,
            shape(packed_shape, F32),
            5,
            smem=1,
            scratch=[
                pltpu.VMEM(flat, F32),
                pltpu.VMEM(flat, F32),
                pltpu.VMEM(land_mask.shape, land_mask.dtype),
                pltpu.VMEM(orography.shape, orography.dtype),
                pltpu.VMEM(packed_shape, F32),
                pltpu.SemaphoreType.DMA((6,)),
            ],
            vmem=56,
            inputs_in=pltpu.HBM,
            outs_in=pltpu.HBM,
            classes=classes,
        )(place, column_state.reshape(flat), cotangent.reshape(flat), land_mask, orography)
        row = exchange(packed, "lon")

    with jax.named_scope("row_halo"):
        inside_swaps, across_swaps = [], []
        for i in range(peers):
            _, q, southern = position(i, sectors)
            inside_swaps.append((i, i - q + (q ^ 1)))
            j = i + sectors if southern else i - sectors
            if 0 <= j < peers:
                across_swaps.append((i, j))

        def edge_row(southern):
            start = southern * (rows - channels)
            return lax.dynamic_slice_in_dim(row, start, channels, 1).astype(BF)

        inside = lax.ppermute(edge_row(1 - pair), PLACE, inside_swaps)
        across = lax.ppermute(edge_row(pair), PLACE, across_swaps)

    high, low, scale = [jnp.asarray(t) for t in filter_tables(lat_total, lon_total)]
    per_hidden = shape((taken, hidden_units, lon_total), F32)
    features_shape = (taken, in_channels, lon_total)
    with jax.named_scope("early"):
        moist_grad, features, preact, hidden_grad = call(
            early_kernel,
            (shape((rows, lon_total), F32), shape(features_shape, BF), per_hidden, per_hidden),
            12,
            smem=2,
            flops=3_000_000_000,
            vmem=24,
        )(
            place,
            member_seeds,
            row,
            scale,
            high,
            low,
            land_table,
            relief_table,
            seed_table,
            w_hidden,
            b_hidden.reshape(1, hidden_units),
            w_tendency,
        )

    pieces = lax.axis_size(PLANE)
    length = lax.axis_size("z")
    half_rows = (hidden_units * in_channels + channels * hidden_units) // (2 * LANES)
    piece_rows = half_rows // pieces + hidden_units // LANES
    share = (pieces, piece_rows, LANES)
    flat_rows = pltpu.VMEM((2, half_rows, LANES), F32)
    with jax.named_scope("weights"):
        block = (sectors, rows, LANES)
        edge = (sectors, channels, LANES)
        to_across, to_inside, moist, grad_rows, own, other = call(
            weights_kernel,
            (
                shape(edge, BF),
                shape(edge, BF),
                shape((rows, lon_total), F32),
                shape(block, F32),
                shape(share, F32),
                shape(share, BF),
            ),
            10,
            smem=1,
            scratch=[
                pltpu.VMEM(features_shape, BF),
                flat_rows,
                pltpu.VMEM((2,) + share, F32),
            ],
            flops=3_000_000_000,
            vmem=28,
        )(
            place,
            across,
            inside,
            row,
            moist_grad,
            features,
            preact,
            hidden_grad,
            w_hidden,
            w_tendency,
        )

    with jax.named_scope("weights_core"):
        swap = [(0, 1), (1, 0)]
        halves = (own + lax.ppermute(other, "core", swap).astype(F32)).astype(BF)

    with jax.named_scope("fields"):
        from_across = lax.ppermute(to_across, PLACE, across_swaps)
        from_inside = lax.ppermute(to_inside, PLACE, inside_swaps)
        fields = call(
            fields_kernel,
            (shape((2 * rows, LANES), BF),) * sectors,
            8,
            smem=1,
            scratch=[pltpu.VMEM((sectors, 2 * rows, LANES), BF)],
            flops=1_000_000_000,
        )(place, moist, scale, high, low, grad_rows, from_across, from_inside)

    with jax.named_scope("weights_plane"):
        copies = call(sum_and_copy_kernel, shape((length, piece_rows, LANES), BF), 2)(
            exchange(halves, PLANE), from_across
        )

    with jax.named_scope("rows_out"):
        received = [fields[0]]
        for t in range(1, sectors):
            received.append(lax.ppermute(fields[t], "lon", [(i, i ^ t) for i in range(sectors)]))

    with jax.named_scope("weights_length"):
        copies = call(sum_and_copy_kernel, shape(share, BF), 2)(
            exchange(copies, "z"), fields[0]
        )

    with jax.named_scope("bands_out"):
        next_state, state_grad = call(
            by_band_kernel,
            (shape(flat, F32), shape(flat, F32)),
            1 + sectors,
            smem=1,
            scratch=[pltpu.VMEM((sectors, 2 * rows, LANES), F32)],
            band=band,
        )(place, *received)
        next_state = next_state.reshape(column_state.shape)
        state_grad = state_grad.reshape(column_state.shape)

    with jax.named_scope("weights_back"):
        own = call(copy_kernel, shape(share, BF), sectors)(exchange(copies, PLANE), *received[1:])
        other = lax.ppermute(own, "core", swap)
        columns = members * lax.axis_size("mem") * lat_total * lon_total
        grad_in, grad_bias, grad_out = call(
            unpack_kernel,
            (
                shape((hidden_units, in_channels), F32),
                shape((hidden_units,), F32),
                shape((channels, hidden_units), F32),
            ),
            3,
            smem=1,
            scratch=[flat_rows],
            scaling=1.0 / math.sqrt(columns),
            sectors=sectors,
        )(place, own, other)
    return next_state, state_grad, grad_in, grad_bias, grad_out


def solution(mesh):
    lat, lon, mem = mesh.devices.shape
    devices = mesh.devices.reshape(2, lat // 4, 2, lon, mem)
    split = Mesh(devices, ("ylo", "z", "core", "lon", "mem"))
    lat_axes = ("ylo", "z", "core")
    field = P("mem", None, lat_axes, "lon")
    surface = P(lat_axes, "lon")
    whole = P()
    return jax.shard_map(
        on_device,
        mesh=split,
        in_specs=(field, field, surface, surface, P("mem")) + (whole,) * 6,
        out_specs=(field, field, whole, whole, whole),
        check_vma=False,
    )
```

```python
import math

import jax
import jax.numpy as jnp
import numpy as np
from jax import lax
from jax.experimental import pallas as pl
from jax.experimental.pallas import tpu as pltpu
from jax.sharding import Mesh, PartitionSpec as P

MODES = 171
DAMP = 2.0
LANES = 128
BF = jnp.bfloat16
F32 = jnp.float32
MIB = 1024 * 1024
PLACE = ("ylo", "z", "core", "lon")
PLANE = ("mem", "ylo", "lon")


def whole_multiple(value, unit):
    return -(-value // unit) * unit


def filter_tables(lat_total, lon_total):
    padded = whole_multiple(2 * MODES, LANES)
    k = np.arange(MODES)
    angles = (k[:, None] * np.arange(lon_total)[None]) % lon_total * (2.0 * math.pi / lon_total)
    analysis = np.zeros((padded, lon_total))
    analysis[: 2 * MODES] = np.concatenate([np.cos(angles), np.sin(angles)], 0)
    lat = math.pi * ((np.arange(lat_total) + 0.5) / lat_total - 0.5)
    removal = 1.0 - np.exp(-DAMP * (k[None] / MODES) ** 2 / np.cos(lat)[:, None] ** 2)
    removal = removal * np.where(k == 0, 1.0, 2.0) / lon_total
    scale = np.zeros((lat_total, padded), np.float32)
    scale[:, : 2 * MODES] = np.concatenate([removal, removal], 1)
    high = analysis.astype(np.float32).astype(BF)
    low = (analysis - high.astype(np.float64)).astype(np.float32).astype(BF)
    return high, low, scale


def split_rows(total, pieces):
    each = total // pieces
    return each // 8 * 8, each % 8


def dot(a, b, dims=((1,), (0,))):
    return lax.dot_general(a, b, (dims, ((), ())), preferred_element_type=F32)


def split_dot(x, high, low, dims=((1,), (0,))):
    x_high = x.astype(BF)
    x_low = (x - x_high.astype(F32)).astype(BF)
    return dot(x_high, high, dims) + (dot(x_low, high, dims) + dot(x_high, low, dims))


def filtered(x, scale, high, low):
    coeffs = split_dot(x, high, low, ((1,), (1,))) * scale
    return x - split_dot(coeffs, high, low)


def joined(ref, start, rows):
    return jnp.concatenate([ref[s, start : start + rows, :] for s in range(ref.shape[0])], axis=1)


def store_split(ref, start, value):
    for s in range(ref.shape[0]):
        ref[s, start : start + value.shape[0], :] = value[:, s * LANES : (s + 1) * LANES].astype(
            ref.dtype
        )


def position(place, sectors):
    band, q = place // sectors, place % sectors
    return band, q, (q + band) % 2


def by_row_kernel(
    place_ref, state_hbm, cotangent_hbm, land_hbm, orography_hbm, out_hbm,
    state_ref, cotangent_ref, land_ref, orography_ref, out_ref, sems, *, classes
):
    sectors, packed_rows = out_ref.shape[:2]
    rows = (packed_rows - 8) // 2
    members = state_ref.shape[0]
    band = land_ref.shape[0]
    taken = band * members // sectors
    channels = rows // taken
    odd = place_ref[0] // sectors % 2
    fields = ((state_hbm, state_ref), (cotangent_hbm, cotangent_ref))
    parts = [(source.at[m], target.at[m]) for source, target in fields for m in range(members)]
    parts += [(land_hbm, land_ref), (orography_hbm, orography_ref)]
    moves = [
        pltpu.make_async_copy(source, target, sems.at[i])
        for i, (source, target) in enumerate(parts)
    ]
    for move in moves:
        move.start()
    leaving = []
    for n in range(2 * members):
        i, m = n // members, n % members
        moves[n].wait()
        if n == members:
            moves[-2].wait()
            moves[-1].wait()
            code = (jnp.where(land_ref[...] == 1, classes, 0) + orography_ref[...]).astype(F32)
        for pair in range(2):
            q = 2 * m + (pair + odd) % 2
            first = pair * taken
            for k in range(taken):
                start = i * rows + k * channels
                out_ref[q, start : start + channels, :] = fields[i][1][
                    m, pl.ds(first + k, channels, stride=band), :
                ]
            if i == 1:
                spare = jnp.zeros((8 - taken, LANES), F32)
                out_ref[q, 2 * rows :, :] = jnp.concatenate(
                    [code[first : first + taken], spare], axis=0
                )
        part = (pl.ds(2 * m, 2), pl.ds(i * rows, rows if i == 0 else rows + 8))
        leaving.append(
            pltpu.make_async_copy(out_ref.at[part], out_hbm.at[part], sems.at[len(parts) + n])
        )
        leaving[n].start()
    for move in leaving:
        move.wait()


def own_scale(place, scale_ref, taken, sectors, rows):
    band, _, pair = position(place, sectors)
    first = (2 * band + pair) * taken
    channels = rows // taken
    wide = (channels, scale_ref.shape[1])
    return jnp.concatenate(
        [jnp.broadcast_to(scale_ref[pl.ds(first + k, 1), :], wide) for k in range(taken)], axis=0
    )


def rolled(value, shift):
    return pltpu.roll(value, shift % value.shape[1], 1) if shift else value


def early_kernel(
    place_ref,
    seeds_ref,
    row_ref,
    scale_ref,
    high_ref,
    low_ref,
    land_ref,
    relief_ref,
    seed_ref,
    w_hidden_ref,
    b_hidden_ref,
    w_tendency_ref,
    moist_grad_ref,
    features_ref,
    preact_ref,
    hidden_grad_ref,
):
    taken = features_ref.shape[0]
    sectors = row_ref.shape[0]
    channels, hidden_units = w_tendency_ref.shape
    rows = taken * channels
    lon_total = features_ref.shape[2]
    classes = relief_ref.shape[0]
    place = place_ref[0]
    scale = own_scale(place, scale_ref, taken, sectors, rows)
    moist_grad = filtered(joined(row_ref, rows, rows), scale, high_ref[...], low_ref[...])
    moist_grad_ref[...] = moist_grad
    rounded = joined(row_ref, 0, rows).astype(BF).astype(F32)
    for j in range(-1, taken + 1):
        for b in range(3):
            if 0 <= j < taken:
                moved = rolled(rounded[j * channels : (j + 1) * channels], 1 - b).astype(BF)
            else:
                moved = jnp.zeros((channels, lon_total), BF)
            for a in range(3):
                if 0 <= j + 1 - a < taken:
                    start = (3 * a + b) * channels
                    features_ref[j + 1 - a, start : start + channels, :] = moved
    class_ids = lax.broadcasted_iota(jnp.int32, (2 * classes, lon_total), 0).astype(F32)
    codes = joined(row_ref, 2 * rows, 8)
    surface = jnp.concatenate(
        [land_ref[0:1, :] + relief_ref[...], land_ref[1:2, :] + relief_ref[...]], axis=0
    )
    seed = seeds_ref[place % sectors // 2]
    table = (surface + seed_ref[pl.ds(seed, 1), :]).astype(BF)
    bias = jnp.transpose(jnp.broadcast_to(b_hidden_ref[...], (8, hidden_units)))[:, 0:1]
    for k in range(taken):
        pick = jnp.where(class_ids == codes[k : k + 1], 1.0, 0.0).astype(BF)
        features_ref[k, 9 * channels :, :] = dot(table, pick, ((0,), (0,))).astype(BF)
        preact_ref[k] = dot(w_hidden_ref[...], features_ref[k]) + bias
        tendency_grad = moist_grad[k * channels : (k + 1) * channels].astype(BF)
        hidden_grad_ref[k] = dot(w_tendency_ref[...], tendency_grad, ((0,), (0,)))


def weights_kernel(
    place_ref,
    across_ref,
    inside_ref,
    row_ref,
    moist_grad_ref,
    early_ref,
    preact_ref,
    hidden_grad_ref,
    w_hidden_ref,
    w_tendency_ref,
    to_across_ref,
    to_inside_ref,
    moist_ref,
    grad_ref,
    own_ref,
    other_ref,
    features_ref,
    flat_ref,
    stage_ref,
):
    taken, in_channels, lon_total = features_ref.shape
    channels, hidden_units = w_tendency_ref.shape
    group = 3 * channels
    w_stencil = w_hidden_ref[:, : 3 * group]
    state = joined(row_ref, 0, taken * channels)
    grad_in = jnp.zeros((hidden_units, in_channels), F32)
    grad_out = jnp.zeros((channels, hidden_units), F32)
    grad_bias = jnp.zeros((16, hidden_units), F32)
    ones = jnp.ones((16, lon_total), BF)
    northern = position(place_ref[0], row_ref.shape[0])[2] == 0
    across = joined(across_ref, 0, channels).astype(F32)
    inside = joined(inside_ref, 0, channels).astype(F32)
    edges = (
        (jnp.where(northern, across, inside), 0, 0),
        (jnp.where(northern, inside, across), 2, taken - 1),
    )
    sums = []
    for k in range(taken):
        part = slice(k * channels, (k + 1) * channels)
        features_ref[k] = early_ref[k]
        preact = preact_ref[k]
        for edge, a, row in edges:
            if row == k:
                halo = jnp.concatenate([rolled(edge, 1 - b).astype(BF) for b in range(3)], axis=0)
                features_ref[k, a * group : (a + 1) * group, :] = halo
                preact = preact + dot(w_hidden_ref[:, a * group : (a + 1) * group], halo)
        logistic = 0.5 + 0.5 * jnp.tanh(0.5 * preact)
        hidden = (preact * logistic).astype(BF)
        slope = logistic * (1.0 + preact * (1.0 - logistic))
        preact_grad = (hidden_grad_ref[k] * slope).astype(BF)
        tendency_grad = moist_grad_ref[part, :].astype(BF)
        grad_out += dot(tendency_grad, hidden, ((1,), (1,)))
        grad_in += dot(preact_grad, features_ref[k], ((1,), (1,)))
        grad_bias += dot(ones, preact_grad, ((1,), (1,)))
        moist_ref[part, :] = state[part] + dot(w_tendency_ref[...], hidden)
        stencil_grad = dot(w_stencil, preact_grad, ((0,), (0,)))
        sums.append([])
        for a in range(3):
            total = None
            for b in range(3):
                start = (3 * a + b) * channels
                piece = rolled(stencil_grad[start : start + channels], b - 1)
                total = piece if total is None else total + piece
            sums[k].append(total)
    to_north, to_south = sums[0][0], sums[-1][2]
    store_split(to_across_ref, 0, jnp.where(northern, to_north, to_south))
    store_split(to_inside_ref, 0, jnp.where(northern, to_south, to_north))
    for k in range(taken):
        total = moist_grad_ref[k * channels : (k + 1) * channels, :] + sums[k][1]
        if k > 0:
            total = total + sums[k - 1][2]
        if k + 1 < taken:
            total = total + sums[k + 1][0]
        store_split(grad_ref, k * channels, total)

    bias_high = grad_bias[0:1].astype(BF).astype(F32)
    bias_low = grad_bias[0:1] - bias_high
    tiles = hidden_units // LANES
    pieces = own_ref.shape[0]
    base, rest = split_rows(flat_ref.shape[1], pieces)
    stage_ref[:, :, base + rest :, :] = jnp.zeros((2, pieces, tiles, LANES), F32)
    for h in range(2):
        start = 0
        for value in (grad_in, grad_out):
            count = value.shape[0] // 2
            for t in range(value.shape[1] // LANES):
                flat_ref[h, start : start + count, :] = value[
                    h * count : (h + 1) * count, t * LANES : (t + 1) * LANES
                ]
                start += count
        for p in range(pieces):
            stage_ref[h, p, :base, :] = flat_ref[h, p * base : (p + 1) * base, :]
            start = pieces * base + p * rest
            stage_ref[h, p, base : base + rest, :] = flat_ref[h, start : start + rest, :]
        for p, half in enumerate((bias_high, bias_low)):
            for t in range(tiles):
                row = base + rest + t
                stage_ref[h, p, row : row + 1, :] = half[:, t * LANES : (t + 1) * LANES]
    core = position(place_ref[0], row_ref.shape[0])[0] % 2
    own_ref[...] = stage_ref[core]
    other_ref[...] = stage_ref[1 - core].astype(BF)


def fields_kernel(
    place_ref, moist_ref, scale_ref, high_ref, low_ref, grad_ref, across_ref, inside_ref, *refs
):
    sends, blocks_ref = refs[:-1], refs[-1]
    sectors, rows = grad_ref.shape[:2]
    channels = across_ref.shape[1]
    place = place_ref[0]
    _, q, pair = position(place, sectors)
    scale = own_scale(place, scale_ref, rows // channels, sectors, rows)
    store_split(blocks_ref, 0, filtered(moist_ref[...], scale, high_ref[...], low_ref[...]))
    for s in range(sectors):
        part = grad_ref[s]
        across, inside = across_ref[s].astype(F32), inside_ref[s].astype(F32)
        first = part[:channels] + jnp.where(pair == 0, across, inside)
        last = part[rows - channels :] + jnp.where(pair == 0, inside, across)
        inner = [part[channels : rows - channels]] if rows > 2 * channels else []
        blocks_ref[s, rows:, :] = jnp.concatenate([first] + inner + [last], axis=0).astype(BF)
    for t in range(sectors):
        sends[t][...] = blocks_ref[q ^ t]


def by_band_kernel(place_ref, *refs, band):
    blocks_ref = refs[-1]
    outs = refs[-3:-1]
    sectors, rows = blocks_ref.shape[0], blocks_ref.shape[1] // 2
    members = outs[0].shape[0]
    taken = band * members // sectors
    channels = rows // taken
    band_index, q, _ = position(place_ref[0], sectors)
    for t in range(sectors):
        blocks_ref[t] = refs[t][...].astype(F32)
    for m in range(members):
        for pair in range(2):
            t = q ^ (2 * m + (pair + band_index) % 2)
            for i in range(2):
                for k in range(taken):
                    start = i * rows + k * channels
                    outs[i][m, pl.ds(pair * taken + k, channels, stride=band), :] = blocks_ref[
                        t, start : start + channels, :
                    ]


def sum_and_copy_kernel(parts_ref, *refs):
    copies_ref = refs[-1]
    total = parts_ref[0].astype(F32)
    for p in range(1, parts_ref.shape[0]):
        total = total + parts_ref[p].astype(F32)
    total = total.astype(BF)
    for p in range(copies_ref.shape[0]):
        copies_ref[p] = total


def unpack_kernel(
    place_ref, own_ref, other_ref, grad_in_ref, grad_bias_ref, grad_out_ref, flat_ref,
    *, scaling, sectors
):
    pieces = own_ref.shape[0]
    base, rest = split_rows(flat_ref.shape[1], pieces)
    core = position(place_ref[0], sectors)[0] % 2
    bias = None
    for ref, h in ((own_ref, core), (other_ref, 1 - core)):
        for p in range(pieces):
            piece = ref[p].astype(F32) * scaling
            flat_ref[h, p * base : (p + 1) * base, :] = piece[:base]
            start = pieces * base + p * rest
            flat_ref[h, start : start + rest, :] = piece[base : base + rest]
            if ref is own_ref and p < 2:
                half = piece[base + rest :]
                bias = half if bias is None else bias + half
    for t in range(grad_bias_ref.shape[0] // LANES):
        grad_bias_ref[t * LANES : (t + 1) * LANES] = bias[t]
    for h in range(2):
        start = 0
        for ref in (grad_in_ref, grad_out_ref):
            count = ref.shape[0] // 2
            for t in range(ref.shape[1] // LANES):
                ref[h * count : (h + 1) * count, t * LANES : (t + 1) * LANES] = flat_ref[
                    h, start : start + count, :
                ]
                start += count


def call(kernel, outs, inputs, smem=0, scratch=(), flops=0, vmem=8, inputs_in=pltpu.VMEM, outs_in=pltpu.VMEM, **static):
    on_output = pl.BlockSpec(memory_space=outs_in)
    on_input = pl.BlockSpec(memory_space=inputs_in)
    on_smem = pl.BlockSpec(memory_space=pltpu.SMEM)

    def body(*refs):
        kernel(*refs, **static)

    return pl.pallas_call(
        body,
        out_shape=outs,
        in_specs=[on_smem] * smem + [on_input] * (inputs - smem),
        out_specs=jax.tree.map(lambda _: on_output, outs),
        scratch_shapes=list(scratch),
        cost_estimate=pl.CostEstimate(flops=flops, bytes_accessed=1_000_000, transcendentals=0),
        compiler_params=pltpu.CompilerParams(vmem_limit_bytes=vmem * MIB),
    )


def copy_kernel(x_ref, *refs):
    refs[-1][...] = x_ref[...]


def exchange(x, axes):
    return lax.all_to_all(x, axes, 0, 0, tiled=True)


def on_device(
    column_state,
    cotangent,
    land_mask,
    orography,
    member_seeds,
    land_table,
    relief_table,
    seed_table,
    w_hidden,
    b_hidden,
    w_tendency,
):
    members, channels, band, lon_cols = column_state.shape
    hidden_units, in_channels = w_hidden.shape
    classes = relief_table.shape[0]
    sectors = lax.axis_size("lon")
    peers = lax.axis_size(PLACE)
    lat_total = band * (peers // sectors)
    lon_total = lon_cols * sectors
    taken = band * members // sectors
    rows = taken * channels
    assert 2 * taken == band and 2 * members == sectors
    shape = jax.ShapeDtypeStruct
    place = lax.axis_index(PLACE)
    band_index, _, pair = position(place, sectors)
    place = place.reshape(1)

    with jax.named_scope("rows_in"):
        flat = (members, channels * band, lon_cols)
        packed_shape = (sectors, 2 * rows + 8, lon_cols)
        packed = call(
            by_row_kernel,
            shape(packed_shape, F32),
            5,
            smem=1,
            scratch=[
                pltpu.VMEM(flat, F32),
                pltpu.VMEM(flat, F32),
                pltpu.VMEM(land_mask.shape, land_mask.dtype),
                pltpu.VMEM(orography.shape, orography.dtype),
                pltpu.VMEM(packed_shape, F32),
                pltpu.SemaphoreType.DMA((4 * members + 2,)),
            ],
            vmem=56,
            inputs_in=pltpu.HBM,
            outs_in=pltpu.HBM,
            classes=classes,
        )(place, column_state.reshape(flat), cotangent.reshape(flat), land_mask, orography)
        row = exchange(packed, "lon")

    with jax.named_scope("row_halo"):
        inside_swaps, across_swaps = [], []
        for i in range(peers):
            _, q, southern = position(i, sectors)
            inside_swaps.append((i, i - q + (q ^ 1)))
            j = i + sectors if southern else i - sectors
            if 0 <= j < peers:
                across_swaps.append((i, j))

        def edge_row(southern):
            start = southern * (rows - channels)
            return lax.dynamic_slice_in_dim(row, start, channels, 1).astype(BF)

        inside = lax.ppermute(edge_row(1 - pair), PLACE, inside_swaps)
        across = lax.ppermute(edge_row(pair), PLACE, across_swaps)

    high, low, scale = [jnp.asarray(t) for t in filter_tables(lat_total, lon_total)]
    per_hidden = shape((taken, hidden_units, lon_total), F32)
    features_shape = (taken, in_channels, lon_total)
    with jax.named_scope("early"):
        moist_grad, features, preact, hidden_grad = call(
            early_kernel,
            (shape((rows, lon_total), F32), shape(features_shape, BF), per_hidden, per_hidden),
            12,
            smem=2,
            flops=3_000_000_000,
            vmem=24,
        )(
            place,
            member_seeds,
            row,
            scale,
            high,
            low,
            land_table,
            relief_table,
            seed_table,
            w_hidden,
            b_hidden.reshape(1, hidden_units),
            w_tendency,
        )

    pieces = lax.axis_size(PLANE)
    length = lax.axis_size("z")
    half_rows = (hidden_units * in_channels + channels * hidden_units) // (2 * LANES)
    piece_rows = half_rows // pieces + hidden_units // LANES
    share = (pieces, piece_rows, LANES)
    flat_rows = pltpu.VMEM((2, half_rows, LANES), F32)
    with jax.named_scope("weights"):
        block = (sectors, rows, LANES)
        edge = (sectors, channels, LANES)
        to_across, to_inside, moist, grad_rows, own, other = call(
            weights_kernel,
            (
                shape(edge, BF),
                shape(edge, BF),
                shape((rows, lon_total), F32),
                shape(block, F32),
                shape(share, F32),
                shape(share, BF),
            ),
            10,
            smem=1,
            scratch=[
                pltpu.VMEM(features_shape, BF),
                flat_rows,
                pltpu.VMEM((2,) + share, F32),
            ],
            flops=3_000_000_000,
            vmem=28,
        )(
            place,
            across,
            inside,
            row,
            moist_grad,
            features,
            preact,
            hidden_grad,
            w_hidden,
            w_tendency,
        )

    with jax.named_scope("weights_core"):
        swap = [(0, 1), (1, 0)]
        halves = (own + lax.ppermute(other, "core", swap).astype(F32)).astype(BF)

    with jax.named_scope("fields"):
        from_across = lax.ppermute(to_across, PLACE, across_swaps)
        from_inside = lax.ppermute(to_inside, PLACE, inside_swaps)
        fields = call(
            fields_kernel,
            (shape((2 * rows, LANES), BF),) * sectors,
            8,
            smem=1,
            scratch=[pltpu.VMEM((sectors, 2 * rows, LANES), BF)],
            flops=1_000_000_000,
        )(place, moist, scale, high, low, grad_rows, from_across, from_inside)

    with jax.named_scope("weights_plane"):
        copies = call(sum_and_copy_kernel, shape((length, piece_rows, LANES), BF), 3)(
            exchange(halves, PLANE), from_across, from_inside
        )

    with jax.named_scope("rows_out"):
        received = [fields[0]]
        for t in range(1, sectors):
            received.append(lax.ppermute(fields[t], "lon", [(i, i ^ t) for i in range(sectors)]))

    with jax.named_scope("weights_length"):
        copies = call(sum_and_copy_kernel, shape(share, BF), 2)(
            exchange(copies, "z"), received[1]
        )

    with jax.named_scope("bands_out"):
        next_state, state_grad = call(
            by_band_kernel,
            (shape(flat, F32), shape(flat, F32)),
            1 + sectors,
            smem=1,
            scratch=[pltpu.VMEM((sectors, 2 * rows, LANES), F32)],
            band=band,
        )(place, *received)
        next_state = next_state.reshape(column_state.shape)
        state_grad = state_grad.reshape(column_state.shape)

    with jax.named_scope("weights_back"):
        own = call(copy_kernel, shape(share, BF), sectors - 1)(exchange(copies, PLANE), *received[2:])
        other = lax.ppermute(own, "core", swap)
        columns = members * lax.axis_size("mem") * lat_total * lon_total
        grad_in, grad_bias, grad_out = call(
            unpack_kernel,
            (
                shape((hidden_units, in_channels), F32),
                shape((hidden_units,), F32),
                shape((channels, hidden_units), F32),
            ),
            3,
            smem=1,
            scratch=[flat_rows],
            scaling=1.0 / math.sqrt(columns),
            sectors=sectors,
        )(place, own, other)
    return next_state, state_grad, grad_in, grad_bias, grad_out


def solution(mesh):
    lat, lon, mem = mesh.devices.shape
    devices = mesh.devices.reshape(2, lat // 4, 2, lon, mem)
    split = Mesh(devices, ("ylo", "z", "core", "lon", "mem"))
    lat_axes = ("ylo", "z", "core")
    field = P("mem", None, lat_axes, "lon")
    surface = P(lat_axes, "lon")
    whole = P()
    return jax.shard_map(
        on_device,
        mesh=split,
        in_specs=(field, field, surface, surface, P("mem")) + (whole,) * 6,
        out_specs=(field, field, whole, whole, whole),
        check_vma=False,
    )
```

```python
import math

import jax
import jax.numpy as jnp
import numpy as np
from jax import lax
from jax.experimental import pallas as pl
from jax.experimental.pallas import tpu as pltpu
from jax.sharding import Mesh, PartitionSpec as P

MODES = 171
DAMP = 2.0
LANES = 128
BF = jnp.bfloat16
F32 = jnp.float32
MIB = 1024 * 1024
PLACE = ("ylo", "z", "core", "lon")
PLANE = ("mem", "ylo", "lon")


def whole_multiple(value, unit):
    return -(-value // unit) * unit


def filter_tables(lat_total, lon_total):
    padded = whole_multiple(2 * MODES, LANES)
    k = np.arange(MODES)
    angles = (k[:, None] * np.arange(lon_total)[None]) % lon_total * (2.0 * math.pi / lon_total)
    analysis = np.zeros((padded, lon_total))
    analysis[: 2 * MODES] = np.concatenate([np.cos(angles), np.sin(angles)], 0)
    lat = math.pi * ((np.arange(lat_total) + 0.5) / lat_total - 0.5)
    removal = 1.0 - np.exp(-DAMP * (k[None] / MODES) ** 2 / np.cos(lat)[:, None] ** 2)
    removal = removal * np.where(k == 0, 1.0, 2.0) / lon_total
    scale = np.zeros((lat_total, padded), np.float32)
    scale[:, : 2 * MODES] = np.concatenate([removal, removal], 1)
    high = analysis.astype(np.float32).astype(BF)
    low = (analysis - high.astype(np.float64)).astype(np.float32).astype(BF)
    return high, low, scale


def split_rows(total, pieces):
    each = total // pieces
    return each // 8 * 8, each % 8


def dot(a, b, dims=((1,), (0,))):
    return lax.dot_general(a, b, (dims, ((), ())), preferred_element_type=F32)


def split_dot(x, high, low, dims=((1,), (0,))):
    x_high = x.astype(BF)
    x_low = (x - x_high.astype(F32)).astype(BF)
    return dot(x_high, high, dims) + (dot(x_low, high, dims) + dot(x_high, low, dims))


def filtered(x, scale, high, low):
    coeffs = split_dot(x, high, low, ((1,), (1,))) * scale
    return x - split_dot(coeffs, high, low)


def joined(ref, start, rows):
    return jnp.concatenate([ref[s, start : start + rows, :] for s in range(ref.shape[0])], axis=1)


def store_split(ref, start, value):
    for s in range(ref.shape[0]):
        ref[s, start : start + value.shape[0], :] = value[:, s * LANES : (s + 1) * LANES].astype(
            ref.dtype
        )


def position(place, sectors):
    band, q = place // sectors, place % sectors
    return band, q, (q + band) % 2


def by_row_kernel(
    place_ref, state_hbm, cotangent_hbm, land_hbm, orography_hbm, out_hbm,
    state_ref, cotangent_ref, land_ref, orography_ref, out_ref, sems, *, classes
):
    sectors, packed_rows = out_ref.shape[:2]
    rows = (packed_rows - 8) // 2
    members = state_ref.shape[0]
    band = land_ref.shape[0]
    taken = band * members // sectors
    channels = rows // taken
    odd = place_ref[0] // sectors % 2
    fields = ((state_hbm, state_ref), (cotangent_hbm, cotangent_ref))
    parts = [(source.at[m], target.at[m]) for source, target in fields for m in range(members)]
    parts += [(land_hbm, land_ref), (orography_hbm, orography_ref)]
    moves = [
        pltpu.make_async_copy(source, target, sems.at[i])
        for i, (source, target) in enumerate(parts)
    ]
    for move in moves:
        move.start()
    leaving = []
    for n in range(2 * members):
        i, m = n // members, n % members
        moves[n].wait()
        if n == members:
            moves[-2].wait()
            moves[-1].wait()
            code = (jnp.where(land_ref[...] == 1, classes, 0) + orography_ref[...]).astype(F32)
        for pair in range(2):
            q = 2 * m + (pair + odd) % 2
            first = pair * taken
            for k in range(taken):
                start = i * rows + k * channels
                out_ref[q, start : start + channels, :] = fields[i][1][
                    m, pl.ds(first + k, channels, stride=band), :
                ]
            if i == 1:
                spare = jnp.zeros((8 - taken, LANES), F32)
                out_ref[q, 2 * rows :, :] = jnp.concatenate(
                    [code[first : first + taken], spare], axis=0
                )
        part = (pl.ds(2 * m, 2), pl.ds(i * rows, rows if i == 0 else rows + 8))
        leaving.append(
            pltpu.make_async_copy(out_ref.at[part], out_hbm.at[part], sems.at[len(parts) + n])
        )
        leaving[n].start()
    for move in leaving:
        move.wait()


def own_scale(place, scale_ref, taken, sectors, rows):
    band, _, pair = position(place, sectors)
    first = (2 * band + pair) * taken
    channels = rows // taken
    wide = (channels, scale_ref.shape[1])
    return jnp.concatenate(
        [jnp.broadcast_to(scale_ref[pl.ds(first + k, 1), :], wide) for k in range(taken)], axis=0
    )


def rolled(value, shift):
    return pltpu.roll(value, shift % value.shape[1], 1) if shift else value


def early_kernel(
    place_ref,
    seeds_ref,
    row_ref,
    scale_ref,
    high_ref,
    low_ref,
    land_ref,
    relief_ref,
    seed_ref,
    w_hidden_ref,
    b_hidden_ref,
    w_tendency_ref,
    moist_grad_ref,
    features_ref,
    preact_ref,
    hidden_grad_ref,
):
    taken = features_ref.shape[0]
    sectors = row_ref.shape[0]
    channels, hidden_units = w_tendency_ref.shape
    rows = taken * channels
    lon_total = features_ref.shape[2]
    classes = relief_ref.shape[0]
    place = place_ref[0]
    scale = own_scale(place, scale_ref, taken, sectors, rows)
    moist_grad = filtered(joined(row_ref, rows, rows), scale, high_ref[...], low_ref[...])
    moist_grad_ref[...] = moist_grad
    rounded = joined(row_ref, 0, rows).astype(BF).astype(F32)
    for j in range(-1, taken + 1):
        for b in range(3):
            if 0 <= j < taken:
                moved = rolled(rounded[j * channels : (j + 1) * channels], 1 - b).astype(BF)
            else:
                moved = jnp.zeros((channels, lon_total), BF)
            for a in range(3):
                if 0 <= j + 1 - a < taken:
                    start = (3 * a + b) * channels
                    features_ref[j + 1 - a, start : start + channels, :] = moved
    class_ids = lax.broadcasted_iota(jnp.int32, (2 * classes, lon_total), 0).astype(F32)
    codes = joined(row_ref, 2 * rows, 8)
    surface = jnp.concatenate(
        [land_ref[0:1, :] + relief_ref[...], land_ref[1:2, :] + relief_ref[...]], axis=0
    )
    seed = seeds_ref[place % sectors // 2]
    table = (surface + seed_ref[pl.ds(seed, 1), :]).astype(BF)
    bias = jnp.transpose(jnp.broadcast_to(b_hidden_ref[...], (8, hidden_units)))[:, 0:1]
    for k in range(taken):
        pick = jnp.where(class_ids == codes[k : k + 1], 1.0, 0.0).astype(BF)
        features_ref[k, 9 * channels :, :] = dot(table, pick, ((0,), (0,))).astype(BF)
        preact_ref[k] = dot(w_hidden_ref[...], features_ref[k]) + bias
        tendency_grad = moist_grad[k * channels : (k + 1) * channels].astype(BF)
        hidden_grad_ref[k] = dot(w_tendency_ref[...], tendency_grad, ((0,), (0,)))


def weights_kernel(
    place_ref,
    across_ref,
    inside_ref,
    row_ref,
    moist_grad_ref,
    early_ref,
    preact_ref,
    hidden_grad_ref,
    w_hidden_ref,
    w_tendency_ref,
    to_across_ref,
    to_inside_ref,
    moist_ref,
    grad_ref,
    own_ref,
    other_ref,
    features_ref,
    flat_ref,
    stage_ref,
):
    taken, in_channels, lon_total = features_ref.shape
    channels, hidden_units = w_tendency_ref.shape
    group = 3 * channels
    w_stencil = w_hidden_ref[:, : 3 * group]
    state = joined(row_ref, 0, taken * channels)
    grad_in = jnp.zeros((hidden_units, in_channels), F32)
    grad_out = jnp.zeros((channels, hidden_units), F32)
    grad_bias = jnp.zeros((16, hidden_units), F32)
    ones = jnp.ones((16, lon_total), BF)
    northern = position(place_ref[0], row_ref.shape[0])[2] == 0
    across = joined(across_ref, 0, channels).astype(F32)
    inside = joined(inside_ref, 0, channels).astype(F32)
    edges = (
        (jnp.where(northern, across, inside), 0, 0),
        (jnp.where(northern, inside, across), 2, taken - 1),
    )
    sums = []
    for k in range(taken):
        part = slice(k * channels, (k + 1) * channels)
        features_ref[k] = early_ref[k]
        preact = preact_ref[k]
        for edge, a, row in edges:
            if row == k:
                halo = jnp.concatenate([rolled(edge, 1 - b).astype(BF) for b in range(3)], axis=0)
                features_ref[k, a * group : (a + 1) * group, :] = halo
                preact = preact + dot(w_hidden_ref[:, a * group : (a + 1) * group], halo)
        logistic = 0.5 + 0.5 * jnp.tanh(0.5 * preact)
        hidden = (preact * logistic).astype(BF)
        slope = logistic * (1.0 + preact * (1.0 - logistic))
        preact_grad = (hidden_grad_ref[k] * slope).astype(BF)
        tendency_grad = moist_grad_ref[part, :].astype(BF)
        grad_out += dot(tendency_grad, hidden, ((1,), (1,)))
        grad_in += dot(preact_grad, features_ref[k], ((1,), (1,)))
        grad_bias += dot(ones, preact_grad, ((1,), (1,)))
        moist_ref[part, :] = state[part] + dot(w_tendency_ref[...], hidden)
        stencil_grad = dot(w_stencil, preact_grad, ((0,), (0,)))
        sums.append([])
        for a in range(3):
            total = None
            for b in range(3):
                start = (3 * a + b) * channels
                piece = rolled(stencil_grad[start : start + channels], b - 1)
                total = piece if total is None else total + piece
            sums[k].append(total)
    to_north, to_south = sums[0][0], sums[-1][2]
    store_split(to_across_ref, 0, jnp.where(northern, to_north, to_south))
    store_split(to_inside_ref, 0, jnp.where(northern, to_south, to_north))
    for k in range(taken):
        total = moist_grad_ref[k * channels : (k + 1) * channels, :] + sums[k][1]
        if k > 0:
            total = total + sums[k - 1][2]
        if k + 1 < taken:
            total = total + sums[k + 1][0]
        store_split(grad_ref, k * channels, total)

    bias_high = grad_bias[0:1].astype(BF).astype(F32)
    bias_low = grad_bias[0:1] - bias_high
    tiles = hidden_units // LANES
    pieces = own_ref.shape[0]
    base, rest = split_rows(flat_ref.shape[1], pieces)
    stage_ref[:, :, base + rest :, :] = jnp.zeros((2, pieces, tiles, LANES), F32)
    for h in range(2):
        start = 0
        for value in (grad_in, grad_out):
            count = value.shape[0] // 2
            for t in range(value.shape[1] // LANES):
                flat_ref[h, start : start + count, :] = value[
                    h * count : (h + 1) * count, t * LANES : (t + 1) * LANES
                ]
                start += count
        for p in range(pieces):
            stage_ref[h, p, :base, :] = flat_ref[h, p * base : (p + 1) * base, :]
            start = pieces * base + p * rest
            stage_ref[h, p, base : base + rest, :] = flat_ref[h, start : start + rest, :]
        for p, half in enumerate((bias_high, bias_low)):
            for t in range(tiles):
                row = base + rest + t
                stage_ref[h, p, row : row + 1, :] = half[:, t * LANES : (t + 1) * LANES]
    core = position(place_ref[0], row_ref.shape[0])[0] % 2
    own_ref[...] = stage_ref[core]
    other_ref[...] = stage_ref[1 - core].astype(BF)


def fields_kernel(
    place_ref, moist_ref, scale_ref, high_ref, low_ref, grad_ref, across_ref, inside_ref, *refs
):
    sends, blocks_ref = refs[:-1], refs[-1]
    sectors, rows = grad_ref.shape[:2]
    channels = across_ref.shape[1]
    place = place_ref[0]
    _, q, pair = position(place, sectors)
    scale = own_scale(place, scale_ref, rows // channels, sectors, rows)
    store_split(blocks_ref, 0, filtered(moist_ref[...], scale, high_ref[...], low_ref[...]))
    for s in range(sectors):
        part = grad_ref[s]
        across, inside = across_ref[s].astype(F32), inside_ref[s].astype(F32)
        first = part[:channels] + jnp.where(pair == 0, across, inside)
        last = part[rows - channels :] + jnp.where(pair == 0, inside, across)
        inner = [part[channels : rows - channels]] if rows > 2 * channels else []
        blocks_ref[s, rows:, :] = jnp.concatenate([first] + inner + [last], axis=0).astype(BF)
    for t in range(sectors):
        sends[t][...] = blocks_ref[q ^ t]


def by_band_kernel(place_ref, *refs, band):
    blocks_ref = refs[-1]
    outs = refs[-3:-1]
    sectors, rows = blocks_ref.shape[0], blocks_ref.shape[1] // 2
    members = outs[0].shape[0]
    taken = band * members // sectors
    channels = rows // taken
    band_index, q, _ = position(place_ref[0], sectors)
    for t in range(sectors):
        blocks_ref[t] = refs[t][...].astype(F32)
    for m in range(members):
        for pair in range(2):
            t = q ^ (2 * m + (pair + band_index) % 2)
            for i in range(2):
                for k in range(taken):
                    start = i * rows + k * channels
                    outs[i][m, pl.ds(pair * taken + k, channels, stride=band), :] = blocks_ref[
                        t, start : start + channels, :
                    ]


def sum_and_copy_kernel(parts_ref, *refs):
    copies_ref = refs[-1]
    total = parts_ref[0].astype(F32)
    for p in range(1, parts_ref.shape[0]):
        total = total + parts_ref[p].astype(F32)
    total = total.astype(BF)
    for p in range(copies_ref.shape[0]):
        copies_ref[p] = total


def unpack_kernel(
    place_ref, own_ref, other_ref, grad_in_ref, grad_bias_ref, grad_out_ref, flat_ref,
    *, scaling, sectors
):
    pieces = own_ref.shape[0]
    base, rest = split_rows(flat_ref.shape[1], pieces)
    core = position(place_ref[0], sectors)[0] % 2
    bias = None
    for ref, h in ((own_ref, core), (other_ref, 1 - core)):
        for p in range(pieces):
            piece = ref[p].astype(F32) * scaling
            flat_ref[h, p * base : (p + 1) * base, :] = piece[:base]
            start = pieces * base + p * rest
            flat_ref[h, start : start + rest, :] = piece[base : base + rest]
            if ref is own_ref and p < 2:
                half = piece[base + rest :]
                bias = half if bias is None else bias + half
    for t in range(grad_bias_ref.shape[0] // LANES):
        grad_bias_ref[t * LANES : (t + 1) * LANES] = bias[t]
    for h in range(2):
        start = 0
        for ref in (grad_in_ref, grad_out_ref):
            count = ref.shape[0] // 2
            for t in range(ref.shape[1] // LANES):
                ref[h * count : (h + 1) * count, t * LANES : (t + 1) * LANES] = flat_ref[
                    h, start : start + count, :
                ]
                start += count


def call(kernel, outs, inputs, smem=0, scratch=(), flops=0, vmem=8, inputs_in=pltpu.VMEM, outs_in=pltpu.VMEM, **static):
    on_output = pl.BlockSpec(memory_space=outs_in)
    on_input = pl.BlockSpec(memory_space=inputs_in)
    on_smem = pl.BlockSpec(memory_space=pltpu.SMEM)

    def body(*refs):
        kernel(*refs, **static)

    return pl.pallas_call(
        body,
        out_shape=outs,
        in_specs=[on_smem] * smem + [on_input] * (inputs - smem),
        out_specs=jax.tree.map(lambda _: on_output, outs),
        scratch_shapes=list(scratch),
        cost_estimate=pl.CostEstimate(flops=flops, bytes_accessed=1_000_000, transcendentals=0),
        compiler_params=pltpu.CompilerParams(vmem_limit_bytes=vmem * MIB),
    )


def copy_kernel(x_ref, *refs):
    refs[-1][...] = x_ref[...]


def exchange(x, axes):
    return lax.all_to_all(x, axes, 0, 0, tiled=True)


def on_device(
    column_state,
    cotangent,
    land_mask,
    orography,
    member_seeds,
    land_table,
    relief_table,
    seed_table,
    w_hidden,
    b_hidden,
    w_tendency,
):
    members, channels, band, lon_cols = column_state.shape
    hidden_units, in_channels = w_hidden.shape
    classes = relief_table.shape[0]
    sectors = lax.axis_size("lon")
    peers = lax.axis_size(PLACE)
    lat_total = band * (peers // sectors)
    lon_total = lon_cols * sectors
    taken = band * members // sectors
    rows = taken * channels
    assert 2 * taken == band and 2 * members == sectors
    shape = jax.ShapeDtypeStruct
    place = lax.axis_index(PLACE)
    band_index, _, pair = position(place, sectors)
    place = place.reshape(1)

    with jax.named_scope("rows_in"):
        flat = (members, channels * band, lon_cols)
        packed_shape = (sectors, 2 * rows + 8, lon_cols)
        packed = call(
            by_row_kernel,
            shape(packed_shape, F32),
            5,
            smem=1,
            scratch=[
                pltpu.VMEM(flat, F32),
                pltpu.VMEM(flat, F32),
                pltpu.VMEM(land_mask.shape, land_mask.dtype),
                pltpu.VMEM(orography.shape, orography.dtype),
                pltpu.VMEM(packed_shape, F32),
                pltpu.SemaphoreType.DMA((4 * members + 2,)),
            ],
            vmem=56,
            inputs_in=pltpu.HBM,
            outs_in=pltpu.HBM,
            classes=classes,
        )(place, column_state.reshape(flat), cotangent.reshape(flat), land_mask, orography)
        row = exchange(packed, "lon")

    with jax.named_scope("row_halo"):
        inside_swaps, across_swaps = [], []
        for i in range(peers):
            _, q, southern = position(i, sectors)
            inside_swaps.append((i, i - q + (q ^ 1)))
            j = i + sectors if southern else i - sectors
            if 0 <= j < peers:
                across_swaps.append((i, j))

        def edge_row(southern):
            start = southern * (rows - channels)
            return lax.dynamic_slice_in_dim(row, start, channels, 1).astype(BF)

        inside = lax.ppermute(edge_row(1 - pair), PLACE, inside_swaps)
        across = lax.ppermute(edge_row(pair), PLACE, across_swaps)

    high, low, scale = [jnp.asarray(t) for t in filter_tables(lat_total, lon_total)]
    per_hidden = shape((taken, hidden_units, lon_total), F32)
    features_shape = (taken, in_channels, lon_total)
    with jax.named_scope("early"):
        moist_grad, features, preact, hidden_grad = call(
            early_kernel,
            (shape((rows, lon_total), F32), shape(features_shape, BF), per_hidden, per_hidden),
            12,
            smem=2,
            flops=3_000_000_000,
            vmem=24,
        )(
            place,
            member_seeds,
            row,
            scale,
            high,
            low,
            land_table,
            relief_table,
            seed_table,
            w_hidden,
            b_hidden.reshape(1, hidden_units),
            w_tendency,
        )

    pieces = lax.axis_size(PLANE)
    length = lax.axis_size("z")
    half_rows = (hidden_units * in_channels + channels * hidden_units) // (2 * LANES)
    piece_rows = half_rows // pieces + hidden_units // LANES
    share = (pieces, piece_rows, LANES)
    flat_rows = pltpu.VMEM((2, half_rows, LANES), F32)
    with jax.named_scope("weights"):
        block = (sectors, rows, LANES)
        edge = (sectors, channels, LANES)
        to_across, to_inside, moist, grad_rows, own, other = call(
            weights_kernel,
            (
                shape(edge, BF),
                shape(edge, BF),
                shape((rows, lon_total), F32),
                shape(block, F32),
                shape(share, F32),
                shape(share, BF),
            ),
            10,
            smem=1,
            scratch=[
                pltpu.VMEM(features_shape, BF),
                flat_rows,
                pltpu.VMEM((2,) + share, F32),
            ],
            flops=3_000_000_000,
            vmem=28,
        )(
            place,
            across,
            inside,
            row,
            moist_grad,
            features,
            preact,
            hidden_grad,
            w_hidden,
            w_tendency,
        )

    with jax.named_scope("weights_core"):
        swap = [(0, 1), (1, 0)]
        halves = (own + lax.ppermute(other, "core", swap).astype(F32)).astype(BF)

    with jax.named_scope("fields"):
        from_across = lax.ppermute(to_across, PLACE, across_swaps)
        from_inside = lax.ppermute(to_inside, PLACE, inside_swaps)
        fields = call(
            fields_kernel,
            (shape((2 * rows, LANES), BF),) * sectors,
            8,
            smem=1,
            scratch=[pltpu.VMEM((sectors, 2 * rows, LANES), BF)],
            flops=1_000_000_000,
        )(place, moist, scale, high, low, grad_rows, from_across, from_inside)

    with jax.named_scope("weights_plane"):
        parts = exchange(halves, PLANE)
        piece = jnp.sum(parts.astype(F32), 0, keepdims=True).astype(BF)
        copies = jnp.broadcast_to(piece, (length, piece_rows, LANES))

    with jax.named_scope("rows_out"):
        received = [fields[0]]
        for t in range(1, sectors):
            received.append(lax.ppermute(fields[t], "lon", [(i, i ^ t) for i in range(sectors)]))

    with jax.named_scope("weights_length"):
        copies = call(sum_and_copy_kernel, shape(share, BF), 2)(
            exchange(copies, "z"), fields[0]
        )

    with jax.named_scope("bands_out"):
        next_state, state_grad = call(
            by_band_kernel,
            (shape(flat, F32), shape(flat, F32)),
            1 + sectors,
            smem=1,
            scratch=[pltpu.VMEM((sectors, 2 * rows, LANES), F32)],
            band=band,
        )(place, *received)
        next_state = next_state.reshape(column_state.shape)
        state_grad = state_grad.reshape(column_state.shape)

    with jax.named_scope("weights_back"):
        own = call(copy_kernel, shape(share, BF), sectors)(exchange(copies, PLANE), *received[1:])
        other = lax.ppermute(own, "core", swap)
        columns = members * lax.axis_size("mem") * lat_total * lon_total
        grad_in, grad_bias, grad_out = call(
            unpack_kernel,
            (
                shape((hidden_units, in_channels), F32),
                shape((hidden_units,), F32),
                shape((channels, hidden_units), F32),
            ),
            3,
            smem=1,
            scratch=[flat_rows],
            scaling=1.0 / math.sqrt(columns),
            sectors=sectors,
        )(place, own, other)
    return next_state, state_grad, grad_in, grad_bias, grad_out


def solution(mesh):
    lat, lon, mem = mesh.devices.shape
    devices = mesh.devices.reshape(2, lat // 4, 2, lon, mem)
    split = Mesh(devices, ("ylo", "z", "core", "lon", "mem"))
    lat_axes = ("ylo", "z", "core")
    field = P("mem", None, lat_axes, "lon")
    surface = P(lat_axes, "lon")
    whole = P()
    return jax.shard_map(
        on_device,
        mesh=split,
        in_specs=(field, field, surface, surface, P("mem")) + (whole,) * 6,
        out_specs=(field, field, whole, whole, whole),
        check_vma=False,
    )
```

```python
import math

import jax
import jax.numpy as jnp
import numpy as np
from jax import lax
from jax.experimental import pallas as pl
from jax.experimental.pallas import tpu as pltpu
from jax.sharding import Mesh, PartitionSpec as P

MODES = 171
DAMP = 2.0
LANES = 128
BF = jnp.bfloat16
F32 = jnp.float32
MIB = 1024 * 1024
PLACE = ("ylo", "z", "core", "lon")
PLANE = ("mem", "ylo", "lon")


def whole_multiple(value, unit):
    return -(-value // unit) * unit


def filter_tables(lat_total, lon_total):
    padded = whole_multiple(2 * MODES, LANES)
    k = np.arange(MODES)
    angles = (k[:, None] * np.arange(lon_total)[None]) % lon_total * (2.0 * math.pi / lon_total)
    analysis = np.zeros((padded, lon_total))
    analysis[: 2 * MODES] = np.concatenate([np.cos(angles), np.sin(angles)], 0)
    lat = math.pi * ((np.arange(lat_total) + 0.5) / lat_total - 0.5)
    removal = 1.0 - np.exp(-DAMP * (k[None] / MODES) ** 2 / np.cos(lat)[:, None] ** 2)
    removal = removal * np.where(k == 0, 1.0, 2.0) / lon_total
    scale = np.zeros((lat_total, padded), np.float32)
    scale[:, : 2 * MODES] = np.concatenate([removal, removal], 1)
    high = analysis.astype(np.float32).astype(BF)
    low = (analysis - high.astype(np.float64)).astype(np.float32).astype(BF)
    return high, low, scale


def split_rows(total, pieces):
    each = total // pieces
    return each // 8 * 8, each % 8


def dot(a, b, dims=((1,), (0,))):
    return lax.dot_general(a, b, (dims, ((), ())), preferred_element_type=F32)


def split_dot(x, high, low, dims=((1,), (0,))):
    x_high = x.astype(BF)
    x_low = (x - x_high.astype(F32)).astype(BF)
    both = dot(jnp.concatenate([x_high, x_low], axis=0), high, dims)
    count = x.shape[0]
    return both[:count] + (both[count:] + dot(x_high, low, dims))


def filtered(x, scale, high, low):
    coeffs = split_dot(x, high, low, ((1,), (1,))) * scale
    return x - split_dot(coeffs, high, low)


def joined(ref, start, rows):
    return jnp.concatenate([ref[s, start : start + rows, :] for s in range(ref.shape[0])], axis=1)


def store_split(ref, start, value):
    for s in range(ref.shape[0]):
        ref[s, start : start + value.shape[0], :] = value[:, s * LANES : (s + 1) * LANES].astype(
            ref.dtype
        )


def position(place, sectors):
    band, q = place // sectors, place % sectors
    return band, q, (q + band) % 2


def by_row_kernel(
    place_ref, state_hbm, cotangent_hbm, land_hbm, orography_hbm, out_hbm,
    state_ref, cotangent_ref, land_ref, orography_ref, out_ref, sems, *, classes
):
    sectors, packed_rows = out_ref.shape[:2]
    rows = (packed_rows - 8) // 2
    members = state_ref.shape[0]
    band = land_ref.shape[0]
    taken = band * members // sectors
    channels = rows // taken
    odd = place_ref[0] // sectors % 2
    fields = ((state_hbm, state_ref), (cotangent_hbm, cotangent_ref))
    parts = [(source.at[m], target.at[m]) for source, target in fields for m in range(members)]
    parts += [(land_hbm, land_ref), (orography_hbm, orography_ref)]
    moves = [
        pltpu.make_async_copy(source, target, sems.at[i])
        for i, (source, target) in enumerate(parts)
    ]
    for move in moves:
        move.start()
    leaving = []
    for n in range(2 * members):
        i, m = n // members, n % members
        moves[n].wait()
        if n == members:
            moves[-2].wait()
            moves[-1].wait()
            code = (jnp.where(land_ref[...] == 1, classes, 0) + orography_ref[...]).astype(F32)
        for pair in range(2):
            q = 2 * m + (pair + odd) % 2
            first = pair * taken
            for k in range(taken):
                start = i * rows + k * channels
                out_ref[q, start : start + channels, :] = fields[i][1][
                    m, pl.ds(first + k, channels, stride=band), :
                ]
            if i == 1:
                spare = jnp.zeros((8 - taken, LANES), F32)
                out_ref[q, 2 * rows :, :] = jnp.concatenate(
                    [code[first : first + taken], spare], axis=0
                )
        part = (pl.ds(2 * m, 2), pl.ds(i * rows, rows if i == 0 else rows + 8))
        leaving.append(
            pltpu.make_async_copy(out_ref.at[part], out_hbm.at[part], sems.at[len(parts) + n])
        )
        leaving[n].start()
    for move in leaving:
        move.wait()


def own_scale(place, scale_ref, taken, sectors, rows):
    band, _, pair = position(place, sectors)
    first = (2 * band + pair) * taken
    channels = rows // taken
    wide = (channels, scale_ref.shape[1])
    return jnp.concatenate(
        [jnp.broadcast_to(scale_ref[pl.ds(first + k, 1), :], wide) for k in range(taken)], axis=0
    )


def rolled(value, shift):
    return pltpu.roll(value, shift % value.shape[1], 1) if shift else value


def early_kernel(
    place_ref,
    seeds_ref,
    row_ref,
    scale_ref,
    high_ref,
    low_ref,
    land_ref,
    relief_ref,
    seed_ref,
    w_hidden_ref,
    b_hidden_ref,
    w_tendency_ref,
    moist_grad_ref,
    features_ref,
    preact_ref,
    hidden_grad_ref,
):
    taken = features_ref.shape[0]
    sectors = row_ref.shape[0]
    hidden_units, channels = w_tendency_ref.shape
    rows = taken * channels
    lon_total = features_ref.shape[2]
    classes = relief_ref.shape[0]
    place = place_ref[0]
    scale = own_scale(place, scale_ref, taken, sectors, rows)
    moist_grad = filtered(joined(row_ref, rows, rows), scale, high_ref[...], low_ref[...])
    moist_grad_ref[...] = moist_grad
    rounded = joined(row_ref, 0, rows).astype(BF).astype(F32)
    for j in range(-1, taken + 1):
        for b in range(3):
            if 0 <= j < taken:
                moved = rolled(rounded[j * channels : (j + 1) * channels], 1 - b).astype(BF)
            else:
                moved = jnp.zeros((channels, lon_total), BF)
            for a in range(3):
                if 0 <= j + 1 - a < taken:
                    start = (3 * a + b) * channels
                    features_ref[j + 1 - a, start : start + channels, :] = moved
    class_ids = lax.broadcasted_iota(jnp.int32, (2 * classes, lon_total), 0).astype(F32)
    codes = joined(row_ref, 2 * rows, 8)
    surface = jnp.concatenate(
        [land_ref[0:1, :] + relief_ref[...], land_ref[1:2, :] + relief_ref[...]], axis=0
    )
    seed = seeds_ref[place % sectors // 2]
    table = (surface + seed_ref[pl.ds(seed, 1), :]).astype(BF)
    bias = jnp.transpose(jnp.broadcast_to(b_hidden_ref[...], (8, hidden_units)))[:, 0:1]
    for k in range(taken):
        pick = jnp.where(class_ids == codes[k : k + 1], 1.0, 0.0).astype(BF)
        features_ref[k, 9 * channels :, :] = dot(table, pick, ((0,), (0,))).astype(BF)
        preact_ref[k] = dot(w_hidden_ref[...], features_ref[k]) + bias
        tendency_grad = moist_grad[k * channels : (k + 1) * channels].astype(BF)
        hidden_grad_ref[k] = dot(w_tendency_ref[...], tendency_grad)


def weights_kernel(
    place_ref,
    across_ref,
    inside_ref,
    row_ref,
    moist_grad_ref,
    early_ref,
    preact_ref,
    hidden_grad_ref,
    w_hidden_ref,
    w_stencil_ref,
    w_tendency_ref,
    to_across_ref,
    to_inside_ref,
    moist_ref,
    grad_ref,
    own_ref,
    other_ref,
    features_ref,
    flat_ref,
    stage_ref,
):
    taken, in_channels, lon_total = features_ref.shape
    channels, hidden_units = w_tendency_ref.shape
    group = 3 * channels
    state = joined(row_ref, 0, taken * channels)
    grad_in = jnp.zeros((hidden_units, in_channels), F32)
    grad_out = jnp.zeros((channels, hidden_units), F32)
    grad_bias = jnp.zeros((16, hidden_units), F32)
    ones = jnp.ones((16, lon_total), BF)
    northern = position(place_ref[0], row_ref.shape[0])[2] == 0
    across = joined(across_ref, 0, channels).astype(F32)
    inside = joined(inside_ref, 0, channels).astype(F32)
    edges = (
        (jnp.where(northern, across, inside), 0, 0),
        (jnp.where(northern, inside, across), 2, taken - 1),
    )
    sums = []
    for k in range(taken):
        part = slice(k * channels, (k + 1) * channels)
        features_ref[k] = early_ref[k]
        preact = preact_ref[k]
        for edge, a, row in edges:
            if row == k:
                halo = jnp.concatenate([rolled(edge, 1 - b).astype(BF) for b in range(3)], axis=0)
                features_ref[k, a * group : (a + 1) * group, :] = halo
                preact = preact + dot(w_hidden_ref[:, a * group : (a + 1) * group], halo)
        logistic = 0.5 + 0.5 * jnp.tanh(0.5 * preact)
        hidden = (preact * logistic).astype(BF)
        slope = logistic * (1.0 + preact * (1.0 - logistic))
        preact_grad = (hidden_grad_ref[k] * slope).astype(BF)
        tendency_grad = moist_grad_ref[part, :].astype(BF)
        grad_out += dot(tendency_grad, hidden, ((1,), (1,)))
        grad_in += dot(preact_grad, features_ref[k], ((1,), (1,)))
        grad_bias += dot(ones, preact_grad, ((1,), (1,)))
        moist_ref[part, :] = state[part] + dot(w_tendency_ref[...], hidden)
        stencil_grad = dot(w_stencil_ref[...], preact_grad)
        sums.append([])
        for a in range(3):
            total = None
            for b in range(3):
                start = (3 * a + b) * channels
                piece = rolled(stencil_grad[start : start + channels], b - 1)
                total = piece if total is None else total + piece
            sums[k].append(total)
    to_north, to_south = sums[0][0], sums[-1][2]
    store_split(to_across_ref, 0, jnp.where(northern, to_north, to_south))
    store_split(to_inside_ref, 0, jnp.where(northern, to_south, to_north))
    for k in range(taken):
        total = moist_grad_ref[k * channels : (k + 1) * channels, :] + sums[k][1]
        if k > 0:
            total = total + sums[k - 1][2]
        if k + 1 < taken:
            total = total + sums[k + 1][0]
        store_split(grad_ref, k * channels, total)

    bias_high = grad_bias[0:1].astype(BF).astype(F32)
    bias_low = grad_bias[0:1] - bias_high
    tiles = hidden_units // LANES
    pieces = own_ref.shape[0]
    base, rest = split_rows(flat_ref.shape[1], pieces)
    stage_ref[:, :, base + rest :, :] = jnp.zeros((2, pieces, tiles, LANES), F32)
    for h in range(2):
        start = 0
        for value in (grad_in, grad_out):
            count = value.shape[0] // 2
            for t in range(value.shape[1] // LANES):
                flat_ref[h, start : start + count, :] = value[
                    h * count : (h + 1) * count, t * LANES : (t + 1) * LANES
                ]
                start += count
        for p in range(pieces):
            stage_ref[h, p, :base, :] = flat_ref[h, p * base : (p + 1) * base, :]
            start = pieces * base + p * rest
            stage_ref[h, p, base : base + rest, :] = flat_ref[h, start : start + rest, :]
        for p, half in enumerate((bias_high, bias_low)):
            for t in range(tiles):
                row = base + rest + t
                stage_ref[h, p, row : row + 1, :] = half[:, t * LANES : (t + 1) * LANES]
    core = position(place_ref[0], row_ref.shape[0])[0] % 2
    own_ref[...] = stage_ref[core]
    other_ref[...] = stage_ref[1 - core].astype(BF)


def fields_kernel(
    place_ref, moist_ref, scale_ref, high_ref, low_ref, grad_ref, across_ref, inside_ref, *refs
):
    sends, blocks_ref = refs[:-1], refs[-1]
    sectors, rows = grad_ref.shape[:2]
    channels = across_ref.shape[1]
    place = place_ref[0]
    _, q, pair = position(place, sectors)
    scale = own_scale(place, scale_ref, rows // channels, sectors, rows)
    store_split(blocks_ref, 0, filtered(moist_ref[...], scale, high_ref[...], low_ref[...]))
    for s in range(sectors):
        part = grad_ref[s]
        across, inside = across_ref[s].astype(F32), inside_ref[s].astype(F32)
        first = part[:channels] + jnp.where(pair == 0, across, inside)
        last = part[rows - channels :] + jnp.where(pair == 0, inside, across)
        inner = [part[channels : rows - channels]] if rows > 2 * channels else []
        blocks_ref[s, rows:, :] = jnp.concatenate([first] + inner + [last], axis=0).astype(BF)
    for t in range(sectors):
        sends[t][...] = blocks_ref[q ^ t]


def by_band_kernel(place_ref, *refs, band):
    blocks_ref = refs[-1]
    outs = refs[-3:-1]
    sectors, rows = blocks_ref.shape[0], blocks_ref.shape[1] // 2
    members = outs[0].shape[0]
    taken = band * members // sectors
    channels = rows // taken
    band_index, q, _ = position(place_ref[0], sectors)
    for t in range(sectors):
        blocks_ref[t] = refs[t][...].astype(F32)
    for m in range(members):
        for pair in range(2):
            t = q ^ (2 * m + (pair + band_index) % 2)
            for i in range(2):
                for k in range(taken):
                    start = i * rows + k * channels
                    outs[i][m, pl.ds(pair * taken + k, channels, stride=band), :] = blocks_ref[
                        t, start : start + channels, :
                    ]


def sum_and_copy_kernel(parts_ref, *refs):
    copies_ref = refs[-1]
    total = parts_ref[0].astype(F32)
    for p in range(1, parts_ref.shape[0]):
        total = total + parts_ref[p].astype(F32)
    total = total.astype(BF)
    for p in range(copies_ref.shape[0]):
        copies_ref[p] = total


def unpack_kernel(
    place_ref, own_ref, other_ref, grad_in_ref, grad_bias_ref, grad_out_ref, flat_ref,
    *, scaling, sectors
):
    pieces = own_ref.shape[0]
    base, rest = split_rows(flat_ref.shape[1], pieces)
    core = position(place_ref[0], sectors)[0] % 2
    bias = None
    for ref, h in ((own_ref, core), (other_ref, 1 - core)):
        for p in range(pieces):
            piece = ref[p].astype(F32) * scaling
            flat_ref[h, p * base : (p + 1) * base, :] = piece[:base]
            start = pieces * base + p * rest
            flat_ref[h, start : start + rest, :] = piece[base : base + rest]
            if ref is own_ref and p < 2:
                half = piece[base + rest :]
                bias = half if bias is None else bias + half
    for t in range(grad_bias_ref.shape[0] // LANES):
        grad_bias_ref[t * LANES : (t + 1) * LANES] = bias[t]
    for h in range(2):
        start = 0
        for ref in (grad_in_ref, grad_out_ref):
            count = ref.shape[0] // 2
            for t in range(ref.shape[1] // LANES):
                ref[h * count : (h + 1) * count, t * LANES : (t + 1) * LANES] = flat_ref[
                    h, start : start + count, :
                ]
                start += count


def call(kernel, outs, inputs, smem=0, scratch=(), flops=0, vmem=8, inputs_in=pltpu.VMEM, outs_in=pltpu.VMEM, **static):
    on_output = pl.BlockSpec(memory_space=outs_in)
    on_input = pl.BlockSpec(memory_space=inputs_in)
    on_smem = pl.BlockSpec(memory_space=pltpu.SMEM)

    def body(*refs):
        kernel(*refs, **static)

    return pl.pallas_call(
        body,
        out_shape=outs,
        in_specs=[on_smem] * smem + [on_input] * (inputs - smem),
        out_specs=jax.tree.map(lambda _: on_output, outs),
        scratch_shapes=list(scratch),
        cost_estimate=pl.CostEstimate(flops=flops, bytes_accessed=1_000_000, transcendentals=0),
        compiler_params=pltpu.CompilerParams(vmem_limit_bytes=vmem * MIB),
    )


def copy_kernel(x_ref, *refs):
    refs[-1][...] = x_ref[...]


def exchange(x, axes):
    return lax.all_to_all(x, axes, 0, 0, tiled=True)


def on_device(
    column_state,
    cotangent,
    land_mask,
    orography,
    member_seeds,
    land_table,
    relief_table,
    seed_table,
    w_hidden,
    b_hidden,
    w_tendency,
):
    members, channels, band, lon_cols = column_state.shape
    hidden_units, in_channels = w_hidden.shape
    classes = relief_table.shape[0]
    sectors = lax.axis_size("lon")
    peers = lax.axis_size(PLACE)
    lat_total = band * (peers // sectors)
    lon_total = lon_cols * sectors
    taken = band * members // sectors
    rows = taken * channels
    assert 2 * taken == band and 2 * members == sectors
    shape = jax.ShapeDtypeStruct
    place = lax.axis_index(PLACE)
    band_index, _, pair = position(place, sectors)
    place = place.reshape(1)

    with jax.named_scope("rows_in"):
        flat = (members, channels * band, lon_cols)
        packed_shape = (sectors, 2 * rows + 8, lon_cols)
        packed = call(
            by_row_kernel,
            shape(packed_shape, F32),
            5,
            smem=1,
            scratch=[
                pltpu.VMEM(flat, F32),
                pltpu.VMEM(flat, F32),
                pltpu.VMEM(land_mask.shape, land_mask.dtype),
                pltpu.VMEM(orography.shape, orography.dtype),
                pltpu.VMEM(packed_shape, F32),
                pltpu.SemaphoreType.DMA((4 * members + 2,)),
            ],
            vmem=56,
            inputs_in=pltpu.HBM,
            outs_in=pltpu.HBM,
            classes=classes,
        )(place, column_state.reshape(flat), cotangent.reshape(flat), land_mask, orography)
        row = exchange(packed, "lon")

    with jax.named_scope("row_halo"):
        inside_swaps, across_swaps = [], []
        for i in range(peers):
            _, q, southern = position(i, sectors)
            inside_swaps.append((i, i - q + (q ^ 1)))
            j = i + sectors if southern else i - sectors
            if 0 <= j < peers:
                across_swaps.append((i, j))

        def edge_row(southern):
            start = southern * (rows - channels)
            return lax.dynamic_slice_in_dim(row, start, channels, 1).astype(BF)

        inside = lax.ppermute(edge_row(1 - pair), PLACE, inside_swaps)
        across = lax.ppermute(edge_row(pair), PLACE, across_swaps)

    high, low, scale = [jnp.asarray(t) for t in filter_tables(lat_total, lon_total)]
    per_hidden = shape((taken, hidden_units, lon_total), F32)
    features_shape = (taken, in_channels, lon_total)
    with jax.named_scope("early"):
        moist_grad, features, preact, hidden_grad = call(
            early_kernel,
            (shape((rows, lon_total), F32), shape(features_shape, BF), per_hidden, per_hidden),
            12,
            smem=2,
            flops=3_000_000_000,
            vmem=24,
        )(
            place,
            member_seeds,
            row,
            scale,
            high,
            low,
            land_table,
            relief_table,
            seed_table,
            w_hidden,
            b_hidden.reshape(1, hidden_units),
            w_tendency.T,
        )

    pieces = lax.axis_size(PLANE)
    length = lax.axis_size("z")
    half_rows = (hidden_units * in_channels + channels * hidden_units) // (2 * LANES)
    piece_rows = half_rows // pieces + hidden_units // LANES
    share = (pieces, piece_rows, LANES)
    flat_rows = pltpu.VMEM((2, half_rows, LANES), F32)
    with jax.named_scope("weights"):
        block = (sectors, rows, LANES)
        edge = (sectors, channels, LANES)
        to_across, to_inside, moist, grad_rows, own, other = call(
            weights_kernel,
            (
                shape(edge, BF),
                shape(edge, BF),
                shape((rows, lon_total), F32),
                shape(block, F32),
                shape(share, F32),
                shape(share, BF),
            ),
            11,
            smem=1,
            scratch=[
                pltpu.VMEM(features_shape, BF),
                flat_rows,
                pltpu.VMEM((2,) + share, F32),
            ],
            flops=3_000_000_000,
            vmem=28,
        )(
            place,
            across,
            inside,
            row,
            moist_grad,
            features,
            preact,
            hidden_grad,
            w_hidden,
            w_hidden[:, : 9 * channels].T,
            w_tendency,
        )

    with jax.named_scope("weights_core"):
        swap = [(0, 1), (1, 0)]
        halves = (own + lax.ppermute(other, "core", swap).astype(F32)).astype(BF)

    with jax.named_scope("fields"):
        from_across = lax.ppermute(to_across, PLACE, across_swaps)
        from_inside = lax.ppermute(to_inside, PLACE, inside_swaps)
        fields = call(
            fields_kernel,
            (shape((2 * rows, LANES), BF),) * sectors,
            8,
            smem=1,
            scratch=[pltpu.VMEM((sectors, 2 * rows, LANES), BF)],
            flops=1_000_000_000,
        )(place, moist, scale, high, low, grad_rows, from_across, from_inside)

    with jax.named_scope("weights_plane"):
        copies = call(sum_and_copy_kernel, shape((length, piece_rows, LANES), BF), 2)(
            exchange(halves, PLANE), from_across
        )

    with jax.named_scope("rows_out"):
        received = [fields[0]]
        for t in range(1, sectors):
            received.append(lax.ppermute(fields[t], "lon", [(i, i ^ t) for i in range(sectors)]))

    with jax.named_scope("weights_length"):
        copies = call(sum_and_copy_kernel, shape(share, BF), 2)(
            exchange(copies, "z"), fields[0]
        )

    with jax.named_scope("bands_out"):
        next_state, state_grad = call(
            by_band_kernel,
            (shape(flat, F32), shape(flat, F32)),
            1 + sectors,
            smem=1,
            scratch=[pltpu.VMEM((sectors, 2 * rows, LANES), F32)],
            band=band,
        )(place, *received)
        next_state = next_state.reshape(column_state.shape)
        state_grad = state_grad.reshape(column_state.shape)

    with jax.named_scope("weights_back"):
        own = call(copy_kernel, shape(share, BF), sectors)(exchange(copies, PLANE), *received[1:])
        other = lax.ppermute(own, "core", swap)
        columns = members * lax.axis_size("mem") * lat_total * lon_total
        grad_in, grad_bias, grad_out = call(
            unpack_kernel,
            (
                shape((hidden_units, in_channels), F32),
                shape((hidden_units,), F32),
                shape((channels, hidden_units), F32),
            ),
            3,
            smem=1,
            scratch=[flat_rows],
            scaling=1.0 / math.sqrt(columns),
            sectors=sectors,
        )(place, own, other)
    return next_state, state_grad, grad_in, grad_bias, grad_out


def solution(mesh):
    lat, lon, mem = mesh.devices.shape
    devices = mesh.devices.reshape(2, lat // 4, 2, lon, mem)
    split = Mesh(devices, ("ylo", "z", "core", "lon", "mem"))
    lat_axes = ("ylo", "z", "core")
    field = P("mem", None, lat_axes, "lon")
    surface = P(lat_axes, "lon")
    whole = P()
    return jax.shard_map(
        on_device,
        mesh=split,
        in_specs=(field, field, surface, surface, P("mem")) + (whole,) * 6,
        out_specs=(field, field, whole, whole, whole),
        check_vma=False,
    )
```

```python
import math

import jax
import jax.numpy as jnp
import numpy as np
from jax import lax
from jax.experimental import pallas as pl
from jax.experimental.pallas import tpu as pltpu
from jax.sharding import Mesh, PartitionSpec as P

MODES = 171
DAMP = 2.0
LANES = 128
BF = jnp.bfloat16
F32 = jnp.float32
MIB = 1024 * 1024
PLACE = ("ylo", "z", "core", "lon")
PLANE = ("mem", "ylo", "lon")


def whole_multiple(value, unit):
    return -(-value // unit) * unit


def filter_tables(lat_total, lon_total):
    padded = whole_multiple(2 * MODES, LANES)
    k = np.arange(MODES)
    angles = (k[:, None] * np.arange(lon_total)[None]) % lon_total * (2.0 * math.pi / lon_total)
    analysis = np.zeros((padded, lon_total))
    analysis[: 2 * MODES] = np.concatenate([np.cos(angles), np.sin(angles)], 0)
    lat = math.pi * ((np.arange(lat_total) + 0.5) / lat_total - 0.5)
    removal = 1.0 - np.exp(-DAMP * (k[None] / MODES) ** 2 / np.cos(lat)[:, None] ** 2)
    removal = removal * np.where(k == 0, 1.0, 2.0) / lon_total
    scale = np.zeros((lat_total, padded), np.float32)
    scale[:, : 2 * MODES] = np.concatenate([removal, removal], 1)
    high = analysis.astype(np.float32).astype(BF)
    low = (analysis - high.astype(np.float64)).astype(np.float32).astype(BF)
    return high, low, scale


def split_rows(total, pieces):
    each = total // pieces
    return each // 8 * 8, each % 8


def dot(a, b, dims=((1,), (0,))):
    return lax.dot_general(a, b, (dims, ((), ())), preferred_element_type=F32)


def split_dot(x, high, low, dims=((1,), (0,))):
    x_high = x.astype(BF)
    x_low = (x - x_high.astype(F32)).astype(BF)
    both = dot(jnp.concatenate([x_high, x_low], axis=0), high, dims)
    count = x.shape[0]
    return both[:count] + (both[count:] + dot(x_high, low, dims))


def filtered(x, scale, high, low):
    coeffs = split_dot(x, high, low, ((1,), (1,))) * scale
    return x - split_dot(coeffs, high, low)


def joined(ref, start, rows):
    return jnp.concatenate([ref[s, start : start + rows, :] for s in range(ref.shape[0])], axis=1)


def store_split(ref, start, value):
    for s in range(ref.shape[0]):
        ref[s, start : start + value.shape[0], :] = value[:, s * LANES : (s + 1) * LANES].astype(
            ref.dtype
        )


def position(place, sectors):
    band, q = place // sectors, place % sectors
    return band, q, (q + band) % 2


def by_row_kernel(
    place_ref, state_hbm, cotangent_hbm, land_hbm, orography_hbm, out_hbm,
    state_ref, cotangent_ref, land_ref, orography_ref, out_ref, sems, *, classes
):
    sectors, packed_rows = out_ref.shape[:2]
    rows = (packed_rows - 8) // 2
    members = state_ref.shape[0]
    band = land_ref.shape[0]
    taken = band * members // sectors
    channels = rows // taken
    odd = place_ref[0] // sectors % 2
    fields = ((state_hbm, state_ref), (cotangent_hbm, cotangent_ref))
    parts = [(source.at[m], target.at[m]) for source, target in fields for m in range(members)]
    parts += [(land_hbm, land_ref), (orography_hbm, orography_ref)]
    moves = [
        pltpu.make_async_copy(source, target, sems.at[i])
        for i, (source, target) in enumerate(parts)
    ]
    for move in moves:
        move.start()
    leaving = []
    for n in range(2 * members):
        i, m = n // members, n % members
        moves[n].wait()
        if n == members:
            moves[-2].wait()
            moves[-1].wait()
            code = (jnp.where(land_ref[...] == 1, classes, 0) + orography_ref[...]).astype(F32)
        for pair in range(2):
            q = 2 * m + (pair + odd) % 2
            first = pair * taken
            for k in range(taken):
                start = i * rows + k * channels
                out_ref[q, start : start + channels, :] = fields[i][1][
                    m, pl.ds(first + k, channels, stride=band), :
                ]
            if i == 1:
                spare = jnp.zeros((8 - taken, LANES), F32)
                out_ref[q, 2 * rows :, :] = jnp.concatenate(
                    [code[first : first + taken], spare], axis=0
                )
        part = (pl.ds(2 * m, 2), pl.ds(i * rows, rows if i == 0 else rows + 8))
        leaving.append(
            pltpu.make_async_copy(out_ref.at[part], out_hbm.at[part], sems.at[len(parts) + n])
        )
        leaving[n].start()
    for move in leaving:
        move.wait()


def own_scale(place, scale_ref, taken, sectors, rows):
    band, _, pair = position(place, sectors)
    first = (2 * band + pair) * taken
    channels = rows // taken
    wide = (channels, scale_ref.shape[1])
    return jnp.concatenate(
        [jnp.broadcast_to(scale_ref[pl.ds(first + k, 1), :], wide) for k in range(taken)], axis=0
    )


def rolled(value, shift):
    return pltpu.roll(value, shift % value.shape[1], 1) if shift else value


def early_kernel(
    place_ref,
    seeds_ref,
    row_ref,
    scale_ref,
    high_ref,
    low_ref,
    land_ref,
    relief_ref,
    seed_ref,
    w_hidden_ref,
    b_hidden_ref,
    w_tendency_ref,
    moist_grad_ref,
    features_ref,
    preact_ref,
    hidden_grad_ref,
):
    taken = features_ref.shape[0]
    sectors = row_ref.shape[0]
    hidden_units, channels = w_tendency_ref.shape
    rows = taken * channels
    lon_total = features_ref.shape[2]
    classes = relief_ref.shape[0]
    place = place_ref[0]
    scale = own_scale(place, scale_ref, taken, sectors, rows)
    moist_grad = filtered(joined(row_ref, rows, rows), scale, high_ref[...], low_ref[...])
    moist_grad_ref[...] = moist_grad
    rounded = joined(row_ref, 0, rows).astype(BF).astype(F32)
    for j in range(-1, taken + 1):
        for b in range(3):
            if 0 <= j < taken:
                moved = rolled(rounded[j * channels : (j + 1) * channels], 1 - b).astype(BF)
            else:
                moved = jnp.zeros((channels, lon_total), BF)
            for a in range(3):
                if 0 <= j + 1 - a < taken:
                    start = (3 * a + b) * channels
                    features_ref[j + 1 - a, start : start + channels, :] = moved
    class_ids = lax.broadcasted_iota(jnp.int32, (2 * classes, lon_total), 0).astype(F32)
    codes = joined(row_ref, 2 * rows, 8)
    surface = jnp.concatenate(
        [land_ref[0:1, :] + relief_ref[...], land_ref[1:2, :] + relief_ref[...]], axis=0
    )
    seed = seeds_ref[place % sectors // 2]
    table = (surface + seed_ref[pl.ds(seed, 1), :]).astype(BF)
    bias = jnp.transpose(jnp.broadcast_to(b_hidden_ref[...], (8, hidden_units)))[:, 0:1]
    for k in range(taken):
        pick = jnp.where(class_ids == codes[k : k + 1], 1.0, 0.0).astype(BF)
        features_ref[k, 9 * channels :, :] = dot(table, pick, ((0,), (0,))).astype(BF)
        preact_ref[k] = dot(w_hidden_ref[...], features_ref[k]) + bias
        tendency_grad = moist_grad[k * channels : (k + 1) * channels].astype(BF)
        hidden_grad_ref[k] = dot(w_tendency_ref[...], tendency_grad)


def weights_kernel(
    place_ref,
    across_ref,
    inside_ref,
    row_ref,
    moist_grad_ref,
    early_ref,
    preact_ref,
    hidden_grad_ref,
    w_hidden_ref,
    w_tendency_ref,
    preact_grad_ref,
    moist_ref,
    own_ref,
    other_ref,
    features_ref,
    flat_ref,
):
    taken, in_channels, lon_total = features_ref.shape
    channels, hidden_units = w_tendency_ref.shape
    group = 3 * channels
    state = joined(row_ref, 0, taken * channels)
    grad_in = jnp.zeros((hidden_units, in_channels), F32)
    grad_out = jnp.zeros((channels, hidden_units), F32)
    grad_bias = jnp.zeros((16, hidden_units), F32)
    ones = jnp.ones((16, lon_total), BF)
    northern = position(place_ref[0], row_ref.shape[0])[2] == 0
    across = joined(across_ref, 0, channels).astype(F32)
    inside = joined(inside_ref, 0, channels).astype(F32)
    edges = (
        (jnp.where(northern, across, inside), 0, 0),
        (jnp.where(northern, inside, across), 2, taken - 1),
    )
    for k in range(taken):
        part = slice(k * channels, (k + 1) * channels)
        features_ref[k] = early_ref[k]
        preact = preact_ref[k]
        for edge, a, row in edges:
            if row == k:
                halo = jnp.concatenate([rolled(edge, 1 - b).astype(BF) for b in range(3)], axis=0)
                features_ref[k, a * group : (a + 1) * group, :] = halo
                preact = preact + dot(w_hidden_ref[:, a * group : (a + 1) * group], halo)
        logistic = 0.5 + 0.5 * jnp.tanh(0.5 * preact)
        hidden = (preact * logistic).astype(BF)
        slope = logistic * (1.0 + preact * (1.0 - logistic))
        preact_grad = (hidden_grad_ref[k] * slope).astype(BF)
        tendency_grad = moist_grad_ref[part, :].astype(BF)
        grad_out += dot(tendency_grad, hidden, ((1,), (1,)))
        grad_in += dot(preact_grad, features_ref[k], ((1,), (1,)))
        grad_bias += dot(ones, preact_grad, ((1,), (1,)))
        moist_ref[part, :] = state[part] + dot(w_tendency_ref[...], hidden)
        preact_grad_ref[k] = preact_grad

    bias_high = grad_bias[0:1].astype(BF).astype(F32)
    bias_low = grad_bias[0:1] - bias_high
    tiles = hidden_units // LANES
    pieces = own_ref.shape[0]
    base, rest = split_rows(flat_ref.shape[1], pieces)
    for h in range(2):
        start = 0
        for value in (grad_in, grad_out):
            count = value.shape[0] // 2
            for t in range(value.shape[1] // LANES):
                flat_ref[h, start : start + count, :] = value[
                    h * count : (h + 1) * count, t * LANES : (t + 1) * LANES
                ]
                start += count
    core = position(place_ref[0], row_ref.shape[0])[0] % 2
    for p in range(pieces):
        start = pieces * base + p * rest
        ends = [jnp.zeros((tiles, LANES), F32)]
        if p < 2:
            half = (bias_high, bias_low)[p]
            ends = [half[:, t * LANES : (t + 1) * LANES] for t in range(tiles)]
        for ref, h in ((own_ref, core), (other_ref, 1 - core)):
            last = [flat_ref[h, start : start + rest, :]] if rest else []
            piece = [flat_ref[h, p * base : (p + 1) * base, :]] + last + ends
            ref[p] = jnp.concatenate(piece, axis=0).astype(ref.dtype)


def stencil_kernel(
    place_ref,
    preact_grad_ref,
    moist_grad_ref,
    w_stencil_ref,
    to_across_ref,
    to_inside_ref,
    grad_ref,
):
    taken = preact_grad_ref.shape[0]
    sectors, channels = to_across_ref.shape[:2]
    northern = position(place_ref[0], sectors)[2] == 0
    sums = []
    for k in range(taken):
        stencil_grad = dot(w_stencil_ref[...], preact_grad_ref[k])
        sums.append([])
        for a in range(3):
            total = None
            for b in range(3):
                start = (3 * a + b) * channels
                piece = rolled(stencil_grad[start : start + channels], b - 1)
                total = piece if total is None else total + piece
            sums[k].append(total)
    to_north, to_south = sums[0][0], sums[-1][2]
    store_split(to_across_ref, 0, jnp.where(northern, to_north, to_south))
    store_split(to_inside_ref, 0, jnp.where(northern, to_south, to_north))
    for k in range(taken):
        total = moist_grad_ref[k * channels : (k + 1) * channels, :] + sums[k][1]
        if k > 0:
            total = total + sums[k - 1][2]
        if k + 1 < taken:
            total = total + sums[k + 1][0]
        store_split(grad_ref, k * channels, total)


def fields_kernel(
    place_ref, moist_ref, scale_ref, high_ref, low_ref, grad_ref, across_ref, inside_ref, *refs
):
    sends, blocks_ref = refs[:-1], refs[-1]
    sectors, rows = grad_ref.shape[:2]
    channels = across_ref.shape[1]
    place = place_ref[0]
    _, q, pair = position(place, sectors)
    scale = own_scale(place, scale_ref, rows // channels, sectors, rows)
    store_split(blocks_ref, 0, filtered(moist_ref[...], scale, high_ref[...], low_ref[...]))
    for s in range(sectors):
        part = grad_ref[s]
        across, inside = across_ref[s].astype(F32), inside_ref[s].astype(F32)
        first = part[:channels] + jnp.where(pair == 0, across, inside)
        last = part[rows - channels :] + jnp.where(pair == 0, inside, across)
        inner = [part[channels : rows - channels]] if rows > 2 * channels else []
        blocks_ref[s, rows:, :] = jnp.concatenate([first] + inner + [last], axis=0).astype(BF)
    for t in range(sectors):
        sends[t][...] = blocks_ref[q ^ t]


def by_band_kernel(place_ref, *refs, band):
    blocks_ref = refs[-1]
    outs = refs[-3:-1]
    sectors, rows = blocks_ref.shape[0], blocks_ref.shape[1] // 2
    members = outs[0].shape[0]
    taken = band * members // sectors
    channels = rows // taken
    band_index, q, _ = position(place_ref[0], sectors)
    for t in range(sectors):
        blocks_ref[t] = refs[t][...].astype(F32)
    for m in range(members):
        for pair in range(2):
            t = q ^ (2 * m + (pair + band_index) % 2)
            for i in range(2):
                for k in range(taken):
                    start = i * rows + k * channels
                    outs[i][m, pl.ds(pair * taken + k, channels, stride=band), :] = blocks_ref[
                        t, start : start + channels, :
                    ]


def sum_and_copy_kernel(parts_ref, *refs):
    copies_ref = refs[-1]
    total = parts_ref[0].astype(F32)
    for p in range(1, parts_ref.shape[0]):
        total = total + parts_ref[p].astype(F32)
    total = total.astype(BF)
    for p in range(copies_ref.shape[0]):
        copies_ref[p] = total


def unpack_kernel(
    place_ref, own_ref, other_ref, grad_in_ref, grad_bias_ref, grad_out_ref, flat_ref,
    *, scaling, sectors
):
    pieces = own_ref.shape[0]
    base, rest = split_rows(flat_ref.shape[1], pieces)
    core = position(place_ref[0], sectors)[0] % 2
    bias = None
    for ref, h in ((own_ref, core), (other_ref, 1 - core)):
        for p in range(pieces):
            piece = ref[p].astype(F32) * scaling
            flat_ref[h, p * base : (p + 1) * base, :] = piece[:base]
            start = pieces * base + p * rest
            flat_ref[h, start : start + rest, :] = piece[base : base + rest]
            if ref is own_ref and p < 2:
                half = piece[base + rest :]
                bias = half if bias is None else bias + half
    for t in range(grad_bias_ref.shape[0] // LANES):
        grad_bias_ref[t * LANES : (t + 1) * LANES] = bias[t]
    for h in range(2):
        start = 0
        for ref in (grad_in_ref, grad_out_ref):
            count = ref.shape[0] // 2
            for t in range(ref.shape[1] // LANES):
                ref[h * count : (h + 1) * count, t * LANES : (t + 1) * LANES] = flat_ref[
                    h, start : start + count, :
                ]
                start += count


def call(kernel, outs, inputs, smem=0, scratch=(), flops=0, vmem=8, inputs_in=pltpu.VMEM, outs_in=pltpu.VMEM, **static):
    on_output = pl.BlockSpec(memory_space=outs_in)
    on_input = pl.BlockSpec(memory_space=inputs_in)
    on_smem = pl.BlockSpec(memory_space=pltpu.SMEM)

    def body(*refs):
        kernel(*refs, **static)

    return pl.pallas_call(
        body,
        out_shape=outs,
        in_specs=[on_smem] * smem + [on_input] * (inputs - smem),
        out_specs=jax.tree.map(lambda _: on_output, outs),
        scratch_shapes=list(scratch),
        cost_estimate=pl.CostEstimate(flops=flops, bytes_accessed=1_000_000, transcendentals=0),
        compiler_params=pltpu.CompilerParams(vmem_limit_bytes=vmem * MIB),
    )


def copy_kernel(x_ref, *refs):
    refs[-1][...] = x_ref[...]


def exchange(x, axes):
    return lax.all_to_all(x, axes, 0, 0, tiled=True)


def on_device(
    column_state,
    cotangent,
    land_mask,
    orography,
    member_seeds,
    land_table,
    relief_table,
    seed_table,
    w_hidden,
    b_hidden,
    w_tendency,
):
    members, channels, band, lon_cols = column_state.shape
    hidden_units, in_channels = w_hidden.shape
    classes = relief_table.shape[0]
    sectors = lax.axis_size("lon")
    peers = lax.axis_size(PLACE)
    lat_total = band * (peers // sectors)
    lon_total = lon_cols * sectors
    taken = band * members // sectors
    rows = taken * channels
    assert 2 * taken == band and 2 * members == sectors
    shape = jax.ShapeDtypeStruct
    place = lax.axis_index(PLACE)
    band_index, _, pair = position(place, sectors)
    place = place.reshape(1)

    with jax.named_scope("rows_in"):
        flat = (members, channels * band, lon_cols)
        packed_shape = (sectors, 2 * rows + 8, lon_cols)
        packed = call(
            by_row_kernel,
            shape(packed_shape, F32),
            5,
            smem=1,
            scratch=[
                pltpu.VMEM(flat, F32),
                pltpu.VMEM(flat, F32),
                pltpu.VMEM(land_mask.shape, land_mask.dtype),
                pltpu.VMEM(orography.shape, orography.dtype),
                pltpu.VMEM(packed_shape, F32),
                pltpu.SemaphoreType.DMA((4 * members + 2,)),
            ],
            vmem=56,
            inputs_in=pltpu.HBM,
            outs_in=pltpu.HBM,
            classes=classes,
        )(place, column_state.reshape(flat), cotangent.reshape(flat), land_mask, orography)
        row = exchange(packed, "lon")

    with jax.named_scope("row_halo"):
        inside_swaps, across_swaps = [], []
        for i in range(peers):
            _, q, southern = position(i, sectors)
            inside_swaps.append((i, i - q + (q ^ 1)))
            j = i + sectors if southern else i - sectors
            if 0 <= j < peers:
                across_swaps.append((i, j))

        def edge_row(southern):
            start = southern * (rows - channels)
            return lax.dynamic_slice_in_dim(row, start, channels, 1).astype(BF)

        inside = lax.ppermute(edge_row(1 - pair), PLACE, inside_swaps)
        across = lax.ppermute(edge_row(pair), PLACE, across_swaps)

    high, low, scale = [jnp.asarray(t) for t in filter_tables(lat_total, lon_total)]
    per_hidden = shape((taken, hidden_units, lon_total), F32)
    features_shape = (taken, in_channels, lon_total)
    with jax.named_scope("early"):
        moist_grad, features, preact, hidden_grad = call(
            early_kernel,
            (shape((rows, lon_total), F32), shape(features_shape, BF), per_hidden, per_hidden),
            12,
            smem=2,
            flops=3_000_000_000,
            vmem=24,
        )(
            place,
            member_seeds,
            row,
            scale,
            high,
            low,
            land_table,
            relief_table,
            seed_table,
            w_hidden,
            b_hidden.reshape(1, hidden_units),
            w_tendency.T,
        )

    pieces = lax.axis_size(PLANE)
    length = lax.axis_size("z")
    half_rows = (hidden_units * in_channels + channels * hidden_units) // (2 * LANES)
    piece_rows = half_rows // pieces + hidden_units // LANES
    share = (pieces, piece_rows, LANES)
    flat_rows = pltpu.VMEM((2, half_rows, LANES), F32)
    with jax.named_scope("weights"):
        block = (sectors, rows, LANES)
        edge = (sectors, channels, LANES)
        preact_grad, moist, own, other = call(
            weights_kernel,
            (
                shape((taken, hidden_units, lon_total), BF),
                shape((rows, lon_total), F32),
                shape(share, F32),
                shape(share, BF),
            ),
            10,
            smem=1,
            scratch=[pltpu.VMEM(features_shape, BF), flat_rows],
            flops=3_000_000_000,
            vmem=24,
        )(
            place,
            across,
            inside,
            row,
            moist_grad,
            features,
            preact,
            hidden_grad,
            w_hidden,
            w_tendency,
        )

    with jax.named_scope("stencil"):
        to_across, to_inside, grad_rows = call(
            stencil_kernel,
            (shape(edge, BF), shape(edge, BF), shape(block, F32)),
            4,
            smem=1,
            flops=1_000_000_000,
        )(place, preact_grad, moist_grad, w_hidden[:, : 9 * channels].T)

    with jax.named_scope("weights_core"):
        swap = [(0, 1), (1, 0)]
        halves = (own + lax.ppermute(other, "core", swap).astype(F32)).astype(BF)

    with jax.named_scope("fields"):
        from_across = lax.ppermute(to_across, PLACE, across_swaps)
        from_inside = lax.ppermute(to_inside, PLACE, inside_swaps)
        fields = call(
            fields_kernel,
            (shape((2 * rows, LANES), BF),) * sectors,
            8,
            smem=1,
            scratch=[pltpu.VMEM((sectors, 2 * rows, LANES), BF)],
            flops=1_000_000_000,
        )(place, moist, scale, high, low, grad_rows, from_across, from_inside)

    with jax.named_scope("weights_plane"):
        copies = call(sum_and_copy_kernel, shape((length, piece_rows, LANES), BF), 2)(
            exchange(halves, PLANE), from_across
        )

    with jax.named_scope("rows_out"):
        received = [fields[0]]
        for t in range(1, sectors):
            received.append(lax.ppermute(fields[t], "lon", [(i, i ^ t) for i in range(sectors)]))

    with jax.named_scope("weights_length"):
        copies = call(sum_and_copy_kernel, shape(share, BF), 2)(
            exchange(copies, "z"), fields[0]
        )

    with jax.named_scope("bands_out"):
        next_state, state_grad = call(
            by_band_kernel,
            (shape(flat, F32), shape(flat, F32)),
            1 + sectors,
            smem=1,
            scratch=[pltpu.VMEM((sectors, 2 * rows, LANES), F32)],
            band=band,
        )(place, *received)
        next_state = next_state.reshape(column_state.shape)
        state_grad = state_grad.reshape(column_state.shape)

    with jax.named_scope("weights_back"):
        own = call(copy_kernel, shape(share, BF), sectors)(exchange(copies, PLANE), *received[1:])
        other = lax.ppermute(own, "core", swap)
        columns = members * lax.axis_size("mem") * lat_total * lon_total
        grad_in, grad_bias, grad_out = call(
            unpack_kernel,
            (
                shape((hidden_units, in_channels), F32),
                shape((hidden_units,), F32),
                shape((channels, hidden_units), F32),
            ),
            3,
            smem=1,
            scratch=[flat_rows],
            scaling=1.0 / math.sqrt(columns),
            sectors=sectors,
        )(place, own, other)
    return next_state, state_grad, grad_in, grad_bias, grad_out


def solution(mesh):
    lat, lon, mem = mesh.devices.shape
    devices = mesh.devices.reshape(2, lat // 4, 2, lon, mem)
    split = Mesh(devices, ("ylo", "z", "core", "lon", "mem"))
    lat_axes = ("ylo", "z", "core")
    field = P("mem", None, lat_axes, "lon")
    surface = P(lat_axes, "lon")
    whole = P()
    return jax.shard_map(
        on_device,
        mesh=split,
        in_specs=(field, field, surface, surface, P("mem")) + (whole,) * 6,
        out_specs=(field, field, whole, whole, whole),
        check_vma=False,
    )
```

```python
import math

import jax
import jax.numpy as jnp
import numpy as np
from jax import lax
from jax.experimental import pallas as pl
from jax.experimental.pallas import tpu as pltpu
from jax.sharding import Mesh, PartitionSpec as P

MODES = 171
DAMP = 2.0
LANES = 128
BF = jnp.bfloat16
F32 = jnp.float32
MIB = 1024 * 1024
PLACE = ("ylo", "z", "core", "lon")
PLANE = ("mem", "ylo", "lon")


def whole_multiple(value, unit):
    return -(-value // unit) * unit


def filter_tables(lat_total, lon_total):
    padded = whole_multiple(2 * MODES, LANES)
    k = np.arange(MODES)
    angles = (k[:, None] * np.arange(lon_total)[None]) % lon_total * (2.0 * math.pi / lon_total)
    analysis = np.zeros((padded, lon_total))
    analysis[: 2 * MODES] = np.concatenate([np.cos(angles), np.sin(angles)], 0)
    lat = math.pi * ((np.arange(lat_total) + 0.5) / lat_total - 0.5)
    removal = 1.0 - np.exp(-DAMP * (k[None] / MODES) ** 2 / np.cos(lat)[:, None] ** 2)
    removal = removal * np.where(k == 0, 1.0, 2.0) / lon_total
    scale = np.zeros((lat_total, padded), np.float32)
    scale[:, : 2 * MODES] = np.concatenate([removal, removal], 1)
    high = analysis.astype(np.float32).astype(BF)
    low = (analysis - high.astype(np.float64)).astype(np.float32).astype(BF)
    return high, low, scale


def split_rows(total, pieces):
    each = total // pieces
    return each // 8 * 8, each % 8


def dot(a, b, dims=((1,), (0,))):
    return lax.dot_general(a, b, (dims, ((), ())), preferred_element_type=F32)


def split_dot(x, high, low, dims=((1,), (0,))):
    x_high = x.astype(BF)
    x_low = (x - x_high.astype(F32)).astype(BF)
    both = dot(jnp.concatenate([x_high, x_low], axis=0), high, dims)
    count = x.shape[0]
    return both[:count] + (both[count:] + dot(x_high, low, dims))


def filtered(x, scale, high, low):
    coeffs = split_dot(x, high, low, ((1,), (1,))) * scale
    return x - split_dot(coeffs, high, low)


def joined(ref, start, rows):
    return jnp.concatenate([ref[s, start : start + rows, :] for s in range(ref.shape[0])], axis=1)


def store_split(ref, start, value):
    for s in range(ref.shape[0]):
        ref[s, start : start + value.shape[0], :] = value[:, s * LANES : (s + 1) * LANES].astype(
            ref.dtype
        )


def position(place, sectors):
    band, q = place // sectors, place % sectors
    return band, q, (q + band) % 2


def by_row_kernel(
    place_ref, state_hbm, cotangent_hbm, land_hbm, orography_hbm, out_hbm,
    state_ref, cotangent_ref, land_ref, orography_ref, out_ref, sems, *, classes
):
    sectors, packed_rows = out_ref.shape[:2]
    rows = (packed_rows - 8) // 2
    members = state_ref.shape[0]
    band = land_ref.shape[0]
    taken = band * members // sectors
    channels = rows // taken
    odd = place_ref[0] // sectors % 2
    fields = ((state_hbm, state_ref), (cotangent_hbm, cotangent_ref))
    parts = [(source.at[m], target.at[m]) for source, target in fields for m in range(members)]
    parts += [(land_hbm, land_ref), (orography_hbm, orography_ref)]
    moves = [
        pltpu.make_async_copy(source, target, sems.at[i])
        for i, (source, target) in enumerate(parts)
    ]
    for move in moves:
        move.start()
    leaving = []
    for n in range(2 * members):
        i, m = n // members, n % members
        moves[n].wait()
        if n == members:
            moves[-2].wait()
            moves[-1].wait()
            code = (jnp.where(land_ref[...] == 1, classes, 0) + orography_ref[...]).astype(F32)
        for pair in range(2):
            q = 2 * m + (pair + odd) % 2
            first = pair * taken
            for k in range(taken):
                start = i * rows + k * channels
                out_ref[q, start : start + channels, :] = fields[i][1][
                    m, pl.ds(first + k, channels, stride=band), :
                ]
            if i == 1:
                spare = jnp.zeros((8 - taken, LANES), F32)
                out_ref[q, 2 * rows :, :] = jnp.concatenate(
                    [code[first : first + taken], spare], axis=0
                )
        part = (pl.ds(2 * m, 2), pl.ds(i * rows, rows if i == 0 else rows + 8))
        leaving.append(
            pltpu.make_async_copy(out_ref.at[part], out_hbm.at[part], sems.at[len(parts) + n])
        )
        leaving[n].start()
    for move in leaving:
        move.wait()


def own_scale(place, scale_ref, taken, sectors, rows):
    band, _, pair = position(place, sectors)
    first = (2 * band + pair) * taken
    channels = rows // taken
    wide = (channels, scale_ref.shape[1])
    return jnp.concatenate(
        [jnp.broadcast_to(scale_ref[pl.ds(first + k, 1), :], wide) for k in range(taken)], axis=0
    )


def rolled(value, shift):
    return pltpu.roll(value, shift % value.shape[1], 1) if shift else value


def early_kernel(
    place_ref,
    seeds_ref,
    row_ref,
    scale_ref,
    high_ref,
    low_ref,
    land_ref,
    relief_ref,
    seed_ref,
    w_hidden_ref,
    b_hidden_ref,
    w_tendency_ref,
    moist_grad_ref,
    features_ref,
    preact_ref,
    hidden_grad_ref,
):
    taken = features_ref.shape[0]
    sectors = row_ref.shape[0]
    hidden_units, channels = w_tendency_ref.shape
    rows = taken * channels
    lon_total = features_ref.shape[2]
    classes = relief_ref.shape[0]
    place = place_ref[0]
    scale = own_scale(place, scale_ref, taken, sectors, rows)
    moist_grad = filtered(joined(row_ref, rows, rows), scale, high_ref[...], low_ref[...])
    moist_grad_ref[...] = moist_grad
    rounded = joined(row_ref, 0, rows).astype(BF).astype(F32)
    for j in range(-1, taken + 1):
        for b in range(3):
            if 0 <= j < taken:
                moved = rolled(rounded[j * channels : (j + 1) * channels], 1 - b).astype(BF)
            else:
                moved = jnp.zeros((channels, lon_total), BF)
            for a in range(3):
                if 0 <= j + 1 - a < taken:
                    start = (3 * a + b) * channels
                    features_ref[j + 1 - a, start : start + channels, :] = moved
    class_ids = lax.broadcasted_iota(jnp.int32, (2 * classes, lon_total), 0).astype(F32)
    codes = joined(row_ref, 2 * rows, 8)
    surface = jnp.concatenate(
        [land_ref[0:1, :] + relief_ref[...], land_ref[1:2, :] + relief_ref[...]], axis=0
    )
    seed = seeds_ref[place % sectors // 2]
    table = (surface + seed_ref[pl.ds(seed, 1), :]).astype(BF)
    bias = jnp.transpose(jnp.broadcast_to(b_hidden_ref[...], (8, hidden_units)))[:, 0:1]
    for k in range(taken):
        pick = jnp.where(class_ids == codes[k : k + 1], 1.0, 0.0).astype(BF)
        features_ref[k, 9 * channels :, :] = dot(table, pick, ((0,), (0,))).astype(BF)
        preact_ref[k] = dot(w_hidden_ref[...], features_ref[k]) + bias
        tendency_grad = moist_grad[k * channels : (k + 1) * channels].astype(BF)
        hidden_grad_ref[k] = dot(w_tendency_ref[...], tendency_grad)


def weights_kernel(
    place_ref,
    inside_ref,
    across_ref,
    row_ref,
    moist_grad_ref,
    early_ref,
    preact_ref,
    hidden_grad_ref,
    w_hidden_ref,
    w_tendency_ref,
    preact_grad_ref,
    moist_ref,
    own_ref,
    other_ref,
    features_ref,
    flat_ref,
):
    taken, in_channels, lon_total = features_ref.shape
    channels, hidden_units = w_tendency_ref.shape
    group = 3 * channels
    state = joined(row_ref, 0, taken * channels)
    grad_in = jnp.zeros((hidden_units, in_channels), F32)
    grad_out = jnp.zeros((channels, hidden_units), F32)
    grad_bias = jnp.zeros((16, hidden_units), F32)
    ones = jnp.ones((16, lon_total), BF)
    northern = position(place_ref[0], row_ref.shape[0])[2] == 0
    across = joined(across_ref, 0, channels).astype(F32)
    inside = joined(inside_ref, 0, channels).astype(F32)
    edges = (
        (jnp.where(northern, across, inside), 0, 0),
        (jnp.where(northern, inside, across), 2, taken - 1),
    )
    for k in range(taken):
        part = slice(k * channels, (k + 1) * channels)
        features_ref[k] = early_ref[k]
        preact = preact_ref[k]
        for edge, a, row in edges:
            if row == k:
                halo = jnp.concatenate([rolled(edge, 1 - b).astype(BF) for b in range(3)], axis=0)
                features_ref[k, a * group : (a + 1) * group, :] = halo
                preact = preact + dot(w_hidden_ref[:, a * group : (a + 1) * group], halo)
        logistic = 0.5 + 0.5 * jnp.tanh(0.5 * preact)
        hidden = (preact * logistic).astype(BF)
        slope = logistic * (1.0 + preact * (1.0 - logistic))
        preact_grad = (hidden_grad_ref[k] * slope).astype(BF)
        tendency_grad = moist_grad_ref[part, :].astype(BF)
        grad_out += dot(tendency_grad, hidden, ((1,), (1,)))
        grad_in += dot(preact_grad, features_ref[k], ((1,), (1,)))
        grad_bias += dot(ones, preact_grad, ((1,), (1,)))
        moist_ref[part, :] = state[part] + dot(w_tendency_ref[...], hidden)
        preact_grad_ref[k] = preact_grad

    bias_high = grad_bias[0:1].astype(BF).astype(F32)
    bias_low = grad_bias[0:1] - bias_high
    tiles = hidden_units // LANES
    pieces = own_ref.shape[0]
    base, rest = split_rows(flat_ref.shape[1], pieces)
    for h in range(2):
        start = 0
        for value in (grad_in, grad_out):
            count = value.shape[0] // 2
            for t in range(value.shape[1] // LANES):
                flat_ref[h, start : start + count, :] = value[
                    h * count : (h + 1) * count, t * LANES : (t + 1) * LANES
                ]
                start += count
    core = position(place_ref[0], row_ref.shape[0])[0] % 2
    for p in range(pieces):
        start = pieces * base + p * rest
        ends = [jnp.zeros((tiles, LANES), F32)]
        if p < 2:
            half = (bias_high, bias_low)[p]
            ends = [half[:, t * LANES : (t + 1) * LANES] for t in range(tiles)]
        for ref, h in ((own_ref, core), (other_ref, 1 - core)):
            last = [flat_ref[h, start : start + rest, :]] if rest else []
            piece = [flat_ref[h, p * base : (p + 1) * base, :]] + last + ends
            ref[p] = jnp.concatenate(piece, axis=0).astype(ref.dtype)


def stencil_kernel(
    place_ref,
    preact_grad_ref,
    moist_grad_ref,
    w_stencil_ref,
    to_across_ref,
    to_inside_ref,
    grad_ref,
):
    taken = preact_grad_ref.shape[0]
    sectors, channels = to_across_ref.shape[:2]
    northern = position(place_ref[0], sectors)[2] == 0
    sums = []
    for k in range(taken):
        stencil_grad = dot(w_stencil_ref[...], preact_grad_ref[k])
        sums.append([])
        for a in range(3):
            total = None
            for b in range(3):
                start = (3 * a + b) * channels
                piece = rolled(stencil_grad[start : start + channels], b - 1)
                total = piece if total is None else total + piece
            sums[k].append(total)
    to_north, to_south = sums[0][0], sums[-1][2]
    store_split(to_across_ref, 0, jnp.where(northern, to_north, to_south))
    store_split(to_inside_ref, 0, jnp.where(northern, to_south, to_north))
    for k in range(taken):
        total = moist_grad_ref[k * channels : (k + 1) * channels, :] + sums[k][1]
        if k > 0:
            total = total + sums[k - 1][2]
        if k + 1 < taken:
            total = total + sums[k + 1][0]
        store_split(grad_ref, k * channels, total)


def fields_kernel(
    place_ref, moist_ref, scale_ref, high_ref, low_ref, grad_ref, across_ref, inside_ref, *refs
):
    sends, blocks_ref = refs[:-1], refs[-1]
    sectors, rows = grad_ref.shape[:2]
    channels = across_ref.shape[1]
    place = place_ref[0]
    _, q, pair = position(place, sectors)
    scale = own_scale(place, scale_ref, rows // channels, sectors, rows)
    store_split(blocks_ref, 0, filtered(moist_ref[...], scale, high_ref[...], low_ref[...]))
    for s in range(sectors):
        part = grad_ref[s]
        across, inside = across_ref[s].astype(F32), inside_ref[s].astype(F32)
        first = part[:channels] + jnp.where(pair == 0, across, inside)
        last = part[rows - channels :] + jnp.where(pair == 0, inside, across)
        inner = [part[channels : rows - channels]] if rows > 2 * channels else []
        blocks_ref[s, rows:, :] = jnp.concatenate([first] + inner + [last], axis=0).astype(BF)
    for t in range(sectors):
        sends[t][...] = blocks_ref[q ^ t]


def by_band_kernel(place_ref, *refs, band):
    blocks_ref = refs[-1]
    outs = refs[-3:-1]
    sectors, rows = blocks_ref.shape[0], blocks_ref.shape[1] // 2
    members = outs[0].shape[0]
    taken = band * members // sectors
    channels = rows // taken
    band_index, q, _ = position(place_ref[0], sectors)
    for t in range(sectors):
        blocks_ref[t] = refs[t][...].astype(F32)
    for m in range(members):
        for pair in range(2):
            t = q ^ (2 * m + (pair + band_index) % 2)
            for i in range(2):
                for k in range(taken):
                    start = i * rows + k * channels
                    outs[i][m, pl.ds(pair * taken + k, channels, stride=band), :] = blocks_ref[
                        t, start : start + channels, :
                    ]


def sum_and_copy_kernel(parts_ref, *refs):
    copies_ref = refs[-1]
    total = parts_ref[0].astype(F32)
    for p in range(1, parts_ref.shape[0]):
        total = total + parts_ref[p].astype(F32)
    total = total.astype(BF)
    for p in range(copies_ref.shape[0]):
        copies_ref[p] = total


def unpack_kernel(
    place_ref, own_ref, other_ref, grad_in_ref, grad_bias_ref, grad_out_ref, flat_ref,
    *, scaling, sectors
):
    pieces = own_ref.shape[0]
    base, rest = split_rows(flat_ref.shape[1], pieces)
    core = position(place_ref[0], sectors)[0] % 2
    bias = None
    for ref, h in ((own_ref, core), (other_ref, 1 - core)):
        for p in range(pieces):
            piece = ref[p].astype(F32) * scaling
            flat_ref[h, p * base : (p + 1) * base, :] = piece[:base]
            start = pieces * base + p * rest
            flat_ref[h, start : start + rest, :] = piece[base : base + rest]
            if ref is own_ref and p < 2:
                half = piece[base + rest :]
                bias = half if bias is None else bias + half
    for t in range(grad_bias_ref.shape[0] // LANES):
        grad_bias_ref[t * LANES : (t + 1) * LANES] = bias[t]
    for h in range(2):
        start = 0
        for ref in (grad_in_ref, grad_out_ref):
            count = ref.shape[0] // 2
            for t in range(ref.shape[1] // LANES):
                ref[h * count : (h + 1) * count, t * LANES : (t + 1) * LANES] = flat_ref[
                    h, start : start + count, :
                ]
                start += count


def call(kernel, outs, inputs, smem=0, scratch=(), flops=0, vmem=8, inputs_in=pltpu.VMEM, outs_in=pltpu.VMEM, **static):
    on_output = pl.BlockSpec(memory_space=outs_in)
    on_input = pl.BlockSpec(memory_space=inputs_in)
    on_smem = pl.BlockSpec(memory_space=pltpu.SMEM)

    def body(*refs):
        kernel(*refs, **static)

    return pl.pallas_call(
        body,
        out_shape=outs,
        in_specs=[on_smem] * smem + [on_input] * (inputs - smem),
        out_specs=jax.tree.map(lambda _: on_output, outs),
        scratch_shapes=list(scratch),
        cost_estimate=pl.CostEstimate(flops=flops, bytes_accessed=1_000_000, transcendentals=0),
        compiler_params=pltpu.CompilerParams(vmem_limit_bytes=vmem * MIB),
    )


def copy_kernel(x_ref, *refs):
    refs[-1][...] = x_ref[...]


def exchange(x, axes):
    return lax.all_to_all(x, axes, 0, 0, tiled=True)


def on_device(
    column_state,
    cotangent,
    land_mask,
    orography,
    member_seeds,
    land_table,
    relief_table,
    seed_table,
    w_hidden,
    b_hidden,
    w_tendency,
):
    members, channels, band, lon_cols = column_state.shape
    hidden_units, in_channels = w_hidden.shape
    classes = relief_table.shape[0]
    sectors = lax.axis_size("lon")
    peers = lax.axis_size(PLACE)
    lat_total = band * (peers // sectors)
    lon_total = lon_cols * sectors
    taken = band * members // sectors
    rows = taken * channels
    assert 2 * taken == band and 2 * members == sectors
    shape = jax.ShapeDtypeStruct
    place = lax.axis_index(PLACE)
    band_index, _, pair = position(place, sectors)
    place = place.reshape(1)

    with jax.named_scope("rows_in"):
        flat = (members, channels * band, lon_cols)
        packed_shape = (sectors, 2 * rows + 8, lon_cols)
        packed = call(
            by_row_kernel,
            shape(packed_shape, F32),
            5,
            smem=1,
            scratch=[
                pltpu.VMEM(flat, F32),
                pltpu.VMEM(flat, F32),
                pltpu.VMEM(land_mask.shape, land_mask.dtype),
                pltpu.VMEM(orography.shape, orography.dtype),
                pltpu.VMEM(packed_shape, F32),
                pltpu.SemaphoreType.DMA((4 * members + 2,)),
            ],
            vmem=56,
            inputs_in=pltpu.HBM,
            outs_in=pltpu.HBM,
            classes=classes,
        )(place, column_state.reshape(flat), cotangent.reshape(flat), land_mask, orography)
        row = exchange(packed, "lon")

    with jax.named_scope("row_halo"):
        inside_swaps, across_swaps = [], []
        for i in range(peers):
            _, q, southern = position(i, sectors)
            inside_swaps.append((i, i - q + (q ^ 1)))
            j = i + sectors if southern else i - sectors
            if 0 <= j < peers:
                across_swaps.append((i, j))

        def edge_row(southern):
            start = southern * (rows - channels)
            return lax.dynamic_slice_in_dim(row, start, channels, 1).astype(BF)

        inside = lax.ppermute(edge_row(1 - pair), PLACE, inside_swaps)
        across = lax.ppermute(edge_row(pair), PLACE, across_swaps)

    high, low, scale = [jnp.asarray(t) for t in filter_tables(lat_total, lon_total)]
    per_hidden = shape((taken, hidden_units, lon_total), F32)
    features_shape = (taken, in_channels, lon_total)
    with jax.named_scope("early"):
        moist_grad, features, preact, hidden_grad = call(
            early_kernel,
            (shape((rows, lon_total), F32), shape(features_shape, BF), per_hidden, per_hidden),
            12,
            smem=2,
            flops=3_000_000_000,
            vmem=16,
        )(
            place,
            member_seeds,
            row,
            scale,
            high,
            low,
            land_table,
            relief_table,
            seed_table,
            w_hidden,
            b_hidden.reshape(1, hidden_units),
            w_tendency.T,
        )

    pieces = lax.axis_size(PLANE)
    length = lax.axis_size("z")
    half_rows = (hidden_units * in_channels + channels * hidden_units) // (2 * LANES)
    piece_rows = half_rows // pieces + hidden_units // LANES
    share = (pieces, piece_rows, LANES)
    flat_rows = pltpu.VMEM((2, half_rows, LANES), F32)
    with jax.named_scope("weights"):
        block = (sectors, rows, LANES)
        edge = (sectors, channels, LANES)
        preact_grad, moist, own, other = call(
            weights_kernel,
            (
                shape((taken, hidden_units, lon_total), BF),
                shape((rows, lon_total), F32),
                shape(share, F32),
                shape(share, BF),
            ),
            10,
            smem=1,
            scratch=[pltpu.VMEM(features_shape, BF), flat_rows],
            flops=3_000_000_000,
            vmem=16,
        )(
            place,
            inside,
            across,
            row,
            moist_grad,
            features,
            preact,
            hidden_grad,
            w_hidden,
            w_tendency,
        )

    with jax.named_scope("stencil"):
        to_across, to_inside, grad_rows = call(
            stencil_kernel,
            (shape(edge, BF), shape(edge, BF), shape(block, F32)),
            4,
            smem=1,
            flops=1_000_000_000,
        )(place, preact_grad, moist_grad, w_hidden[:, : 9 * channels].T)

    with jax.named_scope("weights_core"):
        swap = [(0, 1), (1, 0)]
        halves = (own + lax.ppermute(other, "core", swap).astype(F32)).astype(BF)

    with jax.named_scope("fields"):
        from_across = lax.ppermute(to_across, PLACE, across_swaps)
        from_inside = lax.ppermute(to_inside, PLACE, inside_swaps)
        fields = call(
            fields_kernel,
            (shape((2 * rows, LANES), BF),) * sectors,
            8,
            smem=1,
            scratch=[pltpu.VMEM((sectors, 2 * rows, LANES), BF)],
            flops=1_000_000_000,
        )(place, moist, scale, high, low, grad_rows, from_across, from_inside)

    with jax.named_scope("weights_plane"):
        copies = call(sum_and_copy_kernel, shape((length, piece_rows, LANES), BF), 2)(
            exchange(halves, PLANE), from_across
        )

    with jax.named_scope("rows_out"):
        received = [fields[0]]
        for t in range(1, sectors):
            received.append(lax.ppermute(fields[t], "lon", [(i, i ^ t) for i in range(sectors)]))

    with jax.named_scope("weights_length"):
        copies = call(sum_and_copy_kernel, shape(share, BF), 2)(
            exchange(copies, "z"), fields[0]
        )

    with jax.named_scope("bands_out"):
        next_state, state_grad = call(
            by_band_kernel,
            (shape(flat, F32), shape(flat, F32)),
            1 + sectors,
            smem=1,
            scratch=[pltpu.VMEM((sectors, 2 * rows, LANES), F32)],
            band=band,
        )(place, *received)
        next_state = next_state.reshape(column_state.shape)
        state_grad = state_grad.reshape(column_state.shape)

    with jax.named_scope("weights_back"):
        own = call(copy_kernel, shape(share, BF), sectors)(exchange(copies, PLANE), *received[1:])
        other = lax.ppermute(own, "core", swap)
        columns = members * lax.axis_size("mem") * lat_total * lon_total
        grad_in, grad_bias, grad_out = call(
            unpack_kernel,
            (
                shape((hidden_units, in_channels), F32),
                shape((hidden_units,), F32),
                shape((channels, hidden_units), F32),
            ),
            3,
            smem=1,
            scratch=[flat_rows],
            scaling=1.0 / math.sqrt(columns),
            sectors=sectors,
        )(place, own, other)
    return next_state, state_grad, grad_in, grad_bias, grad_out


def solution(mesh):
    lat, lon, mem = mesh.devices.shape
    devices = mesh.devices.reshape(2, lat // 4, 2, lon, mem)
    split = Mesh(devices, ("ylo", "z", "core", "lon", "mem"))
    lat_axes = ("ylo", "z", "core")
    field = P("mem", None, lat_axes, "lon")
    surface = P(lat_axes, "lon")
    whole = P()
    return jax.shard_map(
        on_device,
        mesh=split,
        in_specs=(field, field, surface, surface, P("mem")) + (whole,) * 6,
        out_specs=(field, field, whole, whole, whole),
        check_vma=False,
    )
```
